32 devices in a mesh: vocab: 8 (over z, y), tok: 4 (over x, core).
Axes of the slice: x: 2, y: 2, z: 4, core: 2. Of those that a mesh axis runs over, the one named last changes fastest.
Arguments:
- hidden: bfloat16 [512, 8192], P('tok', 'vocab'), may hold values from -16 to 16
- head: bfloat16 [4096, 8192], P(('vocab', 'tok')), may hold values from -1 to 1
- factor_rows: bfloat16 [512, 64], P('vocab'), may hold values from -2 to 2
- factor_basis: bfloat16 [64, 8192], replicated, may hold values from -0.0625 to 0.0625
- targets: int32 [512], P('tok'), may hold values from 0 to 4607
- loss_mask: int32 [512], P('tok'), may hold values 0 or 1
Outputs:
- hidden_grad: bfloat16 [512, 8192], P('tok', 'vocab')
- rows_grad: float32 [512, 64], P('vocab')
- basis_grad: float32 [64, 8192], P(None, 'vocab')
The draws below stay inside these ranges and needn't reach their ends.
All inputs are finite; a program needn't handle non-finite values. No bound on the sum of `loss_mask` on one device may be relied on, other than what follows from the above.
Results may differ from the reference program's by a relative error of at most 0.0095.
Values may be sent and summed in bfloat16 or wider, within the bound.
No kernel may reach another device: no remote copies, remote signals or barrier semaphores. Data moves between devices by JAX's collectives and lax.ppermute only.
A program may use at most 64 MiB of HBM per device.

```python
import math
import jax
import jax.numpy as jnp

D = 8192
R = 64
VOCAB = 4096
NEWROWS = 512
TOKENS = 512


def head_row(key, index):
    row_key = jax.random.fold_in(jax.random.fold_in(key, 101), index)
    return jnp.clip(jax.random.normal(row_key, (D,), jnp.float32), -6.0, 6.0)


def draw_head(key, part):
    rows = jax.vmap(lambda index: head_row(key, index))(jnp.arange(VOCAB))
    scaled = rows * (3.0 / math.sqrt(D))
    return jnp.clip(scaled, -1.0, 1.0).astype(jnp.bfloat16)


def draw_hidden(key, part):
    own_key = jax.random.fold_in(key, 7)
    states = jnp.clip(jax.random.normal(own_key, (TOKENS, D), jnp.float32), -6.0, 6.0)
    return jnp.clip(states, -16.0, 16.0).astype(jnp.bfloat16)


def place_ends(drawn, stream_key, least, high):
    place = [jax.random.randint(jax.random.fold_in(stream_key, axis), (), 0, length) for axis, length in enumerate(drawn.shape)]
    widest = drawn.shape.index(max(drawn.shape))
    beside = place[:widest] + [(place[widest] + 1) % drawn.shape[widest]] + place[widest + 1:]
    return drawn.at[tuple(place)].set(least).at[tuple(beside)].set(high)


def shard_levels(stream_key, dims, cuts, least, top_value):
    def one(axis_at, parts):
        draws = jax.random.uniform(jax.random.fold_in(jax.random.fold_in(stream_key, 6), axis_at), (parts,), jnp.float32, least / len(cuts), top_value / len(cuts))
        return jnp.repeat(jnp.exp(draws), dims[axis_at] // parts).reshape((-1,) + (1,) * (len(dims) - axis_at - 1))

    factor_of = one(*cuts[0])
    for cut in cuts[1:]:
        factor_of = factor_of * one(*cut)
    return factor_of


def bell_draw(key, dims, width, most, pieces=(), kind=jnp.bfloat16):
    result = jax.random.normal(key, dims, jnp.float32) * width
    if len(pieces) > 0:
        result = shard_levels(key, dims, pieces, -0.22, 0.18) * result
    return jnp.clip(result, min=-most, max=most).astype(kind)


def setup_inputs(seed: int = 0) -> dict:
    key_of = jax.random.split(jax.random.key(seed), 7)
    return {
        "hidden": draw_hidden(jax.random.fold_in(key_of[6], 71), 0),
        "head": draw_head(jax.random.fold_in(key_of[6], 71), 0),
        "factor_rows": bell_draw(key_of[2], (NEWROWS, R), (max(R // 9, 1)) ** -0.5, 2.0, ((0, 8),)),
        "factor_basis": bell_draw(key_of[3], (R, D), D ** -0.5, 0.0625),
        "targets": place_ends(jax.random.randint(key_of[4], (TOKENS,), 0, VOCAB + NEWROWS), jax.random.fold_in(key_of[4], 1), 0, (VOCAB + NEWROWS) - 1).astype(jnp.int32),
        "loss_mask": place_ends((jax.random.randint(key_of[5], (TOKENS,), 0, 4) < 3).astype(jnp.int32), jax.random.fold_in(key_of[5], 1), 0, 1),
    }


loss_scale = 64.0


def reference(hidden, head, factor_rows, factor_basis, targets, loss_mask):
    frozen_logits = jnp.dot(hidden, head.T, preferred_element_type=jnp.float32)
    hidden_basis = jnp.dot(hidden, factor_basis.T, preferred_element_type=jnp.float32).astype(jnp.bfloat16)
    fresh_logits = jnp.dot(hidden_basis, factor_rows.T, preferred_element_type=jnp.float32)
    logits = jnp.concatenate([frozen_logits, fresh_logits], axis=1)
    row_top = jnp.max(logits, axis=1, keepdims=True)
    shifted = jnp.exp(logits - row_top)
    probs = shifted / jnp.sum(shifted, axis=1, keepdims=True)
    column = jnp.arange(VOCAB + NEWROWS, dtype=jnp.int32)
    onehot_hit = (column[None, :] == targets.astype(jnp.int32)[:, None]).astype(jnp.float32)
    weight_row = loss_scale * loss_mask.astype(jnp.float32)[:, None]
    logit_grad = (weight_row * (probs - onehot_hit)).astype(jnp.bfloat16)
    frozen_grad = logit_grad[:, :VOCAB]
    fresh_grad = logit_grad[:, VOCAB:]
    mix_total = jnp.dot(fresh_grad, factor_rows, preferred_element_type=jnp.float32).astype(jnp.bfloat16)
    hidden_grad = (jnp.dot(frozen_grad, head, preferred_element_type=jnp.float32)
                   + jnp.dot(mix_total, factor_basis, preferred_element_type=jnp.float32)).astype(jnp.bfloat16)
    rows_grad = jnp.dot(fresh_grad.T, hidden_basis, preferred_element_type=jnp.float32)
    basis_grad = jnp.dot(mix_total.T, hidden, preferred_element_type=jnp.float32)
    return hidden_grad, rows_grad, basis_grad
```

```python
import jax
import jax.numpy as jnp
from jax import lax
from jax.sharding import PartitionSpec as P

loss_scale = 64.0
f32 = jnp.float32
bf16 = jnp.bfloat16
contract_last = (((1,), (1,)), ((), ()))
contract_first = (((0,), (0,)), ((), ()))


def dot_last(a, b):
    return lax.dot_general(a, b, contract_last, preferred_element_type=f32)


def dot_first(a, b):
    return lax.dot_general(a, b, contract_first, preferred_element_type=f32)


def swap(value, axis, bit):
    size = lax.axis_size(axis)
    return lax.ppermute(value, axis, [(i, i ^ bit) for i in range(size)])


def swap_core(value):
    return swap(value, "tok", 1)


def swap_x(value):
    return swap(value, "tok", 2)


def swap_y(value):
    return swap(value, "vocab", 1)


def swap_z(value, step):
    return swap(value, "vocab", 2 * step)


def on_few(hidden, head, factor_rows, factor_basis, targets, loss_mask):
    n_z = lax.axis_size("vocab") // 2
    n_tok = lax.axis_size("tok")
    v = lax.axis_index("vocab")
    t = lax.axis_index("tok")
    toks, width = hidden.shape
    rows = head.shape[0]
    new_here = factor_rows.shape[0]
    half = width // 2

    head_other = swap_core(head)
    rows_all = lax.all_gather(factor_rows, "vocab", axis=0, tiled=True)
    token_info = jnp.stack([targets, loss_mask])
    token_info = jnp.concatenate([token_info, swap_x(token_info)], axis=1)
    shards = [hidden] + [swap_z(hidden, k) for k in range(1, n_z)]
    pieces = []
    for shard in shards:
        from_x = swap_x(shard)
        from_y = swap_y(shard)
        diag_a = swap_x(from_y[:, :half])
        diag_b = swap_y(from_x[:, half:])
        pieces.append((from_x, from_y, diag_a, diag_b))

    def weights(dy, dz):
        start = (v ^ (2 * dz + dy)) * width
        cut = lambda a: lax.dynamic_slice_in_dim(a, start, width, 1)
        return jnp.concatenate([cut(head), cut(head_other), cut(factor_basis)], axis=0)

    blocks = [[weights(dy, dz) for dy in range(2)] for dz in range(n_z)]

    own = jnp.zeros((2 * rows + factor_basis.shape[0], toks), f32)
    other = own
    for dz in range(n_z):
        from_x, from_y, diag_a, diag_b = pieces[dz]
        own = own + dot_last(blocks[dz][0], shards[dz])
        own = own + dot_last(blocks[dz][1], from_y)
        other = other + dot_last(blocks[dz][0], from_x)
        other = other + dot_last(blocks[dz][1][:, :half], diag_a)
        other = other + dot_last(blocks[dz][1][:, half:], diag_b)
    both = jnp.concatenate([own, other], axis=1)
    frozen = both[: 2 * rows]
    hidden_basis = both[2 * rows :].astype(bf16)

    def merge(stats):
        top = stats[0][0]
        for s in stats[1:]:
            top = jnp.maximum(top, s[0])
        total = stats[0][1] * jnp.exp(stats[0][0] - top)
        for s in stats[1:]:
            total = total + s[1] * jnp.exp(s[0] - top)
        return jnp.stack([top, total])

    def local(logits):
        top = jnp.max(logits, axis=0)
        return jnp.stack([top, jnp.sum(jnp.exp(logits - top[None, :]), axis=0)])

    def turn(stats):
        return jnp.concatenate([stats[:, toks:], stats[:, :toks]], axis=1)

    mine = local(frozen)
    stat_x = swap_x(mine)
    stat_y = swap_y(mine)
    stat_xy = swap_x(stat_y)
    plane = merge([mine, turn(stat_x), stat_y, turn(stat_xy)])
    fresh = lax.dot_general(
        rows_all, hidden_basis, (((1,), (0,)), ((), ())), preferred_element_type=f32
    )
    stats = merge([plane] + [swap_z(plane, k) for k in range(1, n_z)] + [local(fresh)])
    row_top, sum_exp = stats[0], stats[1]

    weight_row = loss_scale * token_info[1].astype(f32)
    scale_row = weight_row / sum_exp
    row_iota = lax.broadcasted_iota(jnp.int32, (rows, 1), 0)
    row_ids = jnp.concatenate(
        [row_iota + (v * n_tok + t) * rows, row_iota + (v * n_tok + (t ^ 1)) * rows], axis=0
    )
    hit = jnp.where(row_ids == token_info[0][None, :], weight_row[None, :], 0.0)
    grad = (jnp.exp(frozen - row_top[None, :]) * scale_row[None, :] - hit).astype(bf16)
    grad_own, grad_other = grad[:, :toks], grad[:, toks:]

    frozen_rows = rows * n_tok * lax.axis_size("vocab")
    fresh_ids = lax.broadcasted_iota(jnp.int32, (rows_all.shape[0], 1), 0) + frozen_rows
    fresh_hit = jnp.where(fresh_ids == targets[None, :], weight_row[None, :toks], 0.0)
    fresh_grad = (
        jnp.exp(fresh[:, :toks] - row_top[None, :toks]) * scale_row[None, :toks] - fresh_hit
    ).astype(bf16)
    mix_total = dot_first(rows_all, fresh_grad).astype(bf16)
    fresh_here = lax.dynamic_slice_in_dim(fresh_grad, v * new_here, new_here, 0)
    rows_part = dot_last(fresh_here, hidden_basis[:, :toks])
    basis_part = lax.reduce_precision(jnp.dot(mix_total, hidden, preferred_element_type=f32), 8, 7)

    def part(grads, dy, dz, cols=slice(None)):
        return dot_first(grads, blocks[dz][dy][: 2 * rows, cols])

    arrived = []
    for dz in range(n_z - 1, -1, -1):
        diag_a = swap_x(part(grad_other, 1, dz, slice(0, half)).astype(bf16))
        diag_b = swap_y(part(grad_other, 1, dz, slice(half, width)).astype(bf16))
        to_x = part(grad_other, 0, dz) + jnp.pad(diag_b.astype(f32), ((0, 0), (half, 0)))
        to_y = part(grad_own, 1, dz) + jnp.pad(diag_a.astype(f32), ((0, 0), (0, width - half)))
        from_x = swap_x(to_x.astype(bf16))
        from_y = swap_y(to_y.astype(bf16))
        here = part(grad_own, 0, dz) + from_x.astype(f32) + from_y.astype(f32)
        arrived.append(swap_z(here.astype(bf16), dz).astype(f32) if dz else here)

    basis_here = lax.dynamic_slice_in_dim(factor_basis, v * width, width, 1)
    hidden_grad = dot_first(mix_total, basis_here)
    for piece in arrived:
        hidden_grad = hidden_grad + piece
    hidden_grad = hidden_grad.astype(bf16)

    basis_two = basis_part + swap_x(basis_part.astype(bf16)).astype(f32)
    basis_grad = basis_two + swap_core(basis_two)
    rows_two = rows_part + swap_x(rows_part)
    rows_grad = rows_two + swap_core(rows_two)
    return hidden_grad, rows_grad, basis_grad


def on_many(hidden, head, factor_rows, factor_basis, targets, loss_mask):
    n_vocab = lax.axis_size("vocab")
    n_tok = lax.axis_size("tok")
    vocab_index = lax.axis_index("vocab")
    rows_here = head.shape[0] * n_tok
    new_here = factor_rows.shape[0]
    width_here = hidden.shape[1]
    gathered = lax.all_gather(hidden, "vocab", axis=1, tiled=True)
    head_full = lax.all_gather(head, "tok", axis=0, tiled=True)
    frozen = dot_last(gathered, head_full)
    hidden_basis = dot_last(gathered, factor_basis).astype(bf16)
    fresh_logits = dot_last(hidden_basis, factor_rows)
    local_max = jnp.maximum(jnp.max(frozen, axis=1), jnp.max(fresh_logits, axis=1))
    row_top = lax.pmax(local_max, "vocab")
    local_sum = jnp.sum(jnp.exp(frozen - row_top[:, None]), axis=1) + jnp.sum(
        jnp.exp(fresh_logits - row_top[:, None]), axis=1
    )
    sum_exp = lax.psum(local_sum, "vocab")
    frozen_prob = jnp.exp(frozen - row_top[:, None]) / sum_exp[:, None]
    fresh_prob = jnp.exp(fresh_logits - row_top[:, None]) / sum_exp[:, None]
    frozen_offset = targets - vocab_index * rows_here
    fresh_offset = targets - rows_here * n_vocab - vocab_index * new_here
    frozen_hit = (
        lax.broadcasted_iota(jnp.int32, frozen.shape, 1) == frozen_offset[:, None]
    ).astype(f32)
    fresh_hit = (
        lax.broadcasted_iota(jnp.int32, fresh_logits.shape, 1) == fresh_offset[:, None]
    ).astype(f32)
    weight_row = loss_scale * loss_mask.astype(f32)[:, None]
    frozen_grad = (weight_row * (frozen_prob - frozen_hit)).astype(bf16)
    fresh_grad = (weight_row * (fresh_prob - fresh_hit)).astype(bf16)
    mix_term = jnp.dot(fresh_grad, factor_rows, preferred_element_type=f32)
    mix_total = lax.psum(mix_term, "vocab").astype(bf16)
    grad_part = lax.psum_scatter(
        lax.dot_general(
            head_full, frozen_grad, (((0,), (1,)), ((), ())), preferred_element_type=f32
        ),
        "vocab",
        scatter_dimension=0,
        tiled=True,
    )
    basis_cols = lax.dynamic_slice_in_dim(factor_basis, vocab_index * width_here, width_here, 1)
    hidden_grad = (
        grad_part.T + jnp.dot(mix_total, basis_cols, preferred_element_type=f32)
    ).astype(bf16)
    rows_term = dot_first(fresh_grad, hidden_basis)
    basis_term = dot_first(mix_total, hidden)
    rows_grad, basis_grad = (
        lax.psum(rows_term.astype(bf16), "tok").astype(f32),
        lax.psum(basis_term.astype(bf16), "tok").astype(f32),
    )
    return hidden_grad, rows_grad, basis_grad


def solution(mesh):
    in_specs = (
        P("tok", "vocab"),
        P(("vocab", "tok"), None),
        P("vocab", None),
        P(),
        P("tok"),
        P("tok"),
    )
    out_specs = (P("tok", "vocab"), P("vocab", None), P(None, "vocab"))
    few = mesh.shape["vocab"] <= 16 and mesh.shape["tok"] == 4
    return jax.shard_map(
        on_few if few else on_many,
        mesh=mesh,
        in_specs=in_specs,
        out_specs=out_specs,
        check_vma=False,
    )
```

```python
import jax
import jax.numpy as jnp
from jax import lax
from jax.sharding import PartitionSpec as P

loss_scale = 64.0
f32 = jnp.float32
bf16 = jnp.bfloat16
contract_last = (((1,), (1,)), ((), ()))
contract_first = (((0,), (0,)), ((), ()))


def dot_last(a, b):
    return lax.dot_general(a, b, contract_last, preferred_element_type=f32)


def dot_first(a, b):
    return lax.dot_general(a, b, contract_first, preferred_element_type=f32)


def swap(value, axis, bit):
    size = lax.axis_size(axis)
    return lax.ppermute(value, axis, [(i, i ^ bit) for i in range(size)])


def swap_core(value):
    return swap(value, "tok", 1)


def swap_x(value):
    return swap(value, "tok", 2)


def swap_y(value):
    return swap(value, "vocab", 1)


def swap_z(value, step):
    return swap(value, "vocab", 2 * step)


def on_few(hidden, head, factor_rows, factor_basis, targets, loss_mask):
    n_z = lax.axis_size("vocab") // 2
    n_tok = lax.axis_size("tok")
    v = lax.axis_index("vocab")
    t = lax.axis_index("tok")
    toks, width = hidden.shape
    rows = head.shape[0]
    new_here = factor_rows.shape[0]
    half = width // 2

    head_other = swap_core(head)
    rows_all, row_blocks = factor_rows, [0]
    for bit in [1 << b for b in range(1, n_z.bit_length() - 1 + 1)][::-1] + [1]:
        rows_all = jnp.concatenate([rows_all, swap(rows_all, "vocab", bit)], axis=0)
        row_blocks = row_blocks + [j ^ bit for j in row_blocks]
    token_info = jnp.stack([targets, loss_mask])
    token_info = jnp.concatenate([token_info, swap_x(token_info)], axis=1)
    shards = [hidden] + [swap_z(hidden, k) for k in range(1, n_z)]
    pieces = []
    for shard in shards:
        from_x = swap_x(shard)
        from_y = swap_y(shard)
        diag_a = swap_x(from_y[:, :half])
        diag_b = swap_y(from_x[:, half:])
        pieces.append((from_x, from_y, diag_a, diag_b))

    def weights(dy, dz):
        start = (v ^ (2 * dz + dy)) * width
        cut = lambda a: lax.dynamic_slice_in_dim(a, start, width, 1)
        return jnp.concatenate([cut(head), cut(head_other), cut(factor_basis)], axis=0)

    blocks = [[weights(dy, dz) for dy in range(2)] for dz in range(n_z)]

    own = jnp.zeros((2 * rows + factor_basis.shape[0], toks), f32)
    other = own
    for dz in range(n_z):
        from_x, from_y, diag_a, diag_b = pieces[dz]
        own = own + dot_last(blocks[dz][0], shards[dz])
        own = own + dot_last(blocks[dz][1], from_y)
        other = other + dot_last(blocks[dz][0], from_x)
        other = other + dot_last(blocks[dz][1][:, :half], diag_a)
        other = other + dot_last(blocks[dz][1][:, half:], diag_b)
    both = jnp.concatenate([own, other], axis=1)
    frozen = both[: 2 * rows]
    hidden_basis = both[2 * rows :].astype(bf16)

    def merge(stats):
        top = stats[0][0]
        for s in stats[1:]:
            top = jnp.maximum(top, s[0])
        total = stats[0][1] * jnp.exp(stats[0][0] - top)
        for s in stats[1:]:
            total = total + s[1] * jnp.exp(s[0] - top)
        return jnp.stack([top, total])

    def local(logits):
        top = jnp.max(logits, axis=0)
        return jnp.stack([top, jnp.sum(jnp.exp(logits - top[None, :]), axis=0)])

    def turn(stats):
        return jnp.concatenate([stats[:, toks:], stats[:, :toks]], axis=1)

    stats = local(frozen)
    stats = merge([stats, turn(swap_x(stats))])
    stats = merge([stats, swap_y(stats)])
    step = 1
    while step < n_z:
        stats = merge([stats, swap_z(stats, step)])
        step *= 2
    fresh = lax.dot_general(
        rows_all, hidden_basis, (((1,), (0,)), ((), ())), preferred_element_type=f32
    )
    stats = merge([stats, local(fresh)])
    row_top, sum_exp = stats[0], stats[1]

    weight_row = loss_scale * token_info[1].astype(f32)
    scale_row = weight_row / sum_exp
    row_iota = lax.broadcasted_iota(jnp.int32, (rows, 1), 0)
    row_ids = jnp.concatenate(
        [row_iota + (v * n_tok + t) * rows, row_iota + (v * n_tok + (t ^ 1)) * rows], axis=0
    )
    hit = jnp.where(row_ids == token_info[0][None, :], weight_row[None, :], 0.0)
    grad = (jnp.exp(frozen - row_top[None, :]) * scale_row[None, :] - hit).astype(bf16)
    grad_own, grad_other = grad[:, :toks], grad[:, toks:]

    frozen_rows = rows * n_tok * lax.axis_size("vocab")
    new_iota = lax.broadcasted_iota(jnp.int32, (new_here, 1), 0) + frozen_rows
    fresh_ids = jnp.concatenate([new_iota + (v ^ j) * new_here for j in row_blocks], axis=0)
    fresh_hit = jnp.where(fresh_ids == targets[None, :], weight_row[None, :toks], 0.0)
    fresh_grad = (
        jnp.exp(fresh[:, :toks] - row_top[None, :toks]) * scale_row[None, :toks] - fresh_hit
    ).astype(bf16)
    mix_total = dot_first(rows_all, fresh_grad).astype(bf16)
    rows_part = dot_last(fresh_grad[:new_here], hidden_basis[:, :toks])
    basis_part = lax.reduce_precision(jnp.dot(mix_total, hidden, preferred_element_type=f32), 8, 7)

    def part(grads, dy, dz, cols=slice(None)):
        return dot_first(grads, blocks[dz][dy][: 2 * rows, cols])

    arrived = []
    diag_a = diag_b = None
    for dz in range(n_z - 1, -1, -1):
        send_a = part(grad_other, 1, dz, slice(0, half)).astype(bf16)
        send_b = part(grad_other, 1, dz, slice(half, width)).astype(bf16)
        if diag_a is not None:
            send_a, send_b, _, _ = lax.optimization_barrier((send_a, send_b, diag_a, diag_b))
        diag_a = swap_x(send_a)
        diag_b = swap_y(send_b)
        to_x = part(grad_other, 0, dz) + jnp.pad(diag_b.astype(f32), ((0, 0), (half, 0)))
        to_y = part(grad_own, 1, dz) + jnp.pad(diag_a.astype(f32), ((0, 0), (0, width - half)))
        from_x = swap_x(to_x.astype(bf16))
        from_y = swap_y(to_y.astype(bf16))
        here = part(grad_own, 0, dz) + from_x.astype(f32) + from_y.astype(f32)
        arrived.append(swap_z(here.astype(bf16), dz).astype(f32) if dz else here)

    basis_here = lax.dynamic_slice_in_dim(factor_basis, v * width, width, 1)
    hidden_grad = dot_first(mix_total, basis_here)
    for piece in arrived:
        hidden_grad = hidden_grad + piece
    hidden_grad = hidden_grad.astype(bf16)

    basis_two = basis_part + swap_x(basis_part.astype(bf16)).astype(f32)
    basis_grad = basis_two + swap_core(basis_two)
    rows_two = rows_part + swap_x(rows_part)
    rows_grad = rows_two + swap_core(rows_two)
    return hidden_grad, rows_grad, basis_grad


def on_many(hidden, head, factor_rows, factor_basis, targets, loss_mask):
    n_vocab = lax.axis_size("vocab")
    n_tok = lax.axis_size("tok")
    vocab_index = lax.axis_index("vocab")
    rows_here = head.shape[0] * n_tok
    new_here = factor_rows.shape[0]
    width_here = hidden.shape[1]
    gathered = lax.all_gather(hidden, "vocab", axis=1, tiled=True)
    head_full = lax.all_gather(head, "tok", axis=0, tiled=True)
    frozen = dot_last(gathered, head_full)
    hidden_basis = dot_last(gathered, factor_basis).astype(bf16)
    fresh_logits = dot_last(hidden_basis, factor_rows)
    local_max = jnp.maximum(jnp.max(frozen, axis=1), jnp.max(fresh_logits, axis=1))
    row_top = lax.pmax(local_max, "vocab")
    local_sum = jnp.sum(jnp.exp(frozen - row_top[:, None]), axis=1) + jnp.sum(
        jnp.exp(fresh_logits - row_top[:, None]), axis=1
    )
    sum_exp = lax.psum(local_sum, "vocab")
    frozen_prob = jnp.exp(frozen - row_top[:, None]) / sum_exp[:, None]
    fresh_prob = jnp.exp(fresh_logits - row_top[:, None]) / sum_exp[:, None]
    frozen_offset = targets - vocab_index * rows_here
    fresh_offset = targets - rows_here * n_vocab - vocab_index * new_here
    frozen_hit = (
        lax.broadcasted_iota(jnp.int32, frozen.shape, 1) == frozen_offset[:, None]
    ).astype(f32)
    fresh_hit = (
        lax.broadcasted_iota(jnp.int32, fresh_logits.shape, 1) == fresh_offset[:, None]
    ).astype(f32)
    weight_row = loss_scale * loss_mask.astype(f32)[:, None]
    frozen_grad = (weight_row * (frozen_prob - frozen_hit)).astype(bf16)
    fresh_grad = (weight_row * (fresh_prob - fresh_hit)).astype(bf16)
    mix_term = jnp.dot(fresh_grad, factor_rows, preferred_element_type=f32)
    mix_total = lax.psum(mix_term, "vocab").astype(bf16)
    grad_part = lax.psum_scatter(
        lax.dot_general(
            head_full, frozen_grad, (((0,), (1,)), ((), ())), preferred_element_type=f32
        ),
        "vocab",
        scatter_dimension=0,
        tiled=True,
    )
    basis_cols = lax.dynamic_slice_in_dim(factor_basis, vocab_index * width_here, width_here, 1)
    hidden_grad = (
        grad_part.T + jnp.dot(mix_total, basis_cols, preferred_element_type=f32)
    ).astype(bf16)
    rows_term = dot_first(fresh_grad, hidden_basis)
    basis_term = dot_first(mix_total, hidden)
    rows_grad, basis_grad = (
        lax.psum(rows_term.astype(bf16), "tok").astype(f32),
        lax.psum(basis_term.astype(bf16), "tok").astype(f32),
    )
    return hidden_grad, rows_grad, basis_grad


def solution(mesh):
    in_specs = (
        P("tok", "vocab"),
        P(("vocab", "tok"), None),
        P("vocab", None),
        P(),
        P("tok"),
        P("tok"),
    )
    out_specs = (P("tok", "vocab"), P("vocab", None), P(None, "vocab"))
    few = mesh.shape["vocab"] <= 16 and mesh.shape["tok"] == 4
    return jax.shard_map(
        on_few if few else on_many,
        mesh=mesh,
        in_specs=in_specs,
        out_specs=out_specs,
        check_vma=False,
    )
```

```python
import jax
import jax.numpy as jnp
from jax import lax
from jax.sharding import PartitionSpec as P

loss_scale = 64.0
f32 = jnp.float32
bf16 = jnp.bfloat16
contract_last = (((1,), (1,)), ((), ()))
contract_first = (((0,), (0,)), ((), ()))


def dot_last(a, b):
    return lax.dot_general(a, b, contract_last, preferred_element_type=f32)


def dot_first(a, b):
    return lax.dot_general(a, b, contract_first, preferred_element_type=f32)


def swap(value, axis, bit):
    size = lax.axis_size(axis)
    return lax.ppermute(value, axis, [(i, i ^ bit) for i in range(size)])


def swap_core(value):
    return swap(value, "tok", 1)


def swap_x(value):
    return swap(value, "tok", 2)


def swap_y(value):
    return swap(value, "vocab", 1)


def swap_z(value, step):
    return swap(value, "vocab", 2 * step)


def on_few(hidden, head, factor_rows, factor_basis, targets, loss_mask):
    n_z = lax.axis_size("vocab") // 2
    n_tok = lax.axis_size("tok")
    bits = [1 << b for b in range(n_z.bit_length() - 1)]
    v = lax.axis_index("vocab")
    t = lax.axis_index("tok")
    y, z = v & 1, v >> 1
    toks, width = hidden.shape
    rows = head.shape[0]
    new_here = factor_rows.shape[0]
    rank = factor_basis.shape[0]

    def pack(array, which, blocks):
        cuts = [
            lax.dynamic_slice_in_dim(array, (2 * block + which) * width, width, 1)
            for block in blocks
        ]
        return jnp.concatenate(cuts, axis=1) if len(cuts) > 1 else cuts[0]

    first, last = list(range(n_z - 1)), [n_z - 1]
    send_first, hidden = lax.optimization_barrier((pack(head, 1 - y, first), hidden))
    beside_first = swap_y(send_first)

    shards = {0: hidden}
    for bit in reversed(bits):
        for j in list(shards):
            shards[j ^ bit] = swap_z(shards[j], bit)
    cross = {j: swap_x(shards[j]) for j in shards}

    beside_last = swap_y(pack(head, 1 - y, last))
    kept = pack(head, y, range(n_z))
    kept_core = swap_core(kept)
    beside = jnp.concatenate([beside_first, beside_last], axis=1)
    beside_core = jnp.concatenate([swap_core(beside_first), swap_core(beside_last)], axis=1)
    basis_half = pack(factor_basis, y, range(n_z))

    token_info, rows_all, _ = lax.optimization_barrier(
        (jnp.stack([targets, loss_mask]), factor_rows, shards[bits[-1] if bits else 0])
    )
    row_blocks = [0]
    for bit in [2 * b for b in reversed(bits)] + [1]:
        rows_all = jnp.concatenate([rows_all, swap(rows_all, "vocab", bit)], axis=0)
        row_blocks = row_blocks + [j ^ bit for j in row_blocks]
    token_info = jnp.concatenate([token_info, swap_x(token_info)], axis=1)

    def in_order(parts):
        whole = jnp.zeros((toks, n_z * width), bf16)
        for j in sorted(parts):
            whole = lax.dynamic_update_slice_in_dim(whole, parts[j], (z ^ j) * width, 1)
        return whole

    upper = jnp.concatenate([kept, kept_core, basis_half], axis=0)
    lower = jnp.concatenate([beside, beside_core], axis=0)

    def add_over_y(tokens):
        up = dot_last(upper, tokens)
        low = dot_last(lower, tokens)
        mine = jnp.concatenate([up[: 2 * rows], low, up[2 * rows :]], axis=0)
        theirs = swap_y(mine)
        turned = jnp.concatenate(
            [theirs[2 * rows : 4 * rows], theirs[: 2 * rows], theirs[4 * rows :]], axis=0
        )
        return mine + turned

    both = jnp.concatenate([add_over_y(in_order(shards)), add_over_y(in_order(cross))], axis=1)
    frozen = both[: 4 * rows]
    hidden_basis = both[4 * rows :].astype(bf16)

    def merge(a, b):
        top = jnp.maximum(a[0], b[0])
        return jnp.stack([top, a[1] * jnp.exp(a[0] - top) + b[1] * jnp.exp(b[0] - top)])

    def local(logits):
        top = jnp.max(logits, axis=0)
        return jnp.stack([top, jnp.sum(jnp.exp(logits - top[None, :]), axis=0)])

    stats = local(frozen)
    turned = swap_x(stats)
    stats = merge(stats, jnp.concatenate([turned[:, toks:], turned[:, :toks]], axis=1))
    for bit in bits:
        stats = merge(stats, swap_z(stats, bit))
    fresh = lax.dot_general(
        rows_all, hidden_basis, (((1,), (0,)), ((), ())), preferred_element_type=f32
    )
    stats = merge(stats, local(fresh))
    row_top, sum_exp = stats[0], stats[1]

    weight_row = loss_scale * token_info[1].astype(f32)
    scale_row = weight_row / sum_exp
    row_iota = lax.broadcasted_iota(jnp.int32, (rows, 1), 0)
    row_ids = jnp.concatenate(
        [row_iota + (vv * n_tok + tt) * rows for vv in (v, v ^ 1) for tt in (t, t ^ 1)], axis=0
    )
    hit = jnp.where(row_ids == token_info[0][None, :], weight_row[None, :], 0.0)
    grad = (jnp.exp(frozen - row_top[None, :]) * scale_row[None, :] - hit).astype(bf16)

    frozen_rows = rows * n_tok * lax.axis_size("vocab")
    new_iota = lax.broadcasted_iota(jnp.int32, (new_here, 1), 0) + frozen_rows
    fresh_ids = jnp.concatenate([new_iota + (v ^ j) * new_here for j in row_blocks], axis=0)
    fresh_hit = jnp.where(fresh_ids == targets[None, :], weight_row[None, :toks], 0.0)
    fresh_grad = (
        jnp.exp(fresh[:, :toks] - row_top[None, :toks]) * scale_row[None, :toks] - fresh_hit
    ).astype(bf16)
    mix_total = dot_first(rows_all, fresh_grad).astype(bf16)
    rows_part = dot_last(fresh_grad[:new_here], hidden_basis[:, :toks])
    basis_part = lax.reduce_precision(jnp.dot(mix_total, hidden, preferred_element_type=f32), 8, 7)

    weights = jnp.concatenate([upper[: 2 * rows], lower], axis=0)

    def part(grads, j):
        return dot_first(grads, lax.dynamic_slice_in_dim(weights, (z ^ j) * width, width, 1))

    sums = {}
    for j in reversed(range(n_z)):
        from_x = swap_x(part(grad[:, toks:], j).astype(bf16))
        sums[j] = part(grad[:, :toks], j) + from_x.astype(f32)
    for bit in bits:
        for j in [j for j in sorted(sums, reverse=True) if j & bit]:
            sums[j ^ bit] = sums[j ^ bit] + swap_z(sums.pop(j).astype(bf16), bit).astype(f32)
    basis_here = lax.dynamic_slice_in_dim(factor_basis, v * width, width, 1)
    hidden_grad = (sums[0] + dot_first(mix_total, basis_here)).astype(bf16)

    basis_two = basis_part + swap_x(basis_part.astype(bf16)).astype(f32)
    basis_grad = basis_two + swap_core(basis_two)
    rows_two = rows_part + swap_x(rows_part)
    rows_grad = rows_two + swap_core(rows_two)
    return hidden_grad, rows_grad, basis_grad


def on_many(hidden, head, factor_rows, factor_basis, targets, loss_mask):
    n_vocab = lax.axis_size("vocab")
    n_tok = lax.axis_size("tok")
    vocab_index = lax.axis_index("vocab")
    rows_here = head.shape[0] * n_tok
    new_here = factor_rows.shape[0]
    width_here = hidden.shape[1]
    gathered = lax.all_gather(hidden, "vocab", axis=1, tiled=True)
    head_full = lax.all_gather(head, "tok", axis=0, tiled=True)
    frozen = dot_last(gathered, head_full)
    hidden_basis = dot_last(gathered, factor_basis).astype(bf16)
    fresh_logits = dot_last(hidden_basis, factor_rows)
    local_max = jnp.maximum(jnp.max(frozen, axis=1), jnp.max(fresh_logits, axis=1))
    row_top = lax.pmax(local_max, "vocab")
    local_sum = jnp.sum(jnp.exp(frozen - row_top[:, None]), axis=1) + jnp.sum(
        jnp.exp(fresh_logits - row_top[:, None]), axis=1
    )
    sum_exp = lax.psum(local_sum, "vocab")
    frozen_prob = jnp.exp(frozen - row_top[:, None]) / sum_exp[:, None]
    fresh_prob = jnp.exp(fresh_logits - row_top[:, None]) / sum_exp[:, None]
    frozen_offset = targets - vocab_index * rows_here
    fresh_offset = targets - rows_here * n_vocab - vocab_index * new_here
    frozen_hit = (
        lax.broadcasted_iota(jnp.int32, frozen.shape, 1) == frozen_offset[:, None]
    ).astype(f32)
    fresh_hit = (
        lax.broadcasted_iota(jnp.int32, fresh_logits.shape, 1) == fresh_offset[:, None]
    ).astype(f32)
    weight_row = loss_scale * loss_mask.astype(f32)[:, None]
    frozen_grad = (weight_row * (frozen_prob - frozen_hit)).astype(bf16)
    fresh_grad = (weight_row * (fresh_prob - fresh_hit)).astype(bf16)
    mix_term = jnp.dot(fresh_grad, factor_rows, preferred_element_type=f32)
    mix_total = lax.psum(mix_term, "vocab").astype(bf16)
    grad_part = lax.psum_scatter(
        lax.dot_general(
            head_full, frozen_grad, (((0,), (1,)), ((), ())), preferred_element_type=f32
        ),
        "vocab",
        scatter_dimension=0,
        tiled=True,
    )
    basis_cols = lax.dynamic_slice_in_dim(factor_basis, vocab_index * width_here, width_here, 1)
    hidden_grad = (
        grad_part.T + jnp.dot(mix_total, basis_cols, preferred_element_type=f32)
    ).astype(bf16)
    rows_term = dot_first(fresh_grad, hidden_basis)
    basis_term = dot_first(mix_total, hidden)
    rows_grad, basis_grad = (
        lax.psum(rows_term.astype(bf16), "tok").astype(f32),
        lax.psum(basis_term.astype(bf16), "tok").astype(f32),
    )
    return hidden_grad, rows_grad, basis_grad


def solution(mesh):
    in_specs = (
        P("tok", "vocab"),
        P(("vocab", "tok"), None),
        P("vocab", None),
        P(),
        P("tok"),
        P("tok"),
    )
    out_specs = (P("tok", "vocab"), P("vocab", None), P(None, "vocab"))
    few = mesh.shape["vocab"] <= 16 and mesh.shape["tok"] == 4
    return jax.shard_map(
        on_few if few else on_many,
        mesh=mesh,
        in_specs=in_specs,
        out_specs=out_specs,
        check_vma=False,
    )
```

```python
import jax
import jax.numpy as jnp
from jax import lax
from jax.experimental import pallas as pl
from jax.experimental.pallas import tpu as pltpu
from jax.sharding import PartitionSpec as P

loss_scale = 64.0
f32 = jnp.float32
bf16 = jnp.bfloat16
contract_last = (((1,), (1,)), ((), ()))
contract_first = (((0,), (0,)), ((), ()))


def dot_last(a, b):
    return lax.dot_general(a, b, contract_last, preferred_element_type=f32)


def dot_first(a, b):
    return lax.dot_general(a, b, contract_first, preferred_element_type=f32)


def swap(value, axis, bit):
    size = lax.axis_size(axis)
    return lax.ppermute(value, axis, [(i, i ^ bit) for i in range(size)])


def swap_core(value):
    return swap(value, "tok", 1)


def swap_x(value):
    return swap(value, "tok", 2)


def swap_y(value):
    return swap(value, "vocab", 1)


def swap_z(value, step):
    return swap(value, "vocab", 2 * step)


anywhere = pl.BlockSpec(memory_space=pl.ANY)


def copy_blocks(shapes, moves, *arrays):
    def kernel(*refs):
        ins, outs, sems = refs[: len(arrays)], refs[len(arrays) : -1], refs[-1]
        copies = []
        for n, (source, columns, target, row, column) in enumerate(moves()):
            src, dst = ins[source], outs[target]
            if columns is not None:
                src = src.at[:, pl.ds(pl.multiple_of(columns[0], 128), columns[1])]
            dst = dst.at[pl.ds(row, src.shape[0]), pl.ds(column, src.shape[1])]
            copies.append(pltpu.make_async_copy(src, dst, sems.at[n]))
        for copy in copies:
            copy.start()
        for copy in copies:
            copy.wait()

    size = sum(2 * shape[0] * shape[1] for shape in shapes)
    return pl.pallas_call(
        kernel,
        out_shape=[jax.ShapeDtypeStruct(shape, bf16) for shape in shapes],
        in_specs=[anywhere] * len(arrays),
        out_specs=[anywhere] * len(shapes),
        scratch_shapes=[pltpu.SemaphoreType.DMA((32,))],
        cost_estimate=pl.CostEstimate(flops=0, bytes_accessed=2 * size, transcendentals=0),
    )(*arrays)


def partial_logits(groups, tokens):
    heights = [group[0].shape[0] for group in groups]
    depth = sum(a.shape[1] for a in tokens)
    toks = tokens[0].shape[0]
    flat = [a for group in groups for a in group]
    n_flat = len(flat)

    def kernel(*refs):
        ins, out = refs[: n_flat + len(tokens)], refs[n_flat + len(tokens)]
        weight, token, sems = refs[n_flat + len(tokens) + 1 :]
        copies = []
        at, row = 0, 0
        for group, height in zip(groups, heights):
            column = 0
            for a in group:
                dst = weight.at[pl.ds(row, height), pl.ds(column, a.shape[1])]
                copies.append(pltpu.make_async_copy(ins[at], dst, sems.at[at]))
                column += a.shape[1]
                at += 1
            row += height
        column = 0
        for a in tokens:
            dst = token.at[:, pl.ds(column, a.shape[1])]
            copies.append(pltpu.make_async_copy(ins[at], dst, sems.at[at]))
            column += a.shape[1]
            at += 1
        for copy in copies:
            copy.start()
        for copy in copies[n_flat:]:
            copy.wait()
        at, row = 0, 0
        for group, height in zip(groups, heights):
            for _ in group:
                copies[at].wait()
                at += 1
            out[row : row + height, :] = dot_last(weight[row : row + height, :], token[...])
            row += height

    total = sum(heights)
    return pl.pallas_call(
        kernel,
        out_shape=jax.ShapeDtypeStruct((total, toks), f32),
        in_specs=[anywhere] * (n_flat + len(tokens)),
        out_specs=pl.BlockSpec(memory_space=pltpu.VMEM),
        scratch_shapes=[
            pltpu.VMEM((total, depth), bf16),
            pltpu.VMEM((toks, depth), bf16),
            pltpu.SemaphoreType.DMA((n_flat + len(tokens),)),
        ],
        compiler_params=pltpu.CompilerParams(vmem_limit_bytes=24 << 20),
        cost_estimate=pl.CostEstimate(
            flops=2 * total * depth * toks,
            bytes_accessed=2 * (total + toks) * depth + 4 * total * toks,
            transcendentals=0,
        ),
    )(*flat, *tokens)


def on_few(hidden, head, factor_rows, factor_basis, targets, loss_mask):
    n_z = lax.axis_size("vocab") // 2
    n_tok = lax.axis_size("tok")
    bits = [1 << b for b in range(n_z.bit_length() - 1)]
    v = lax.axis_index("vocab")
    t = lax.axis_index("tok")
    toks, width = hidden.shape
    rows = head.shape[0]
    new_here = factor_rows.shape[0]
    rank = factor_basis.shape[0]
    depth = n_z * width

    def start_of(j, other):
        return (lax.axis_index("vocab") ^ (2 * j + other)) * width

    cut = (n_z - 1) * width
    send_first, send_last = copy_blocks(
        [(rows, cut), (rows, width)],
        lambda: [(0, (start_of(j, 1), width), 0, 0, j * width) for j in range(n_z - 1)]
        + [(0, (start_of(n_z - 1, 1), width), 1, 0, 0)],
        head,
    )
    beside_first = swap_y(send_first)

    shards = {0: hidden}
    for bit in reversed(bits):
        near = swap_z(hidden, bit)
        for j in [j for j in shards if j]:
            shards[j], _ = lax.optimization_barrier((shards[j], near))
            shards[j ^ bit] = swap_z(shards[j], bit)
        shards[bit] = near
    cross = {}
    for j in range(n_z):
        sent = shards[j]
        if j > 1:
            sent, _ = lax.optimization_barrier((sent, cross[j - 2]))
        cross[j] = swap_x(sent)

    beside_last = swap_y(send_last)
    head_after, basis_after, _ = lax.optimization_barrier(
        (head, factor_basis, shards[n_z - 1])
    )
    kept, basis_half = copy_blocks(
        [(rows, depth), (rank, depth)],
        lambda: [
            (a, (start_of(j, 0), width), a, 0, j * width) for j in range(n_z) for a in range(2)
        ],
        head_after,
        basis_after,
    )
    kept_core = swap_core(kept)
    beside = [beside_first, beside_last]
    first_after, *_ = lax.optimization_barrier(
        (beside_first, *[cross[j] for j in range(n_z - 1)])
    )
    last_after, _ = lax.optimization_barrier((beside_last, shards[n_z - 1]))
    beside_core = [swap_core(first_after), swap_core(last_after)]

    groups = [[kept], [kept_core], beside, beside_core, [basis_half]]
    in_order = lambda parts: [parts[j] for j in range(n_z)]
    mine_own = partial_logits(groups, in_order(shards))
    mine_cross = partial_logits(groups, in_order(cross))
    theirs_own, theirs_cross = swap_y(mine_own), swap_y(mine_cross)
    mine = jnp.concatenate([mine_own, mine_cross], axis=1)
    theirs = jnp.concatenate([theirs_own, theirs_cross], axis=1)
    frozen_near = mine[: 2 * rows] + theirs[2 * rows : 4 * rows]
    frozen_far = mine[2 * rows : 4 * rows] + theirs[: 2 * rows]
    hidden_basis = (mine[4 * rows :] + theirs[4 * rows :]).astype(bf16)

    near_rows, _ = lax.optimization_barrier((factor_rows, beside_core[1]))
    rows_all = jnp.concatenate([factor_rows, swap_y(near_rows)], axis=0)
    row_blocks = [0, 1]
    rows_all, _ = lax.optimization_barrier((rows_all, mine_own))
    for bit in [2 * b for b in reversed(bits)]:
        rows_all = jnp.concatenate([rows_all, swap(rows_all, "vocab", bit)], axis=0)
        row_blocks = row_blocks + [j ^ bit for j in row_blocks]

    def merge(a, b):
        top = jnp.maximum(a[0], b[0])
        return jnp.stack([top, a[1] * jnp.exp(a[0] - top) + b[1] * jnp.exp(b[0] - top)])

    def local(*logits):
        top = jnp.max(logits[0], axis=0)
        for l in logits[1:]:
            top = jnp.maximum(top, jnp.max(l, axis=0))
        total = jnp.sum(jnp.exp(logits[0] - top[None, :]), axis=0)
        for l in logits[1:]:
            total = total + jnp.sum(jnp.exp(l - top[None, :]), axis=0)
        return jnp.stack([top, total])

    info = jnp.stack([targets.astype(f32), loss_mask.astype(f32)])
    stats = local(frozen_near, frozen_far)
    sent = jnp.concatenate([stats, jnp.concatenate([info, info], axis=1)], axis=0)
    came = swap_x(sent)
    stats = merge(stats, jnp.concatenate([came[:2, toks:], came[:2, :toks]], axis=1))
    info = jnp.concatenate([info, came[2:, :toks]], axis=1)
    target_row = info[0].astype(jnp.int32)
    weight_row = loss_scale * info[1]
    for bit in bits:
        stats = merge(stats, swap_z(stats, bit))
    fresh = lax.dot_general(
        rows_all, hidden_basis, (((1,), (0,)), ((), ())), preferred_element_type=f32
    )
    stats = merge(stats, local(fresh))
    row_top, sum_exp = stats[0], stats[1]
    scale_row = weight_row / sum_exp

    row_iota = lax.broadcasted_iota(jnp.int32, (rows, 1), 0)

    def grad_of(frozen, vv):
        row_ids = jnp.concatenate(
            [row_iota + (vv * n_tok + tt) * rows for tt in (t, t ^ 1)], axis=0
        )
        hit = jnp.where(row_ids == target_row[None, :], weight_row[None, :], 0.0)
        return (jnp.exp(frozen - row_top[None, :]) * scale_row[None, :] - hit).astype(bf16)

    grad = jnp.concatenate([grad_of(frozen_near, v), grad_of(frozen_far, v ^ 1)], axis=0)

    frozen_rows = rows * n_tok * lax.axis_size("vocab")
    new_iota = lax.broadcasted_iota(jnp.int32, (new_here, 1), 0) + frozen_rows
    fresh_ids = jnp.concatenate([new_iota + (v ^ j) * new_here for j in row_blocks], axis=0)
    fresh_hit = jnp.where(fresh_ids == targets[None, :], weight_row[None, :toks], 0.0)
    fresh_grad = (
        jnp.exp(fresh[:, :toks] - row_top[None, :toks]) * scale_row[None, :toks] - fresh_hit
    ).astype(bf16)
    mix_total = dot_first(rows_all, fresh_grad).astype(bf16)
    rows_part = dot_last(fresh_grad[:new_here], hidden_basis[:, :toks])
    basis_part = lax.reduce_precision(jnp.dot(mix_total, hidden, preferred_element_type=f32), 8, 7)

    (weights,) = copy_blocks(
        [(4 * rows, depth)],
        lambda: [
            (0, None, 0, 0, 0),
            (1, None, 0, rows, 0),
            (2, None, 0, 2 * rows, 0),
            (3, None, 0, 2 * rows, cut),
            (4, None, 0, 3 * rows, 0),
            (5, None, 0, 3 * rows, cut),
        ],
        kept,
        kept_core,
        *beside,
        *beside_core,
    )

    def part(grads, j):
        return dot_first(grads, weights[:, j * width : (j + 1) * width])

    sums, from_x = {}, {}
    for j in reversed(range(n_z)):
        send = part(grad[:, toks:], j).astype(bf16)
        if j + 2 in from_x:
            send, _ = lax.optimization_barrier((send, from_x[j + 2]))
        from_x[j] = swap_x(send)
        sums[j] = part(grad[:, :toks], j) + from_x[j].astype(f32)
    for bit in bits:
        for j in [j for j in sorted(sums, reverse=True) if j & bit]:
            sums[j ^ bit] = sums[j ^ bit] + swap_z(sums.pop(j).astype(bf16), bit).astype(f32)
    basis_here = lax.dynamic_slice_in_dim(factor_basis, v * width, width, 1)
    hidden_grad = (sums[0] + dot_first(mix_total, basis_here)).astype(bf16)

    basis_part, rows_part, _ = lax.optimization_barrier(
        (basis_part, rows_part, from_x[min(1, n_z - 1)])
    )
    basis_two = basis_part + swap_x(basis_part.astype(bf16)).astype(f32)
    basis_grad = basis_two + swap_core(basis_two)
    rows_two = rows_part + swap_x(rows_part)
    rows_grad = rows_two + swap_core(rows_two)
    return hidden_grad, rows_grad, basis_grad


def on_many(hidden, head, factor_rows, factor_basis, targets, loss_mask):
    n_vocab = lax.axis_size("vocab")
    n_tok = lax.axis_size("tok")
    vocab_index = lax.axis_index("vocab")
    rows_here = head.shape[0] * n_tok
    new_here = factor_rows.shape[0]
    width_here = hidden.shape[1]
    gathered = lax.all_gather(hidden, "vocab", axis=1, tiled=True)
    head_full = lax.all_gather(head, "tok", axis=0, tiled=True)
    frozen = dot_last(gathered, head_full)
    hidden_basis = dot_last(gathered, factor_basis).astype(bf16)
    fresh_logits = dot_last(hidden_basis, factor_rows)
    local_max = jnp.maximum(jnp.max(frozen, axis=1), jnp.max(fresh_logits, axis=1))
    row_top = lax.pmax(local_max, "vocab")
    local_sum = jnp.sum(jnp.exp(frozen - row_top[:, None]), axis=1) + jnp.sum(
        jnp.exp(fresh_logits - row_top[:, None]), axis=1
    )
    sum_exp = lax.psum(local_sum, "vocab")
    frozen_prob = jnp.exp(frozen - row_top[:, None]) / sum_exp[:, None]
    fresh_prob = jnp.exp(fresh_logits - row_top[:, None]) / sum_exp[:, None]
    frozen_offset = targets - vocab_index * rows_here
    fresh_offset = targets - rows_here * n_vocab - vocab_index * new_here
    frozen_hit = (
        lax.broadcasted_iota(jnp.int32, frozen.shape, 1) == frozen_offset[:, None]
    ).astype(f32)
    fresh_hit = (
        lax.broadcasted_iota(jnp.int32, fresh_logits.shape, 1) == fresh_offset[:, None]
    ).astype(f32)
    weight_row = loss_scale * loss_mask.astype(f32)[:, None]
    frozen_grad = (weight_row * (frozen_prob - frozen_hit)).astype(bf16)
    fresh_grad = (weight_row * (fresh_prob - fresh_hit)).astype(bf16)
    mix_term = jnp.dot(fresh_grad, factor_rows, preferred_element_type=f32)
    mix_total = lax.psum(mix_term, "vocab").astype(bf16)
    grad_part = lax.psum_scatter(
        lax.dot_general(
            head_full, frozen_grad, (((0,), (1,)), ((), ())), preferred_element_type=f32
        ),
        "vocab",
        scatter_dimension=0,
        tiled=True,
    )
    basis_cols = lax.dynamic_slice_in_dim(factor_basis, vocab_index * width_here, width_here, 1)
    hidden_grad = (
        grad_part.T + jnp.dot(mix_total, basis_cols, preferred_element_type=f32)
    ).astype(bf16)
    rows_term = dot_first(fresh_grad, hidden_basis)
    basis_term = dot_first(mix_total, hidden)
    rows_grad, basis_grad = (
        lax.psum(rows_term.astype(bf16), "tok").astype(f32),
        lax.psum(basis_term.astype(bf16), "tok").astype(f32),
    )
    return hidden_grad, rows_grad, basis_grad


def solution(mesh):
    in_specs = (
        P("tok", "vocab"),
        P(("vocab", "tok"), None),
        P("vocab", None),
        P(),
        P("tok"),
        P("tok"),
    )
    out_specs = (P("tok", "vocab"), P("vocab", None), P(None, "vocab"))
    few = mesh.shape["vocab"] <= 16 and mesh.shape["tok"] == 4
    return jax.shard_map(
        on_few if few else on_many,
        mesh=mesh,
        in_specs=in_specs,
        out_specs=out_specs,
        check_vma=False,
    )
```

```python
import jax
import jax.numpy as jnp
from jax import lax
from jax.experimental import pallas as pl
from jax.experimental.pallas import tpu as pltpu
from jax.sharding import PartitionSpec as P

loss_scale = 64.0
f32 = jnp.float32
bf16 = jnp.bfloat16
contract_last = (((1,), (1,)), ((), ()))
contract_first = (((0,), (0,)), ((), ()))


def dot_last(a, b):
    return lax.dot_general(a, b, contract_last, preferred_element_type=f32)


def dot_first(a, b):
    return lax.dot_general(a, b, contract_first, preferred_element_type=f32)


def swap(value, axis, bit):
    size = lax.axis_size(axis)
    return lax.ppermute(value, axis, [(i, i ^ bit) for i in range(size)])


def swap_core(value):
    return swap(value, "tok", 1)


def swap_x(value):
    return swap(value, "tok", 2)


def swap_y(value):
    return swap(value, "vocab", 1)


def swap_z(value, step):
    return swap(value, "vocab", 2 * step)


anywhere = pl.BlockSpec(memory_space=pl.ANY)
in_vmem = pl.BlockSpec(memory_space=pltpu.VMEM)


def copy_blocks(shapes, moves, *arrays):
    def kernel(*refs):
        ins, outs, sems = refs[: len(arrays)], refs[len(arrays) : -1], refs[-1]
        copies = []
        for n, (source, columns, target, row, column) in enumerate(moves()):
            src, dst = ins[source], outs[target]
            if columns is not None:
                src = src.at[:, pl.ds(pl.multiple_of(columns[0], 128), columns[1])]
            dst = dst.at[pl.ds(row, src.shape[0]), pl.ds(column, src.shape[1])]
            copies.append(pltpu.make_async_copy(src, dst, sems.at[n]))
        for copy in copies:
            copy.start()
        for copy in copies:
            copy.wait()

    size = sum(2 * shape[0] * shape[1] for shape in shapes)
    return pl.pallas_call(
        kernel,
        out_shape=[jax.ShapeDtypeStruct(shape, bf16) for shape in shapes],
        in_specs=[anywhere] * len(arrays),
        out_specs=[in_vmem] * len(shapes),
        scratch_shapes=[pltpu.SemaphoreType.DMA((32,))],
        compiler_params=pltpu.CompilerParams(vmem_limit_bytes=4 << 20),
        cost_estimate=pl.CostEstimate(flops=0, bytes_accessed=2 * size, transcendentals=0),
    )(*arrays)


def side_by_side(parts, into, row, sems, first):
    copies, column = [], 0
    for n, part in enumerate(parts):
        dst = into.at[pl.ds(row, part.shape[0]), pl.ds(column, part.shape[1])]
        copies.append(pltpu.make_async_copy(part, dst, sems.at[first + n]))
        column += part.shape[1]
    return copies


def first_logits(groups, tokens):
    heights = [group[0].shape[0] for group in groups]
    sizes = [len(group) for group in groups]
    total, depth = sum(heights), sum(a.shape[1] for a in tokens)
    toks = tokens[0].shape[0]
    flat = [a for group in groups for a in group]
    n_flat, n_all = len(flat), len(flat) + len(tokens)

    def kernel(*refs):
        out, weight, token, sems = refs[n_all:]
        token_copies = side_by_side(refs[n_flat:n_all], token, 0, sems, n_flat)
        row_copies, at, row = [], 0, 0
        for size, height in zip(sizes, heights):
            row_copies.append(side_by_side(refs[at : at + size], weight, row, sems, at))
            at, row = at + size, row + height
        for copy in token_copies + [copy for copies in row_copies for copy in copies]:
            copy.start()
        for copy in token_copies:
            copy.wait()
        row = 0
        for copies, height in zip(row_copies, heights):
            for copy in copies:
                copy.wait()
            out[row : row + height, :] = dot_last(weight[row : row + height, :], token[...])
            row += height

    return pl.pallas_call(
        kernel,
        out_shape=[
            jax.ShapeDtypeStruct((total, toks), f32),
            jax.ShapeDtypeStruct((total, depth), bf16),
        ],
        in_specs=[anywhere] * n_all,
        out_specs=[in_vmem] * 2,
        scratch_shapes=[pltpu.VMEM((toks, depth), bf16), pltpu.SemaphoreType.DMA((n_all,))],
        compiler_params=pltpu.CompilerParams(vmem_limit_bytes=12 << 20),
        cost_estimate=pl.CostEstimate(
            flops=2 * total * depth * toks,
            bytes_accessed=4 * (total + toks) * depth + 4 * total * toks,
            transcendentals=0,
        ),
    )(*flat, *tokens)


def second_logits(weight, tokens):
    total, depth = weight.shape
    toks, width = tokens[0].shape

    def kernel(weight_ref, *refs):
        out = refs[-1]
        for j, token in enumerate(refs[:-1]):
            part = dot_last(weight_ref[:, j * width : (j + 1) * width], token[...])
            out[...] = part if j == 0 else out[...] + part

    return pl.pallas_call(
        kernel,
        out_shape=jax.ShapeDtypeStruct((total, toks), f32),
        in_specs=[in_vmem] * (1 + len(tokens)),
        out_specs=in_vmem,
        compiler_params=pltpu.CompilerParams(vmem_limit_bytes=12 << 20),
        cost_estimate=pl.CostEstimate(
            flops=2 * total * depth * toks,
            bytes_accessed=2 * (total + toks) * depth + 4 * total * toks,
            transcendentals=0,
        ),
    )(weight, *tokens)


def on_few(hidden, head, factor_rows, factor_basis, targets, loss_mask):
    n_z = lax.axis_size("vocab") // 2
    n_tok = lax.axis_size("tok")
    bits = [1 << b for b in range(n_z.bit_length() - 1)]
    v = lax.axis_index("vocab")
    t = lax.axis_index("tok")
    toks, width = hidden.shape
    rows = head.shape[0]
    new_here = factor_rows.shape[0]
    rank = factor_basis.shape[0]
    depth = n_z * width

    def start_of(j, other):
        return (lax.axis_index("vocab") ^ (2 * j + other)) * width

    cut = (n_z - 1) * width
    send_first, send_last = copy_blocks(
        [(rows, cut), (rows, width)],
        lambda: [(0, (start_of(j, 1), width), 0, 0, j * width) for j in range(n_z - 1)]
        + [(0, (start_of(n_z - 1, 1), width), 1, 0, 0)],
        head,
    )
    beside_first = swap_y(send_first)

    shards = {0: hidden}
    for bit in reversed(bits):
        near = swap_z(hidden, bit)
        for j in [j for j in shards if j]:
            shards[j], _ = lax.optimization_barrier((shards[j], near))
            shards[j ^ bit] = swap_z(shards[j], bit)
        shards[bit] = near
    cross = {}
    for j in range(n_z):
        sent = shards[j]
        if j > 1:
            sent, _ = lax.optimization_barrier((sent, cross[j - 2]))
        cross[j] = swap_x(sent)

    beside_last = swap_y(send_last)
    head_after, basis_after, _ = lax.optimization_barrier(
        (head, factor_basis, shards[n_z - 1])
    )
    kept, basis_half = copy_blocks(
        [(rows, depth), (rank, depth)],
        lambda: [
            (a, (start_of(j, 0), width), a, 0, j * width) for j in range(n_z) for a in range(2)
        ],
        head_after,
        basis_after,
    )
    kept_core = swap_core(kept)
    beside = [beside_first, beside_last]
    first_after, *_ = lax.optimization_barrier(
        (beside_first, *[cross[j] for j in range(n_z - 1)])
    )
    last_after, _ = lax.optimization_barrier((beside_last, shards[n_z - 1]))
    beside_core = [swap_core(first_after), swap_core(last_after)]

    groups = [[kept], [kept_core], beside, beside_core, [basis_half]]
    in_order = lambda parts: [parts[j] for j in range(n_z)]
    mine_own, weights = first_logits(groups, in_order(shards))
    mine_cross = second_logits(weights, in_order(cross))
    theirs_own, theirs_cross = swap_y(mine_own), swap_y(mine_cross)
    mine = jnp.concatenate([mine_own, mine_cross], axis=1)
    theirs = jnp.concatenate([theirs_own, theirs_cross], axis=1)
    frozen_near = mine[: 2 * rows] + theirs[2 * rows : 4 * rows]
    frozen_far = mine[2 * rows : 4 * rows] + theirs[: 2 * rows]
    hidden_basis = (mine[4 * rows :] + theirs[4 * rows :]).astype(bf16)

    near_rows, _ = lax.optimization_barrier((factor_rows, beside_core[1]))
    rows_all = jnp.concatenate([factor_rows, swap_y(near_rows)], axis=0)
    row_blocks = [0, 1]
    rows_all, _ = lax.optimization_barrier((rows_all, mine_own))
    for bit in [2 * b for b in reversed(bits)]:
        rows_all = jnp.concatenate([rows_all, swap(rows_all, "vocab", bit)], axis=0)
        row_blocks = row_blocks + [j ^ bit for j in row_blocks]

    def merge(a, b):
        top = jnp.maximum(a[0], b[0])
        return jnp.stack([top, a[1] * jnp.exp(a[0] - top) + b[1] * jnp.exp(b[0] - top)])

    def local(*logits):
        top = jnp.max(logits[0], axis=0)
        for l in logits[1:]:
            top = jnp.maximum(top, jnp.max(l, axis=0))
        total = jnp.sum(jnp.exp(logits[0] - top[None, :]), axis=0)
        for l in logits[1:]:
            total = total + jnp.sum(jnp.exp(l - top[None, :]), axis=0)
        return jnp.stack([top, total])

    info = jnp.stack([targets.astype(f32), loss_mask.astype(f32)])
    stats = local(frozen_near, frozen_far)
    sent = jnp.concatenate([stats, jnp.concatenate([info, info], axis=1)], axis=0)
    came = swap_x(sent)
    stats = merge(stats, jnp.concatenate([came[:2, toks:], came[:2, :toks]], axis=1))
    info = jnp.concatenate([info, came[2:, :toks]], axis=1)
    target_row = info[0].astype(jnp.int32)
    weight_row = loss_scale * info[1]
    for bit in bits:
        stats = merge(stats, swap_z(stats, bit))
    fresh = lax.dot_general(
        rows_all, hidden_basis, (((1,), (0,)), ((), ())), preferred_element_type=f32
    )
    stats = merge(stats, local(fresh))
    row_top, sum_exp = stats[0], stats[1]
    scale_row = weight_row / sum_exp

    row_iota = lax.broadcasted_iota(jnp.int32, (rows, 1), 0)

    def grad_of(frozen, vv):
        row_ids = jnp.concatenate(
            [row_iota + (vv * n_tok + tt) * rows for tt in (t, t ^ 1)], axis=0
        )
        hit = jnp.where(row_ids == target_row[None, :], weight_row[None, :], 0.0)
        return (jnp.exp(frozen - row_top[None, :]) * scale_row[None, :] - hit).astype(bf16)

    grad = jnp.concatenate([grad_of(frozen_near, v), grad_of(frozen_far, v ^ 1)], axis=0)

    frozen_rows = rows * n_tok * lax.axis_size("vocab")
    new_iota = lax.broadcasted_iota(jnp.int32, (new_here, 1), 0) + frozen_rows
    fresh_ids = jnp.concatenate([new_iota + (v ^ j) * new_here for j in row_blocks], axis=0)
    fresh_hit = jnp.where(fresh_ids == targets[None, :], weight_row[None, :toks], 0.0)
    fresh_grad = (
        jnp.exp(fresh[:, :toks] - row_top[None, :toks]) * scale_row[None, :toks] - fresh_hit
    ).astype(bf16)
    mix_total = dot_first(rows_all, fresh_grad).astype(bf16)
    rows_part = dot_last(fresh_grad[:new_here], hidden_basis[:, :toks])
    basis_part = lax.reduce_precision(jnp.dot(mix_total, hidden, preferred_element_type=f32), 8, 7)

    def part(grads, j):
        return dot_first(grads, weights[: 4 * rows, j * width : (j + 1) * width])

    sums, from_x = {}, {}
    for j in reversed(range(n_z)):
        send = part(grad[:, toks:], j).astype(bf16)
        if j + 2 in from_x:
            send, _ = lax.optimization_barrier((send, from_x[j + 2]))
        from_x[j] = swap_x(send)
        sums[j] = part(grad[:, :toks], j) + from_x[j].astype(f32)
    for bit in bits:
        for j in [j for j in sorted(sums, reverse=True) if j & bit]:
            sums[j ^ bit] = sums[j ^ bit] + swap_z(sums.pop(j).astype(bf16), bit).astype(f32)
    basis_here = lax.dynamic_slice_in_dim(factor_basis, v * width, width, 1)
    hidden_grad = (sums[0] + dot_first(mix_total, basis_here)).astype(bf16)

    basis_part, rows_part, _ = lax.optimization_barrier(
        (basis_part, rows_part, from_x[min(1, n_z - 1)])
    )
    basis_two = basis_part + swap_x(basis_part.astype(bf16)).astype(f32)
    basis_grad = basis_two + swap_core(basis_two)
    rows_two = rows_part + swap_x(rows_part)
    rows_grad = rows_two + swap_core(rows_two)
    return hidden_grad, rows_grad, basis_grad


def on_many(hidden, head, factor_rows, factor_basis, targets, loss_mask):
    n_vocab = lax.axis_size("vocab")
    n_tok = lax.axis_size("tok")
    vocab_index = lax.axis_index("vocab")
    rows_here = head.shape[0] * n_tok
    new_here = factor_rows.shape[0]
    width_here = hidden.shape[1]
    gathered = lax.all_gather(hidden, "vocab", axis=1, tiled=True)
    head_full = lax.all_gather(head, "tok", axis=0, tiled=True)
    frozen = dot_last(gathered, head_full)
    hidden_basis = dot_last(gathered, factor_basis).astype(bf16)
    fresh_logits = dot_last(hidden_basis, factor_rows)
    local_max = jnp.maximum(jnp.max(frozen, axis=1), jnp.max(fresh_logits, axis=1))
    row_top = lax.pmax(local_max, "vocab")
    local_sum = jnp.sum(jnp.exp(frozen - row_top[:, None]), axis=1) + jnp.sum(
        jnp.exp(fresh_logits - row_top[:, None]), axis=1
    )
    sum_exp = lax.psum(local_sum, "vocab")
    frozen_prob = jnp.exp(frozen - row_top[:, None]) / sum_exp[:, None]
    fresh_prob = jnp.exp(fresh_logits - row_top[:, None]) / sum_exp[:, None]
    frozen_offset = targets - vocab_index * rows_here
    fresh_offset = targets - rows_here * n_vocab - vocab_index * new_here
    frozen_hit = (
        lax.broadcasted_iota(jnp.int32, frozen.shape, 1) == frozen_offset[:, None]
    ).astype(f32)
    fresh_hit = (
        lax.broadcasted_iota(jnp.int32, fresh_logits.shape, 1) == fresh_offset[:, None]
    ).astype(f32)
    weight_row = loss_scale * loss_mask.astype(f32)[:, None]
    frozen_grad = (weight_row * (frozen_prob - frozen_hit)).astype(bf16)
    fresh_grad = (weight_row * (fresh_prob - fresh_hit)).astype(bf16)
    mix_term = jnp.dot(fresh_grad, factor_rows, preferred_element_type=f32)
    mix_total = lax.psum(mix_term, "vocab").astype(bf16)
    grad_part = lax.psum_scatter(
        lax.dot_general(
            head_full, frozen_grad, (((0,), (1,)), ((), ())), preferred_element_type=f32
        ),
        "vocab",
        scatter_dimension=0,
        tiled=True,
    )
    basis_cols = lax.dynamic_slice_in_dim(factor_basis, vocab_index * width_here, width_here, 1)
    hidden_grad = (
        grad_part.T + jnp.dot(mix_total, basis_cols, preferred_element_type=f32)
    ).astype(bf16)
    rows_term = dot_first(fresh_grad, hidden_basis)
    basis_term = dot_first(mix_total, hidden)
    rows_grad, basis_grad = (
        lax.psum(rows_term.astype(bf16), "tok").astype(f32),
        lax.psum(basis_term.astype(bf16), "tok").astype(f32),
    )
    return hidden_grad, rows_grad, basis_grad


def solution(mesh):
    in_specs = (
        P("tok", "vocab"),
        P(("vocab", "tok"), None),
        P("vocab", None),
        P(),
        P("tok"),
        P("tok"),
    )
    out_specs = (P("tok", "vocab"), P("vocab", None), P(None, "vocab"))
    few = mesh.shape["vocab"] <= 16 and mesh.shape["tok"] == 4
    return jax.shard_map(
        on_few if few else on_many,
        mesh=mesh,
        in_specs=in_specs,
        out_specs=out_specs,
        check_vma=False,
    )
```

```python
import jax
import jax.numpy as jnp
from jax import lax
from jax.experimental import pallas as pl
from jax.experimental.pallas import tpu as pltpu
from jax.sharding import PartitionSpec as P

loss_scale = 64.0
f32 = jnp.float32
bf16 = jnp.bfloat16
contract_last = (((1,), (1,)), ((), ()))
contract_first = (((0,), (0,)), ((), ()))


def dot_last(a, b):
    return lax.dot_general(a, b, contract_last, preferred_element_type=f32)


def dot_first(a, b):
    return lax.dot_general(a, b, contract_first, preferred_element_type=f32)


def swap(value, axis, bit):
    size = lax.axis_size(axis)
    return lax.ppermute(value, axis, [(i, i ^ bit) for i in range(size)])


def swap_core(value):
    return swap(value, "tok", 1)


def swap_x(value):
    return swap(value, "tok", 2)


def swap_y(value):
    return swap(value, "vocab", 1)


def swap_z(value, step):
    return swap(value, "vocab", 2 * step)


in_vmem = pl.BlockSpec(memory_space=pltpu.VMEM)


def copy_blocks(shapes, moves, *arrays, source=pltpu.HBM):
    def kernel(*refs):
        ins, outs, sems = refs[: len(arrays)], refs[len(arrays) : -1], refs[-1]
        copies = []
        for n, (origin, columns, target, row, column) in enumerate(moves()):
            src, dst = ins[origin], outs[target]
            if columns is not None:
                src = src.at[:, pl.ds(pl.multiple_of(columns[0], 128), columns[1])]
            dst = dst.at[pl.ds(row, src.shape[0]), pl.ds(column, src.shape[1])]
            copies.append(pltpu.make_async_copy(src, dst, sems.at[n]))
        for copy in copies:
            copy.start()
        for copy in copies:
            copy.wait()

    size = sum(2 * shape[0] * shape[1] for shape in shapes)
    return pl.pallas_call(
        kernel,
        out_shape=[jax.ShapeDtypeStruct(shape, bf16) for shape in shapes],
        in_specs=[pl.BlockSpec(memory_space=source)] * len(arrays),
        out_specs=[in_vmem] * len(shapes),
        scratch_shapes=[pltpu.SemaphoreType.DMA((32,))],
        compiler_params=pltpu.CompilerParams(vmem_limit_bytes=12 << 20),
        cost_estimate=pl.CostEstimate(flops=0, bytes_accessed=2 * size, transcendentals=0),
    )(*arrays)


def logits_of(groups, tokens):
    toks, width = tokens[0].shape
    heights = [group[0].shape[0] for group in groups]
    total, depth = sum(heights), width * len(tokens)
    flat = [a for group in groups for a in group]
    n_flat, n_all = len(flat), len(flat) + len(tokens)

    def kernel(*refs):
        out = refs[n_all]
        at, row = 0, 0
        for group, height in zip(groups, heights):
            result, column = None, 0
            for part in group:
                for c in range(0, part.shape[1], width):
                    token = refs[n_flat + (column + c) // width]
                    term = dot_last(refs[at][:, c : c + width], token[...])
                    result = term if result is None else result + term
                at, column = at + 1, column + part.shape[1]
            out[row : row + height, :] = result
            row += height

    return pl.pallas_call(
        kernel,
        out_shape=jax.ShapeDtypeStruct((total, toks), f32),
        in_specs=[in_vmem] * n_all,
        out_specs=in_vmem,
        compiler_params=pltpu.CompilerParams(vmem_limit_bytes=12 << 20),
        cost_estimate=pl.CostEstimate(
            flops=2 * total * depth * toks,
            bytes_accessed=2 * (total + toks) * depth + 4 * total * toks,
            transcendentals=0,
        ),
    )(*flat, *tokens)


def on_few(hidden, head, factor_rows, factor_basis, targets, loss_mask):
    n_z = lax.axis_size("vocab") // 2
    n_tok = lax.axis_size("tok")
    bits = [1 << b for b in range(n_z.bit_length() - 1)]
    v = lax.axis_index("vocab")
    t = lax.axis_index("tok")
    toks, width = hidden.shape
    rows = head.shape[0]
    new_here = factor_rows.shape[0]
    rank = factor_basis.shape[0]
    depth = n_z * width

    def start_of(j, other):
        return (lax.axis_index("vocab") ^ (2 * j + other)) * width

    cuts = [0, n_z // 2, 3 * n_z // 4, n_z] if n_z > 2 else list(range(n_z + 1))
    chunks = [range(a, b) for a, b in zip(cuts, cuts[1:])]
    sends = copy_blocks(
        [(rows, len(chunk) * width) for chunk in chunks],
        lambda: [
            (0, (start_of(j, 1), width), n, 0, (j - chunk[0]) * width)
            for n, chunk in enumerate(chunks)
            for j in chunk
        ],
        head,
    )
    beside = []
    for n, send in enumerate(sends):
        if n > 1:
            send, _ = lax.optimization_barrier((send, beside[0]))
        beside.append(swap_y(send))

    shards = {0: hidden}
    for bit in reversed(bits):
        near = swap_z(hidden, bit)
        for j in [j for j in shards if j]:
            shards[j], _ = lax.optimization_barrier((shards[j], near))
            shards[j ^ bit] = swap_z(shards[j], bit)
        shards[bit] = near
    cross = {}
    for j in range(n_z):
        sent = shards[j]
        if j > 1:
            sent, _ = lax.optimization_barrier((sent, cross[j - 2]))
        cross[j] = swap_x(sent)

    head_after, basis_after, _ = lax.optimization_barrier(
        (head, factor_basis, cross[0])
    )
    kept, basis_half = copy_blocks(
        [(rows, depth), (rank, depth)],
        lambda: [
            (a, (start_of(j, 0), width), a, 0, j * width) for j in range(n_z) for a in range(2)
        ],
        head_after,
        basis_after,
    )
    kept_core = swap_core(kept)
    beside_core = []
    for n, came in enumerate(beside):
        after = shards[n_z - 1] if n else cross[min(1, n_z - 1)]
        came, _ = lax.optimization_barrier((came, after))
        beside_core.append(swap_core(came))

    in_order = lambda parts: [parts[j] for j in range(n_z)]
    upper = [[kept], [kept_core], [basis_half]]
    upper_own = logits_of(upper, in_order(shards))
    beside_core[-1], _ = lax.optimization_barrier((beside_core[-1], upper_own))
    lower_own = logits_of([beside, beside_core], in_order(shards))
    both_cross = logits_of(upper + [beside, beside_core], in_order(cross))
    n_up = 2 * rows + rank

    def add_over_y(up, low, up_came, low_came):
        near = up[: 2 * rows] + low_came
        far = low + up_came[: 2 * rows]
        return near, far, (up[2 * rows :] + up_came[2 * rows :]).astype(bf16)

    upper_came, lower_came = swap_y(upper_own), swap_y(lower_own)
    cross_came = swap_y(both_cross)
    near_own, far_own, basis_own = add_over_y(upper_own, lower_own, upper_came, lower_came)
    near_cross, far_cross, basis_cross = add_over_y(
        both_cross[:n_up], both_cross[n_up:], cross_came[:n_up], cross_came[n_up:]
    )
    hidden_basis = jnp.concatenate([basis_own, basis_cross], axis=1)

    near_rows, _ = lax.optimization_barrier((factor_rows, beside[-1]))
    rows_came = swap_y(near_rows)
    row_blocks = [0, 1]
    rows_came, _ = lax.optimization_barrier((rows_came, upper_own))
    rows_all = jnp.concatenate([factor_rows, rows_came], axis=0)
    for bit in [2 * b for b in reversed(bits)]:
        rows_all = jnp.concatenate([rows_all, swap(rows_all, "vocab", bit)], axis=0)
        row_blocks = row_blocks + [j ^ bit for j in row_blocks]

    def merge(a, b):
        top = jnp.maximum(a[0], b[0])
        return jnp.stack([top, a[1] * jnp.exp(a[0] - top) + b[1] * jnp.exp(b[0] - top)])

    def local(*logits):
        top = jnp.max(logits[0], axis=0)
        for l in logits[1:]:
            top = jnp.maximum(top, jnp.max(l, axis=0))
        total = jnp.sum(jnp.exp(logits[0] - top[None, :]), axis=0)
        for l in logits[1:]:
            total = total + jnp.sum(jnp.exp(l - top[None, :]), axis=0)
        return jnp.stack([top, total])

    info = jnp.stack([targets.astype(f32), loss_mask.astype(f32)])
    stats = jnp.concatenate([local(near_own, far_own), local(near_cross, far_cross)], axis=1)
    sent = jnp.concatenate([stats, jnp.concatenate([info, info], axis=1)], axis=0)
    came = swap_x(sent)
    stats = merge(stats, jnp.concatenate([came[:2, toks:], came[:2, :toks]], axis=1))
    info = jnp.concatenate([info, came[2:, :toks]], axis=1)
    target_row = info[0].astype(jnp.int32)
    weight_row = loss_scale * info[1]
    for bit in bits:
        stats = merge(stats, swap_z(stats, bit))
    fresh = lax.dot_general(
        rows_all, hidden_basis, (((1,), (0,)), ((), ())), preferred_element_type=f32
    )
    stats = merge(stats, local(fresh))
    row_top, sum_exp = stats[0], stats[1]
    scale_row = weight_row / sum_exp

    row_iota = lax.broadcasted_iota(jnp.int32, (rows, 1), 0)

    def grad_of(frozen, vv, cols):
        row_ids = jnp.concatenate(
            [row_iota + (vv * n_tok + tt) * rows for tt in (t, t ^ 1)], axis=0
        )
        hit = jnp.where(row_ids == target_row[None, cols], weight_row[None, cols], 0.0)
        return (jnp.exp(frozen - row_top[None, cols]) * scale_row[None, cols] - hit).astype(bf16)

    at_own, at_cross = slice(0, toks), slice(toks, 2 * toks)
    grad_cross = (grad_of(near_cross, v, at_cross), grad_of(far_cross, v ^ 1, at_cross))
    grad_own = (grad_of(near_own, v, at_own), grad_of(far_own, v ^ 1, at_own))

    laid = [kept, kept_core] + beside + beside_core
    laid[0], _ = lax.optimization_barrier((kept, both_cross))
    places, row = [], 0
    for group in ([kept], [kept_core], beside, beside_core):
        column = 0
        for array in group:
            places.append((len(places), None, 0, row, column))
            column += array.shape[1]
        row += rows
    (weights,) = copy_blocks([(4 * rows, depth)], lambda: places, *laid, source=pltpu.VMEM)

    def part(grads, j):
        return dot_first(grads, weights[:, j * width : (j + 1) * width])

    grad_cross = jnp.concatenate(grad_cross, axis=0)
    grad_own = jnp.concatenate(grad_own, axis=0)
    sums, from_x, first_z = {}, {}, None
    for j in reversed(range(n_z)):
        send = part(grad_cross, j).astype(bf16)
        if j + 2 in from_x:
            send, _, _ = lax.optimization_barrier((send, from_x[j + 2], first_z))
        first_send = send if j == n_z - 1 else first_send
        from_x[j] = swap_x(send)
        sums[j] = part(grad_own, j) + from_x[j].astype(f32)
        if first_z is None:
            first_z = sums[j].astype(bf16)
    fresh, _ = lax.optimization_barrier((fresh, first_send))
    frozen_rows = rows * n_tok * lax.axis_size("vocab")
    new_iota = lax.broadcasted_iota(jnp.int32, (new_here, 1), 0) + frozen_rows
    fresh_ids = jnp.concatenate([new_iota + (v ^ j) * new_here for j in row_blocks], axis=0)
    fresh_hit = jnp.where(fresh_ids == targets[None, :], weight_row[None, :toks], 0.0)
    fresh_grad = (
        jnp.exp(fresh[:, :toks] - row_top[None, :toks]) * scale_row[None, :toks] - fresh_hit
    ).astype(bf16)
    mix_total = dot_first(rows_all, fresh_grad).astype(bf16)
    rows_part = dot_last(fresh_grad[:new_here], hidden_basis[:, :toks])
    basis_part = jnp.dot(mix_total, hidden, preferred_element_type=f32)

    for bit in bits:
        for j in [j for j in sorted(sums, reverse=True) if j & bit]:
            total = sums.pop(j)
            send = first_z if j == n_z - 1 else total.astype(bf16)
            sums[j ^ bit] = sums[j ^ bit] + swap_z(send, bit).astype(f32)
    basis_here = lax.dynamic_slice_in_dim(factor_basis, v * width, width, 1)
    hidden_grad = (sums[0] + dot_first(mix_total, basis_here)).astype(bf16)

    basis_two = lax.reduce_precision(basis_part + swap_core(basis_part), 8, 7)
    rows_two = rows_part + swap_core(rows_part)
    basis_two, rows_two, _ = lax.optimization_barrier(
        (basis_two, rows_two, from_x[min(1, n_z - 1)])
    )
    basis_grad = basis_two + swap_x(basis_two.astype(bf16)).astype(f32)
    rows_grad = rows_two + swap_x(rows_two)
    return hidden_grad, rows_grad, basis_grad


def on_many(hidden, head, factor_rows, factor_basis, targets, loss_mask):
    n_vocab = lax.axis_size("vocab")
    n_tok = lax.axis_size("tok")
    vocab_index = lax.axis_index("vocab")
    rows_here = head.shape[0] * n_tok
    new_here = factor_rows.shape[0]
    width_here = hidden.shape[1]
    gathered = lax.all_gather(hidden, "vocab", axis=1, tiled=True)
    head_full = lax.all_gather(head, "tok", axis=0, tiled=True)
    frozen = dot_last(gathered, head_full)
    hidden_basis = dot_last(gathered, factor_basis).astype(bf16)
    fresh_logits = dot_last(hidden_basis, factor_rows)
    local_max = jnp.maximum(jnp.max(frozen, axis=1), jnp.max(fresh_logits, axis=1))
    row_top = lax.pmax(local_max, "vocab")
    local_sum = jnp.sum(jnp.exp(frozen - row_top[:, None]), axis=1) + jnp.sum(
        jnp.exp(fresh_logits - row_top[:, None]), axis=1
    )
    sum_exp = lax.psum(local_sum, "vocab")
    frozen_prob = jnp.exp(frozen - row_top[:, None]) / sum_exp[:, None]
    fresh_prob = jnp.exp(fresh_logits - row_top[:, None]) / sum_exp[:, None]
    frozen_offset = targets - vocab_index * rows_here
    fresh_offset = targets - rows_here * n_vocab - vocab_index * new_here
    frozen_hit = (
        lax.broadcasted_iota(jnp.int32, frozen.shape, 1) == frozen_offset[:, None]
    ).astype(f32)
    fresh_hit = (
        lax.broadcasted_iota(jnp.int32, fresh_logits.shape, 1) == fresh_offset[:, None]
    ).astype(f32)
    weight_row = loss_scale * loss_mask.astype(f32)[:, None]
    frozen_grad = (weight_row * (frozen_prob - frozen_hit)).astype(bf16)
    fresh_grad = (weight_row * (fresh_prob - fresh_hit)).astype(bf16)
    mix_term = jnp.dot(fresh_grad, factor_rows, preferred_element_type=f32)
    mix_total = lax.psum(mix_term, "vocab").astype(bf16)
    grad_part = lax.psum_scatter(
        lax.dot_general(
            head_full, frozen_grad, (((0,), (1,)), ((), ())), preferred_element_type=f32
        ),
        "vocab",
        scatter_dimension=0,
        tiled=True,
    )
    basis_cols = lax.dynamic_slice_in_dim(factor_basis, vocab_index * width_here, width_here, 1)
    hidden_grad = (
        grad_part.T + jnp.dot(mix_total, basis_cols, preferred_element_type=f32)
    ).astype(bf16)
    rows_term = dot_first(fresh_grad, hidden_basis)
    basis_term = dot_first(mix_total, hidden)
    rows_grad, basis_grad = (
        lax.psum(rows_term.astype(bf16), "tok").astype(f32),
        lax.psum(basis_term.astype(bf16), "tok").astype(f32),
    )
    return hidden_grad, rows_grad, basis_grad


def solution(mesh):
    in_specs = (
        P("tok", "vocab"),
        P(("vocab", "tok"), None),
        P("vocab", None),
        P(),
        P("tok"),
        P("tok"),
    )
    out_specs = (P("tok", "vocab"), P("vocab", None), P(None, "vocab"))
    few = mesh.shape["vocab"] <= 16 and mesh.shape["tok"] == 4
    return jax.shard_map(
        on_few if few else on_many,
        mesh=mesh,
        in_specs=in_specs,
        out_specs=out_specs,
        check_vma=False,
    )
```

```python
import jax
import jax.numpy as jnp
from jax import lax
from jax.experimental import pallas as pl
from jax.experimental.pallas import tpu as pltpu
from jax.sharding import PartitionSpec as P

loss_scale = 64.0
f32 = jnp.float32
bf16 = jnp.bfloat16
contract_last = (((1,), (1,)), ((), ()))
contract_first = (((0,), (0,)), ((), ()))


def dot_last(a, b):
    return lax.dot_general(a, b, contract_last, preferred_element_type=f32)


def dot_first(a, b):
    return lax.dot_general(a, b, contract_first, preferred_element_type=f32)


def swap(value, axis, bit):
    size = lax.axis_size(axis)
    return lax.ppermute(value, axis, [(i, i ^ bit) for i in range(size)])


def swap_core(value):
    return swap(value, "tok", 1)


def swap_x(value):
    return swap(value, "tok", 2)


def swap_y(value):
    return swap(value, "vocab", 1)


def swap_z(value, step):
    return swap(value, "vocab", 2 * step)


in_vmem = pl.BlockSpec(memory_space=pltpu.VMEM)


def copy_blocks(shapes, moves, *arrays, source=pltpu.HBM):
    def kernel(*refs):
        ins, outs, sems = refs[: len(arrays)], refs[len(arrays) : -1], refs[-1]
        copies = []
        for n, (origin, columns, target, row, column) in enumerate(moves()):
            src, dst = ins[origin], outs[target]
            if columns is not None:
                src = src.at[:, pl.ds(pl.multiple_of(columns[0], 128), columns[1])]
            dst = dst.at[pl.ds(row, src.shape[0]), pl.ds(column, src.shape[1])]
            copies.append(pltpu.make_async_copy(src, dst, sems.at[n]))
        for copy in copies:
            copy.start()
        for copy in copies:
            copy.wait()

    size = sum(2 * shape[0] * shape[1] for shape in shapes)
    return pl.pallas_call(
        kernel,
        out_shape=[jax.ShapeDtypeStruct(shape, bf16) for shape in shapes],
        in_specs=[pl.BlockSpec(memory_space=source)] * len(arrays),
        out_specs=[in_vmem] * len(shapes),
        scratch_shapes=[pltpu.SemaphoreType.DMA((32,))],
        compiler_params=pltpu.CompilerParams(vmem_limit_bytes=12 << 20),
        cost_estimate=pl.CostEstimate(flops=0, bytes_accessed=2 * size, transcendentals=0),
    )(*arrays)


def logits_of(groups, tokens):
    toks, width = tokens[0].shape
    heights = [group[0].shape[0] for group in groups]
    total, depth = sum(heights), width * len(tokens)
    flat = [a for group in groups for a in group]
    n_flat, n_all = len(flat), len(flat) + len(tokens)

    def kernel(*refs):
        out = refs[n_all]
        at, row = 0, 0
        for group, height in zip(groups, heights):
            result, column = None, 0
            for part in group:
                for c in range(0, part.shape[1], width):
                    token = refs[n_flat + (column + c) // width]
                    term = dot_last(refs[at][:, c : c + width], token[...])
                    result = term if result is None else result + term
                at, column = at + 1, column + part.shape[1]
            out[row : row + height, :] = result
            row += height

    return pl.pallas_call(
        kernel,
        out_shape=jax.ShapeDtypeStruct((total, toks), f32),
        in_specs=[in_vmem] * n_all,
        out_specs=in_vmem,
        compiler_params=pltpu.CompilerParams(vmem_limit_bytes=12 << 20),
        cost_estimate=pl.CostEstimate(
            flops=2 * total * depth * toks,
            bytes_accessed=2 * (total + toks) * depth + 4 * total * toks,
            transcendentals=0,
        ),
    )(*flat, *tokens)


def on_few(hidden, head, factor_rows, factor_basis, targets, loss_mask):
    n_vocab, n_tok = lax.axis_size("vocab"), lax.axis_size("tok")
    n_z = n_vocab // 2
    bits = [1 << b for b in range(n_z.bit_length() - 1)]
    v = lax.axis_index("vocab")
    t = lax.axis_index("tok")
    toks, width = hidden.shape
    rows = head.shape[0]
    new_here = factor_rows.shape[0]
    rank = factor_basis.shape[0]
    depth = n_z * width

    near_first = v * (n_tok * rows) + (t >> 1) * (2 * rows)
    far_first = (v ^ 1) * (n_tok * rows) + (t >> 1) * (2 * rows)
    turn = (t & 1) * rows
    new_first = v * new_here
    hidden, head, near_first, far_first, turn, new_first = lax.optimization_barrier(
        (hidden, head, near_first, far_first, turn, new_first)
    )

    def start_of(j, other):
        return (lax.axis_index("vocab") ^ (2 * j + other)) * width

    cuts = [0, n_z // 2, 3 * n_z // 4, n_z] if n_z > 2 else list(range(n_z + 1))
    chunks = [range(a, b) for a, b in zip(cuts, cuts[1:])]
    sends = copy_blocks(
        [(rows, len(chunk) * width) for chunk in chunks],
        lambda: [
            (0, (start_of(j, 1), width), n, 0, (j - chunk[0]) * width)
            for n, chunk in enumerate(chunks)
            for j in chunk
        ],
        head,
    )
    beside = [swap_y(sends[0])]

    head_after, basis_after, _ = lax.optimization_barrier((head, factor_basis, sends[0]))
    kept, basis_half = copy_blocks(
        [(rows, depth), (rank, depth)],
        lambda: [
            (a, (start_of(j, 0), width), a, 0, j * width) for j in range(n_z) for a in range(2)
        ],
        head_after,
        basis_after,
    )

    hidden, _ = lax.optimization_barrier((hidden, kept))
    shards, cross = {0: hidden}, {0: swap_x(hidden)}
    for bit in reversed(bits):
        near = swap_z(hidden, bit)
        for j in [j for j in shards if j]:
            shards[j], _, _ = lax.optimization_barrier((shards[j], near, cross[0]))
            shards[j ^ bit] = swap_z(shards[j], bit)
        shards[bit] = near
    for n, send in list(enumerate(sends))[1:]:
        send, _ = lax.optimization_barrier((send, shards[bits[0]] if n == 1 else beside[n - 2]))
        beside.append(swap_y(send))
    for j in range(1, n_z):
        sent = shards[j]
        if j > 1:
            sent, _, _ = lax.optimization_barrier((sent, cross[j - 2], beside[j // 2 - 1]))
        cross[j] = swap_x(sent)

    kept_core = swap_core(kept)
    beside_core = []
    for n, came in enumerate(beside):
        if n < len(beside) - 1:
            came, _ = lax.optimization_barrier((came, cross[max(0, n_z - 2)]))
        beside_core.append(swap_core(came))

    rows_all, _ = lax.optimization_barrier((factor_rows, shards[n_z - 1]))
    for bit in bits:
        rows_all = jnp.concatenate([rows_all, swap_z(rows_all, bit)], axis=0)
    basis_ready, _, _ = lax.optimization_barrier((basis_half, rows_all, cross[n_z - 1]))

    in_order = lambda parts: [parts[j] for j in range(n_z)]
    upper = [[kept], [kept_core], [basis_ready]]
    upper_own = logits_of(upper, in_order(shards))
    beside_core[-1], _ = lax.optimization_barrier((beside_core[-1], upper_own))
    lower_own = logits_of([beside, beside_core], in_order(shards))
    both_cross = logits_of(upper + [beside, beside_core], in_order(cross))
    n_up = 2 * rows + rank

    def add_over_y(up, low, up_came, low_came):
        near = up[: 2 * rows] + low_came
        far = low + up_came[: 2 * rows]
        return near, far, (up[2 * rows :] + up_came[2 * rows :]).astype(bf16)

    upper_came, lower_came = swap_y(upper_own), swap_y(lower_own)
    cross_came = swap_y(both_cross)
    near_own, far_own, basis_own = add_over_y(upper_own, lower_own, upper_came, lower_came)
    near_cross, far_cross, basis_cross = add_over_y(
        both_cross[:n_up], both_cross[n_up:], cross_came[:n_up], cross_came[n_up:]
    )
    hidden_basis = jnp.concatenate([basis_own, basis_cross], axis=1)

    rows_after, _ = lax.optimization_barrier((rows_all, upper_own))
    rows_all = jnp.concatenate([rows_all, swap_y(rows_after)], axis=0)

    def merge(a, b):
        top = jnp.maximum(a[0], b[0])
        return jnp.stack([top, a[1] * jnp.exp(a[0] - top) + b[1] * jnp.exp(b[0] - top)])

    def local(*logits):
        top = jnp.max(logits[0], axis=0)
        for l in logits[1:]:
            top = jnp.maximum(top, jnp.max(l, axis=0))
        total = jnp.sum(jnp.exp(logits[0] - top[None, :]), axis=0)
        for l in logits[1:]:
            total = total + jnp.sum(jnp.exp(l - top[None, :]), axis=0)
        return jnp.stack([top, total])

    info = jnp.stack([targets.astype(f32), loss_mask.astype(f32)])
    stats = jnp.concatenate([local(near_own, far_own), local(near_cross, far_cross)], axis=1)
    sent = jnp.concatenate([stats, jnp.concatenate([info, info], axis=1)], axis=0)
    came = swap_x(sent)
    stats = merge(stats, jnp.concatenate([came[:2, toks:], came[:2, :toks]], axis=1))
    info = jnp.concatenate([info, came[2:, :toks]], axis=1)
    target_row = info[0].astype(jnp.int32)
    weight_row = loss_scale * info[1]
    for bit in bits:
        stats = merge(stats, swap_z(stats, bit))
    fresh = lax.dot_general(
        rows_all, hidden_basis, (((1,), (0,)), ((), ())), preferred_element_type=f32
    )
    stats = merge(stats, local(fresh))
    row_top, sum_exp = stats[0], stats[1]
    scale_row = weight_row / sum_exp

    def grad_of(frozen, first, cols):
        row_ids = (lax.broadcasted_iota(jnp.int32, frozen.shape, 0) ^ turn) + first
        hit = jnp.where(row_ids == target_row[None, cols], weight_row[None, cols], 0.0)
        return (jnp.exp(frozen - row_top[None, cols]) * scale_row[None, cols] - hit).astype(bf16)

    at_own, at_cross = slice(0, toks), slice(toks, 2 * toks)
    grad_cross = (grad_of(near_cross, near_first, at_cross), grad_of(far_cross, far_first, at_cross))
    grad_own = (grad_of(near_own, near_first, at_own), grad_of(far_own, far_first, at_own))

    laid = [kept, kept_core] + beside + beside_core
    laid[0], _ = lax.optimization_barrier((kept, both_cross))
    places, row = [], 0
    for group in ([kept], [kept_core], beside, beside_core):
        column = 0
        for array in group:
            places.append((len(places), None, 0, row, column))
            column += array.shape[1]
        row += rows
    (weights,) = copy_blocks([(4 * rows, depth)], lambda: places, *laid, source=pltpu.VMEM)

    def part(grads, j):
        return dot_first(grads, weights[:, j * width : (j + 1) * width])

    grad_cross = jnp.concatenate(grad_cross, axis=0)
    grad_own = jnp.concatenate(grad_own, axis=0)
    sums, from_x, first_z = {}, {}, None
    for j in reversed(range(n_z)):
        send = part(grad_cross, j).astype(bf16)
        if j + 2 in from_x:
            send, _, _ = lax.optimization_barrier((send, from_x[j + 2], first_z))
        first_send = send if j == n_z - 1 else first_send
        from_x[j] = swap_x(send)
        sums[j] = part(grad_own, j) + from_x[j].astype(f32)
        if first_z is None:
            first_z = sums[j].astype(bf16)
    fresh, _ = lax.optimization_barrier((fresh, from_x[max(0, n_z - 2)]))
    fresh_iota = lax.broadcasted_iota(jnp.int32, (n_vocab * new_here, toks), 0)
    in_block = fresh_iota & (new_here - 1)
    from_block = fresh_iota - in_block
    from_block = ((from_block & (n_z * new_here - 1)) << 1) + (from_block & (n_z * new_here)) // n_z
    fresh_ids = ((from_block + in_block) ^ new_first) + rows * n_tok * n_vocab
    fresh_hit = jnp.where(fresh_ids == targets[None, :], weight_row[None, :toks], 0.0)
    fresh_grad = (
        jnp.exp(fresh[:, :toks] - row_top[None, :toks]) * scale_row[None, :toks] - fresh_hit
    ).astype(bf16)
    mix_total = dot_first(rows_all, fresh_grad).astype(bf16)
    rows_part = dot_last(fresh_grad[:new_here], hidden_basis[:, :toks])
    basis_part = jnp.dot(mix_total, hidden, preferred_element_type=f32)

    came_z = None
    for bit in bits:
        for j in [j for j in sorted(sums, reverse=True) if j & bit]:
            total = sums.pop(j)
            send = first_z if j == n_z - 1 else total.astype(bf16)
            if bit == bits[0] and came_z is not None:
                send, _ = lax.optimization_barrier((send, came_z))
            came = swap_z(send, bit)
            came_z = came if came_z is None else came_z
            sums[j ^ bit] = sums[j ^ bit] + came.astype(f32)
    hidden_grad = (sums[0] + dot_first(mix_total, basis_half[:, :width])).astype(bf16)

    basis_two = lax.reduce_precision(basis_part + swap_core(basis_part), 8, 7)
    rows_two = rows_part + swap_core(rows_part)
    basis_two, rows_two, _ = lax.optimization_barrier(
        (basis_two, rows_two, from_x[min(1, n_z - 1)])
    )
    basis_grad = basis_two + swap_x(basis_two.astype(bf16)).astype(f32)
    rows_grad = rows_two + swap_x(rows_two)
    return hidden_grad, rows_grad, basis_grad


def on_many(hidden, head, factor_rows, factor_basis, targets, loss_mask):
    n_vocab = lax.axis_size("vocab")
    n_tok = lax.axis_size("tok")
    vocab_index = lax.axis_index("vocab")
    rows_here = head.shape[0] * n_tok
    new_here = factor_rows.shape[0]
    width_here = hidden.shape[1]
    gathered = lax.all_gather(hidden, "vocab", axis=1, tiled=True)
    head_full = lax.all_gather(head, "tok", axis=0, tiled=True)
    frozen = dot_last(gathered, head_full)
    hidden_basis = dot_last(gathered, factor_basis).astype(bf16)
    fresh_logits = dot_last(hidden_basis, factor_rows)
    local_max = jnp.maximum(jnp.max(frozen, axis=1), jnp.max(fresh_logits, axis=1))
    row_top = lax.pmax(local_max, "vocab")
    local_sum = jnp.sum(jnp.exp(frozen - row_top[:, None]), axis=1) + jnp.sum(
        jnp.exp(fresh_logits - row_top[:, None]), axis=1
    )
    sum_exp = lax.psum(local_sum, "vocab")
    frozen_prob = jnp.exp(frozen - row_top[:, None]) / sum_exp[:, None]
    fresh_prob = jnp.exp(fresh_logits - row_top[:, None]) / sum_exp[:, None]
    frozen_offset = targets - vocab_index * rows_here
    fresh_offset = targets - rows_here * n_vocab - vocab_index * new_here
    frozen_hit = (
        lax.broadcasted_iota(jnp.int32, frozen.shape, 1) == frozen_offset[:, None]
    ).astype(f32)
    fresh_hit = (
        lax.broadcasted_iota(jnp.int32, fresh_logits.shape, 1) == fresh_offset[:, None]
    ).astype(f32)
    weight_row = loss_scale * loss_mask.astype(f32)[:, None]
    frozen_grad = (weight_row * (frozen_prob - frozen_hit)).astype(bf16)
    fresh_grad = (weight_row * (fresh_prob - fresh_hit)).astype(bf16)
    mix_term = jnp.dot(fresh_grad, factor_rows, preferred_element_type=f32)
    mix_total = lax.psum(mix_term, "vocab").astype(bf16)
    grad_part = lax.psum_scatter(
        lax.dot_general(
            head_full, frozen_grad, (((0,), (1,)), ((), ())), preferred_element_type=f32
        ),
        "vocab",
        scatter_dimension=0,
        tiled=True,
    )
    basis_cols = lax.dynamic_slice_in_dim(factor_basis, vocab_index * width_here, width_here, 1)
    hidden_grad = (
        grad_part.T + jnp.dot(mix_total, basis_cols, preferred_element_type=f32)
    ).astype(bf16)
    rows_term = dot_first(fresh_grad, hidden_basis)
    basis_term = dot_first(mix_total, hidden)
    rows_grad, basis_grad = (
        lax.psum(rows_term.astype(bf16), "tok").astype(f32),
        lax.psum(basis_term.astype(bf16), "tok").astype(f32),
    )
    return hidden_grad, rows_grad, basis_grad


def solution(mesh):
    in_specs = (
        P("tok", "vocab"),
        P(("vocab", "tok"), None),
        P("vocab", None),
        P(),
        P("tok"),
        P("tok"),
    )
    out_specs = (P("tok", "vocab"), P("vocab", None), P(None, "vocab"))

    def on_device(hidden, head, factor_rows, *rest):
        even = [n & (n - 1) == 0 for n in (mesh.shape["vocab"], head.shape[0], factor_rows.shape[0])]
        few = 2 <= mesh.shape["vocab"] <= 16 and mesh.shape["tok"] == 4 and all(even)
        return (on_few if few else on_many)(hidden, head, factor_rows, *rest)

    return jax.shard_map(
        on_device, mesh=mesh, in_specs=in_specs, out_specs=out_specs, check_vma=False
    )
```

```python
import jax
import jax.numpy as jnp
from jax import lax
from jax.experimental import pallas as pl
from jax.experimental.pallas import tpu as pltpu
from jax.sharding import PartitionSpec as P

loss_scale = 64.0
f32 = jnp.float32
bf16 = jnp.bfloat16
contract_last = (((1,), (1,)), ((), ()))
contract_first = (((0,), (0,)), ((), ()))


def dot_last(a, b):
    return lax.dot_general(a, b, contract_last, preferred_element_type=f32)


def dot_first(a, b):
    return lax.dot_general(a, b, contract_first, preferred_element_type=f32)


def swap(value, axis, bit):
    size = lax.axis_size(axis)
    return lax.ppermute(value, axis, [(i, i ^ bit) for i in range(size)])


def swap_core(value):
    return swap(value, "tok", 1)


def swap_x(value):
    return swap(value, "tok", 2)


def swap_y(value):
    return swap(value, "vocab", 1)


def swap_z(value, step):
    return swap(value, "vocab", 2 * step)


in_vmem = pl.BlockSpec(memory_space=pltpu.VMEM)


def copy_blocks(shapes, moves, *arrays, source=pltpu.HBM, limit=12):
    def kernel(*refs):
        ins, outs, sems = refs[: len(arrays)], refs[len(arrays) : -1], refs[-1]
        copies = []
        for n, (origin, columns, target, row, column) in enumerate(moves()):
            src, dst = ins[origin], outs[target]
            if columns is not None:
                src = src.at[:, pl.ds(pl.multiple_of(columns[0], 128), columns[1])]
            dst = dst.at[pl.ds(row, src.shape[0]), pl.ds(column, src.shape[1])]
            copies.append(pltpu.make_async_copy(src, dst, sems.at[n]))
        for copy in copies:
            copy.start()
        for copy in copies:
            copy.wait()

    size = sum(2 * shape[0] * shape[1] for shape in shapes)
    return pl.pallas_call(
        kernel,
        out_shape=[jax.ShapeDtypeStruct(shape, bf16) for shape in shapes],
        in_specs=[pl.BlockSpec(memory_space=source)] * len(arrays),
        out_specs=[in_vmem] * len(shapes),
        scratch_shapes=[pltpu.SemaphoreType.DMA((32,))],
        compiler_params=pltpu.CompilerParams(vmem_limit_bytes=limit << 20),
        cost_estimate=pl.CostEstimate(flops=0, bytes_accessed=2 * size, transcendentals=0),
    )(*arrays)


def logits_of(groups, tokens):
    toks, width = tokens[0].shape
    heights = [group[0].shape[0] for group in groups]
    total, depth = sum(heights), width * len(tokens)
    flat = [a for group in groups for a in group]
    n_flat, n_all = len(flat), len(flat) + len(tokens)

    def kernel(*refs):
        out = refs[n_all]
        at, row = 0, 0
        for group, height in zip(groups, heights):
            result, column = None, 0
            for part in group:
                for c in range(0, part.shape[1], width):
                    token = refs[n_flat + (column + c) // width]
                    term = dot_last(refs[at][:, c : c + width], token[...])
                    result = term if result is None else result + term
                at, column = at + 1, column + part.shape[1]
            out[row : row + height, :] = result
            row += height

    return pl.pallas_call(
        kernel,
        out_shape=jax.ShapeDtypeStruct((total, toks), f32),
        in_specs=[in_vmem] * n_all,
        out_specs=in_vmem,
        compiler_params=pltpu.CompilerParams(vmem_limit_bytes=12 << 20),
        cost_estimate=pl.CostEstimate(
            flops=2 * total * depth * toks,
            bytes_accessed=2 * (total + toks) * depth + 4 * total * toks,
            transcendentals=0,
        ),
    )(*flat, *tokens)


def on_few(hidden, head, factor_rows, factor_basis, targets, loss_mask):
    n_vocab, n_tok = lax.axis_size("vocab"), lax.axis_size("tok")
    n_z = n_vocab // 2
    bits = [1 << b for b in range(n_z.bit_length() - 1)]
    v = lax.axis_index("vocab")
    t = lax.axis_index("tok")
    toks, width = hidden.shape
    rows = head.shape[0]
    new_here = factor_rows.shape[0]
    rank = factor_basis.shape[0]
    depth = n_z * width

    near_first = v * (n_tok * rows) + (t >> 1) * (2 * rows)
    far_first = (v ^ 1) * (n_tok * rows) + (t >> 1) * (2 * rows)
    turn = (t & 1) * rows
    new_first = v * new_here
    hidden, head, near_first, far_first, turn, new_first = lax.optimization_barrier(
        (hidden, head, near_first, far_first, turn, new_first)
    )

    def start_of(j, other):
        return (lax.axis_index("vocab") ^ (2 * j + other)) * width

    cuts = [0, n_z]
    chunks = [range(a, b) for a, b in zip(cuts, cuts[1:]) if a < b]
    sends = copy_blocks(
        [(rows, len(chunk) * width) for chunk in chunks],
        lambda: [
            (0, (start_of(j, 1), width), n, 0, (j - chunk[0]) * width)
            for n, chunk in enumerate(chunks)
            for j in chunk
        ],
        head,
        limit=56,
    )
    beside = [swap_y(sends[0])]

    def half(array, after):
        array, _ = lax.optimization_barrier((array, after))
        moves = lambda: [(0, (start_of(j, 0), width), 0, 0, j * width) for j in range(n_z)]
        return copy_blocks([(array.shape[0], depth)], moves, array)[0]

    kept = half(head, sends[0])
    kept_core = swap_core(kept)

    z_hidden, _ = lax.optimization_barrier((hidden, sends[0]))
    x_hidden, _ = lax.optimization_barrier((hidden, sends[0]))
    shards, cross = {0: hidden}, {0: swap_x(x_hidden)}
    for bit in reversed(bits):
        near = swap_z(z_hidden, bit)
        for j in [j for j in shards if j]:
            shards[j], *_ = lax.optimization_barrier((shards[j], near, cross[0], kept_core))
            shards[j ^ bit] = swap_z(shards[j], bit)
        shards[bit] = near
    waits = []
    for send, wait in zip(sends[1:], waits):
        send, _ = lax.optimization_barrier((send, wait))
        beside.append(swap_y(send))
    for j in range(1, n_z):
        sent = shards[j]
        if j > 1:
            sent, *_ = lax.optimization_barrier((sent, cross[j - 2], kept_core))
        cross[j] = swap_x(sent)
    basis_half = half(factor_basis, shards[n_z // 2])

    beside_core = []
    for n, came in enumerate(beside):
        came, *_ = lax.optimization_barrier((came, cross[1], cross[n_z - 2], shards[n_z - 1]))
        beside_core.append(swap_core(came))

    in_order = lambda parts: [parts[j] for j in range(n_z)]
    basis_ready, *_ = lax.optimization_barrier((basis_half, cross[n_z - 2], shards[n_z - 1]))
    upper = [[kept], [kept_core], [basis_ready]]
    upper_own = logits_of(upper, in_order(shards))
    beside_core[-1], *_ = lax.optimization_barrier((beside_core[-1], upper_own, cross[n_z - 1]))
    lower_own = logits_of([beside, beside_core], in_order(shards))
    cross[0], _ = lax.optimization_barrier((cross[0], lower_own))
    both_cross = logits_of(upper + [beside, beside_core], in_order(cross))
    n_up = 2 * rows + rank

    def add_over_y(up, low, up_came, low_came):
        near = up[: 2 * rows] + low_came
        far = low + up_came[: 2 * rows]
        return near, far, (up[2 * rows :] + up_came[2 * rows :]).astype(bf16)

    upper_came, lower_came = swap_y(upper_own), swap_y(lower_own)
    cross_came = swap_y(both_cross)
    near_own, far_own, basis_own = add_over_y(upper_own, lower_own, upper_came, lower_came)
    near_cross, far_cross, basis_cross = add_over_y(
        both_cross[:n_up], both_cross[n_up:], cross_came[:n_up], cross_came[n_up:]
    )
    hidden_basis = jnp.concatenate([basis_own, basis_cross], axis=1)

    rows_all, _ = lax.optimization_barrier((factor_rows, both_cross))
    for bit in bits:
        rows_all = jnp.concatenate([rows_all, swap_z(rows_all, bit)], axis=0)
    rows_all = jnp.concatenate([rows_all, swap_y(rows_all)], axis=0)

    def merge(a, b):
        top = jnp.maximum(a[0], b[0])
        return jnp.stack([top, a[1] * jnp.exp(a[0] - top) + b[1] * jnp.exp(b[0] - top)])

    def local(*logits):
        top = jnp.max(logits[0], axis=0)
        for l in logits[1:]:
            top = jnp.maximum(top, jnp.max(l, axis=0))
        total = jnp.sum(jnp.exp(logits[0] - top[None, :]), axis=0)
        for l in logits[1:]:
            total = total + jnp.sum(jnp.exp(l - top[None, :]), axis=0)
        return jnp.stack([top, total])

    info = jnp.stack([targets.astype(f32), loss_mask.astype(f32)])
    stats = jnp.concatenate([local(near_own, far_own), local(near_cross, far_cross)], axis=1)
    sent = jnp.concatenate([stats, jnp.concatenate([info, info], axis=1)], axis=0)
    came = swap_x(sent)
    stats = merge(stats, jnp.concatenate([came[:2, toks:], came[:2, :toks]], axis=1))
    info = jnp.concatenate([info, came[2:, :toks]], axis=1)
    target_row = info[0].astype(jnp.int32)
    weight_row = loss_scale * info[1]
    for bit in bits:
        stats = merge(stats, swap_z(stats, bit))
    fresh = lax.dot_general(
        rows_all, hidden_basis, (((1,), (0,)), ((), ())), preferred_element_type=f32
    )
    stats = merge(stats, local(fresh))
    row_top, sum_exp = stats[0], stats[1]
    scale_row = weight_row / sum_exp

    def grad_of(frozen, first, cols):
        row_ids = (lax.broadcasted_iota(jnp.int32, frozen.shape, 0) ^ turn) + first
        hit = jnp.where(row_ids == target_row[None, cols], weight_row[None, cols], 0.0)
        return (jnp.exp(frozen - row_top[None, cols]) * scale_row[None, cols] - hit).astype(bf16)

    at_own, at_cross = slice(0, toks), slice(toks, 2 * toks)
    grad_cross = (grad_of(near_cross, near_first, at_cross), grad_of(far_cross, far_first, at_cross))
    grad_own = (grad_of(near_own, near_first, at_own), grad_of(far_own, far_first, at_own))

    laid = [kept, kept_core] + beside + beside_core
    laid[0], _ = lax.optimization_barrier((kept, both_cross))
    places, row = [], 0
    for group in ([kept], [kept_core], beside, beside_core):
        column = 0
        for array in group:
            places.append((len(places), None, 0, row, column))
            column += array.shape[1]
        row += rows
    (weights,) = copy_blocks([(4 * rows, depth)], lambda: places, *laid, source=pltpu.VMEM)

    def part(grads, j):
        return dot_first(grads, weights[:, j * width : (j + 1) * width])

    grad_cross = jnp.concatenate(grad_cross, axis=0)
    grad_own = jnp.concatenate(grad_own, axis=0)
    sums, from_x, first_z = {}, {}, None
    for j in reversed(range(n_z)):
        send = part(grad_cross, j).astype(bf16)
        if j + 2 in from_x:
            send, _, _ = lax.optimization_barrier((send, from_x[j + 2], first_z))
        first_send = send if j == n_z - 1 else first_send
        from_x[j] = swap_x(send)
        sums[j] = part(grad_own, j) + from_x[j].astype(f32)
        if first_z is None:
            first_z = sums[j].astype(bf16)
    fresh, _ = lax.optimization_barrier((fresh, from_x[max(0, n_z - 2)]))
    fresh_iota = lax.broadcasted_iota(jnp.int32, (n_vocab * new_here, toks), 0)
    in_block = fresh_iota & (new_here - 1)
    from_block = fresh_iota - in_block
    from_block = ((from_block & (n_z * new_here - 1)) << 1) + (from_block & (n_z * new_here)) // n_z
    fresh_ids = ((from_block + in_block) ^ new_first) + rows * n_tok * n_vocab
    fresh_hit = jnp.where(fresh_ids == targets[None, :], weight_row[None, :toks], 0.0)
    fresh_grad = (
        jnp.exp(fresh[:, :toks] - row_top[None, :toks]) * scale_row[None, :toks] - fresh_hit
    ).astype(bf16)
    mix_total = dot_first(rows_all, fresh_grad).astype(bf16)
    rows_part = dot_last(fresh_grad[:new_here], hidden_basis[:, :toks])
    basis_part = jnp.dot(mix_total, hidden, preferred_element_type=f32)

    came_z = None
    for bit in bits:
        for j in [j for j in sorted(sums, reverse=True) if j & bit]:
            total = sums.pop(j)
            send = first_z if j == n_z - 1 else total.astype(bf16)
            if bit == bits[0] and came_z is not None:
                send, _ = lax.optimization_barrier((send, came_z))
            came = swap_z(send, bit)
            came_z = came if came_z is None else came_z
            sums[j ^ bit] = sums[j ^ bit] + came.astype(f32)
    hidden_grad = (sums[0] + dot_first(mix_total, basis_half[:, :width])).astype(bf16)

    factor_part = jnp.concatenate([basis_part, rows_part], axis=1)
    factor_two = lax.reduce_precision(factor_part + swap_core(factor_part), 8, 7)
    factor_two, _ = lax.optimization_barrier((factor_two, from_x[min(1, n_z - 1)]))
    factor_grad = factor_two + swap_x(factor_two.astype(bf16)).astype(f32)
    basis_grad, rows_grad = factor_grad[:, :width], factor_grad[:, width:]
    return hidden_grad, rows_grad, basis_grad


def on_many(hidden, head, factor_rows, factor_basis, targets, loss_mask):
    n_vocab = lax.axis_size("vocab")
    n_tok = lax.axis_size("tok")
    vocab_index = lax.axis_index("vocab")
    rows_here = head.shape[0] * n_tok
    new_here = factor_rows.shape[0]
    width_here = hidden.shape[1]
    gathered = lax.all_gather(hidden, "vocab", axis=1, tiled=True)
    head_full = lax.all_gather(head, "tok", axis=0, tiled=True)
    frozen = dot_last(gathered, head_full)
    hidden_basis = dot_last(gathered, factor_basis).astype(bf16)
    fresh_logits = dot_last(hidden_basis, factor_rows)
    local_max = jnp.maximum(jnp.max(frozen, axis=1), jnp.max(fresh_logits, axis=1))
    row_top = lax.pmax(local_max, "vocab")
    local_sum = jnp.sum(jnp.exp(frozen - row_top[:, None]), axis=1) + jnp.sum(
        jnp.exp(fresh_logits - row_top[:, None]), axis=1
    )
    sum_exp = lax.psum(local_sum, "vocab")
    frozen_prob = jnp.exp(frozen - row_top[:, None]) / sum_exp[:, None]
    fresh_prob = jnp.exp(fresh_logits - row_top[:, None]) / sum_exp[:, None]
    frozen_offset = targets - vocab_index * rows_here
    fresh_offset = targets - rows_here * n_vocab - vocab_index * new_here
    frozen_hit = (
        lax.broadcasted_iota(jnp.int32, frozen.shape, 1) == frozen_offset[:, None]
    ).astype(f32)
    fresh_hit = (
        lax.broadcasted_iota(jnp.int32, fresh_logits.shape, 1) == fresh_offset[:, None]
    ).astype(f32)
    weight_row = loss_scale * loss_mask.astype(f32)[:, None]
    frozen_grad = (weight_row * (frozen_prob - frozen_hit)).astype(bf16)
    fresh_grad = (weight_row * (fresh_prob - fresh_hit)).astype(bf16)
    mix_term = jnp.dot(fresh_grad, factor_rows, preferred_element_type=f32)
    mix_total = lax.psum(mix_term, "vocab").astype(bf16)
    grad_part = lax.psum_scatter(
        lax.dot_general(
            head_full, frozen_grad, (((0,), (1,)), ((), ())), preferred_element_type=f32
        ),
        "vocab",
        scatter_dimension=0,
        tiled=True,
    )
    basis_cols = lax.dynamic_slice_in_dim(factor_basis, vocab_index * width_here, width_here, 1)
    hidden_grad = (
        grad_part.T + jnp.dot(mix_total, basis_cols, preferred_element_type=f32)
    ).astype(bf16)
    rows_term = dot_first(fresh_grad, hidden_basis)
    basis_term = dot_first(mix_total, hidden)
    rows_grad, basis_grad = (
        lax.psum(rows_term.astype(bf16), "tok").astype(f32),
        lax.psum(basis_term.astype(bf16), "tok").astype(f32),
    )
    return hidden_grad, rows_grad, basis_grad


def solution(mesh):
    in_specs = (
        P("tok", "vocab"),
        P(("vocab", "tok"), None),
        P("vocab", None),
        P(),
        P("tok"),
        P("tok"),
    )
    out_specs = (P("tok", "vocab"), P("vocab", None), P(None, "vocab"))

    def on_device(hidden, head, factor_rows, *rest):
        even = [n & (n - 1) == 0 for n in (mesh.shape["vocab"], head.shape[0], factor_rows.shape[0])]
        few = 2 <= mesh.shape["vocab"] <= 16 and mesh.shape["tok"] == 4 and all(even)
        return (on_few if few else on_many)(hidden, head, factor_rows, *rest)

    return jax.shard_map(
        on_device, mesh=mesh, in_specs=in_specs, out_specs=out_specs, check_vma=False
    )
```

```python
import jax
import jax.numpy as jnp
from jax import lax
from jax.experimental import pallas as pl
from jax.experimental.pallas import tpu as pltpu
from jax.sharding import PartitionSpec as P

loss_scale = 64.0
f32 = jnp.float32
bf16 = jnp.bfloat16
contract_last = (((1,), (1,)), ((), ()))
contract_first = (((0,), (0,)), ((), ()))


def dot_last(a, b):
    return lax.dot_general(a, b, contract_last, preferred_element_type=f32)


def dot_first(a, b):
    return lax.dot_general(a, b, contract_first, preferred_element_type=f32)


def swap(value, axis, bit):
    size = lax.axis_size(axis)
    return lax.ppermute(value, axis, [(i, i ^ bit) for i in range(size)])


def swap_core(value):
    return swap(value, "tok", 1)


def swap_x(value):
    return swap(value, "tok", 2)


def swap_y(value):
    return swap(value, "vocab", 1)


def swap_z(value, step):
    return swap(value, "vocab", 2 * step)


in_vmem = pl.BlockSpec(memory_space=pltpu.VMEM)


def copy_blocks(shapes, moves, *arrays, source=pltpu.HBM):
    def kernel(*refs):
        ins, outs, sems = refs[: len(arrays)], refs[len(arrays) : -1], refs[-1]
        copies = []
        for n, (origin, columns, target, row, column) in enumerate(moves()):
            src, dst = ins[origin], outs[target]
            if columns is not None:
                src = src.at[:, pl.ds(pl.multiple_of(columns[0], 128), columns[1])]
            dst = dst.at[pl.ds(row, src.shape[0]), pl.ds(column, src.shape[1])]
            copies.append(pltpu.make_async_copy(src, dst, sems.at[n]))
        for copy in copies:
            copy.start()
        for copy in copies:
            copy.wait()

    size = sum(2 * shape[0] * shape[1] for shape in shapes)
    return pl.pallas_call(
        kernel,
        out_shape=[jax.ShapeDtypeStruct(shape, bf16) for shape in shapes],
        in_specs=[pl.BlockSpec(memory_space=source)] * len(arrays),
        out_specs=[in_vmem] * len(shapes),
        scratch_shapes=[pltpu.SemaphoreType.DMA((32,))],
        compiler_params=pltpu.CompilerParams(vmem_limit_bytes=12 << 20),
        cost_estimate=pl.CostEstimate(flops=0, bytes_accessed=2 * size, transcendentals=0),
    )(*arrays)


def logits_of(groups, tokens, rider=None):
    toks, width = tokens[0].shape
    heights = [group[0].shape[0] for group in groups]
    total, depth = sum(heights), width * len(tokens)
    flat = [a for group in groups for a in group]
    riders = [] if rider is None else [rider]
    extra = 0 if rider is None else rider.shape[0] // 2
    n_flat, n_all = len(flat), len(flat) + len(tokens) + len(riders)

    def kernel(*refs):
        out = refs[n_all]
        at, row = 0, 0
        for group, height in zip(groups, heights):
            result, column = None, 0
            for part in group:
                for c in range(0, part.shape[1], width):
                    token = refs[n_flat + (column + c) // width]
                    term = dot_last(refs[at][:, c : c + width], token[...])
                    result = term if result is None else result + term
                at, column = at + 1, column + part.shape[1]
            out[row : row + height, :] = result
            row += height
        if extra:
            wide = refs[n_all - 1][...].astype(f32)
            out[row:, :] = jnp.concatenate([wide[:extra], wide[extra:]], axis=1)

    return pl.pallas_call(
        kernel,
        out_shape=jax.ShapeDtypeStruct((total + extra, toks), f32),
        in_specs=[in_vmem] * n_all,
        out_specs=in_vmem,
        compiler_params=pltpu.CompilerParams(vmem_limit_bytes=12 << 20),
        cost_estimate=pl.CostEstimate(
            flops=2 * total * depth * toks,
            bytes_accessed=2 * (total + toks) * depth + 4 * total * toks,
            transcendentals=0,
        ),
    )(*flat, *tokens, *riders)


def on_few(hidden, head, factor_rows, factor_basis, targets, loss_mask):
    n_vocab, n_tok = lax.axis_size("vocab"), lax.axis_size("tok")
    n_z = n_vocab // 2
    bits = [1 << b for b in range(n_z.bit_length() - 1)]
    v = lax.axis_index("vocab")
    t = lax.axis_index("tok")
    toks, width = hidden.shape
    rows = head.shape[0]
    new_here = factor_rows.shape[0]
    rank = factor_basis.shape[0]
    depth = n_z * width

    near_first = v * (n_tok * rows) + (t >> 1) * (2 * rows)
    far_first = (v ^ 1) * (n_tok * rows) + (t >> 1) * (2 * rows)
    turn = (t & 1) * rows
    new_first = v * new_here
    hidden, head, near_first, far_first, turn, new_first = lax.optimization_barrier(
        (hidden, head, near_first, far_first, turn, new_first)
    )

    def start_of(j, other):
        return (lax.axis_index("vocab") ^ (2 * j + other)) * width

    cuts = [0, 1, n_z]
    chunks = [range(a, b) for a, b in zip(cuts, cuts[1:]) if a < b]
    sends = copy_blocks(
        [(rows, len(chunk) * width) for chunk in chunks],
        lambda: [
            (0, (start_of(j, 1), width), n, 0, (j - chunk[0]) * width)
            for n, chunk in enumerate(chunks)
            for j in chunk
        ],
        head,
    )
    beside = [swap_y(send) for send in sends]

    def half(array, after):
        array, _ = lax.optimization_barrier((array, after))
        moves = lambda: [(0, (start_of(j, 0), width), 0, 0, j * width) for j in range(n_z)]
        return copy_blocks([(array.shape[0], depth)], moves, array)[0]

    kept = half(head, beside[0])
    kept_core = swap_core(kept)

    later, _ = lax.optimization_barrier((hidden, sends[0]))
    shards, cross = {0: hidden}, {0: swap_x(later)}
    for bit in reversed(bits):
        near = swap_z(hidden if bit == bits[-1] else later, bit)
        for j in [j for j in shards if j]:
            shards[j], *_ = lax.optimization_barrier((shards[j], near, beside[0]))
            shards[j ^ bit] = swap_z(shards[j], bit)
        shards[bit] = near
    for j in range(1, n_z):
        sent = shards[j]
        if j == 1:
            sent, *_ = lax.optimization_barrier((sent, shards[n_z // 2]))
        if j > 1:
            sent, *_ = lax.optimization_barrier((sent, cross[j - 2]))
        cross[j] = swap_x(sent)
    basis_half = half(factor_basis, shards[n_z // 2])

    beside_core = []
    for n, came in enumerate(beside):
        came, *_ = lax.optimization_barrier((came, cross[1], cross[n_z - 2], shards[n_z - 1]))
        beside_core.append(swap_core(came))

    in_order = lambda parts: [parts[j] for j in range(n_z)]
    basis_ready, *_ = lax.optimization_barrier((basis_half, cross[n_z - 2], shards[n_z - 1]))
    upper = [[kept], [kept_core], [basis_ready]]
    upper_own = logits_of(upper, in_order(shards))
    beside_core[-1], *_ = lax.optimization_barrier((beside_core[-1], upper_own))
    lower_own = logits_of([beside, beside_core], in_order(shards))
    cross[0], _ = lax.optimization_barrier((cross[0], lower_own))
    rows_all, _ = lax.optimization_barrier((factor_rows, shards[n_z - 1]))
    for bit in bits:
        rows_all = jnp.concatenate([rows_all, swap_z(rows_all, bit)], axis=0)
    both_cross = logits_of(upper + [beside, beside_core], in_order(cross), rows_all)
    n_up = 2 * rows + rank

    def add_over_y(up, low, up_came, low_came):
        near = up[: 2 * rows] + low_came
        far = low + up_came[: 2 * rows]
        return near, far, (up[2 * rows :] + up_came[2 * rows :]).astype(bf16)

    upper_came, lower_came = swap_y(upper_own), swap_y(lower_own)
    cross_came = swap_y(both_cross)
    upper_came, _ = lax.optimization_barrier((upper_came, both_cross))
    near_own, far_own, basis_own = add_over_y(upper_own, lower_own, upper_came, lower_came)
    near_cross, far_cross, basis_cross = add_over_y(
        both_cross[:n_up], both_cross[n_up : n_up + 2 * rows], cross_came[:n_up], cross_came[n_up : n_up + 2 * rows]
    )
    hidden_basis = jnp.concatenate([basis_own, basis_cross], axis=1)

    n_rows = n_up + 2 * rows
    rows_came = cross_came[n_rows:].astype(bf16)
    rows_all = jnp.concatenate([rows_all, rows_came[:, :rank], rows_came[:, rank:]], axis=0)

    def merge(a, b):
        top = jnp.maximum(a[0], b[0])
        return jnp.stack([top, a[1] * jnp.exp(a[0] - top) + b[1] * jnp.exp(b[0] - top)])

    def local(*logits):
        top = jnp.max(logits[0], axis=0)
        for l in logits[1:]:
            top = jnp.maximum(top, jnp.max(l, axis=0))
        total = jnp.sum(jnp.exp(logits[0] - top[None, :]), axis=0)
        for l in logits[1:]:
            total = total + jnp.sum(jnp.exp(l - top[None, :]), axis=0)
        return jnp.stack([top, total])

    info = jnp.stack([targets.astype(f32), loss_mask.astype(f32)])
    stats = jnp.concatenate([local(near_own, far_own), local(near_cross, far_cross)], axis=1)
    sent = jnp.concatenate([stats, jnp.concatenate([info, info], axis=1)], axis=0)
    came = swap_x(sent)
    stats = merge(stats, jnp.concatenate([came[:2, toks:], came[:2, :toks]], axis=1))
    info = jnp.concatenate([info, came[2:, :toks]], axis=1)
    target_row = info[0].astype(jnp.int32)
    weight_row = loss_scale * info[1]
    for bit in bits:
        stats = merge(stats, swap_z(stats, bit))
    fresh = lax.dot_general(
        rows_all, hidden_basis, (((1,), (0,)), ((), ())), preferred_element_type=f32
    )
    stats = merge(stats, local(fresh))
    row_top, sum_exp = stats[0], stats[1]
    scale_row = weight_row / sum_exp

    def grad_of(frozen, first, cols):
        row_ids = (lax.broadcasted_iota(jnp.int32, frozen.shape, 0) ^ turn) + first
        hit = jnp.where(row_ids == target_row[None, cols], weight_row[None, cols], 0.0)
        return (jnp.exp(frozen - row_top[None, cols]) * scale_row[None, cols] - hit).astype(bf16)

    at_own, at_cross = slice(0, toks), slice(toks, 2 * toks)
    grad_cross = (grad_of(near_cross, near_first, at_cross), grad_of(far_cross, far_first, at_cross))
    grad_own = (grad_of(near_own, near_first, at_own), grad_of(far_own, far_first, at_own))

    laid = [kept, kept_core] + beside + beside_core
    laid[0], _ = lax.optimization_barrier((kept, both_cross))
    places, row = [], 0
    for group in ([kept], [kept_core], beside, beside_core):
        column = 0
        for array in group:
            places.append((len(places), None, 0, row, column))
            column += array.shape[1]
        row += rows
    (weights,) = copy_blocks([(4 * rows, depth)], lambda: places, *laid, source=pltpu.VMEM)

    def part(grads, j):
        return dot_first(grads, weights[:, j * width : (j + 1) * width])

    grad_cross = jnp.concatenate(grad_cross, axis=0)
    grad_own = jnp.concatenate(grad_own, axis=0)
    sums, from_x, first_z = {}, {}, None
    for j in reversed(range(n_z)):
        send = part(grad_cross, j).astype(bf16)
        if j + 2 in from_x:
            send, _, _ = lax.optimization_barrier((send, from_x[j + 2], first_z))
        first_send = send if j == n_z - 1 else first_send
        from_x[j] = swap_x(send)
        sums[j] = part(grad_own, j) + from_x[j].astype(f32)
        if first_z is None:
            first_z = sums[j].astype(bf16)
    fresh, _ = lax.optimization_barrier((fresh, from_x[max(0, n_z - 2)]))
    fresh_iota = lax.broadcasted_iota(jnp.int32, (n_vocab * new_here, toks), 0)
    in_block = fresh_iota & (new_here - 1)
    from_block = fresh_iota - in_block
    from_block = ((from_block & (n_z * new_here - 1)) << 1) + (from_block & (n_z * new_here)) // n_z
    fresh_ids = ((from_block + in_block) ^ new_first) + rows * n_tok * n_vocab
    fresh_hit = jnp.where(fresh_ids == targets[None, :], weight_row[None, :toks], 0.0)
    fresh_grad = (
        jnp.exp(fresh[:, :toks] - row_top[None, :toks]) * scale_row[None, :toks] - fresh_hit
    ).astype(bf16)
    mix_total = dot_first(rows_all, fresh_grad).astype(bf16)
    rows_part = dot_last(fresh_grad[:new_here], hidden_basis[:, :toks])
    basis_part = jnp.dot(mix_total, hidden, preferred_element_type=f32)

    came_z = None
    for bit in bits:
        for j in [j for j in sorted(sums, reverse=True) if j & bit]:
            total = sums.pop(j)
            send = first_z if j == n_z - 1 else total.astype(bf16)
            if bit == bits[0] and came_z is not None:
                send, _ = lax.optimization_barrier((send, came_z))
            came = swap_z(send, bit)
            came_z = came if came_z is None else came_z
            sums[j ^ bit] = sums[j ^ bit] + came.astype(f32)
    hidden_grad = (sums[0] + dot_first(mix_total, basis_half[:, :width])).astype(bf16)

    factor_part = jnp.concatenate([basis_part, rows_part], axis=1)
    factor_two = lax.reduce_precision(factor_part + swap_core(factor_part), 8, 7)
    factor_two, _ = lax.optimization_barrier((factor_two, from_x[min(1, n_z - 1)]))
    factor_grad = factor_two + swap_x(factor_two.astype(bf16)).astype(f32)
    basis_grad, rows_grad = factor_grad[:, :width], factor_grad[:, width:]
    return hidden_grad, rows_grad, basis_grad


def on_many(hidden, head, factor_rows, factor_basis, targets, loss_mask):
    n_vocab = lax.axis_size("vocab")
    n_tok = lax.axis_size("tok")
    vocab_index = lax.axis_index("vocab")
    rows_here = head.shape[0] * n_tok
    new_here = factor_rows.shape[0]
    width_here = hidden.shape[1]
    gathered = lax.all_gather(hidden, "vocab", axis=1, tiled=True)
    head_full = lax.all_gather(head, "tok", axis=0, tiled=True)
    frozen = dot_last(gathered, head_full)
    hidden_basis = dot_last(gathered, factor_basis).astype(bf16)
    fresh_logits = dot_last(hidden_basis, factor_rows)
    local_max = jnp.maximum(jnp.max(frozen, axis=1), jnp.max(fresh_logits, axis=1))
    row_top = lax.pmax(local_max, "vocab")
    local_sum = jnp.sum(jnp.exp(frozen - row_top[:, None]), axis=1) + jnp.sum(
        jnp.exp(fresh_logits - row_top[:, None]), axis=1
    )
    sum_exp = lax.psum(local_sum, "vocab")
    frozen_prob = jnp.exp(frozen - row_top[:, None]) / sum_exp[:, None]
    fresh_prob = jnp.exp(fresh_logits - row_top[:, None]) / sum_exp[:, None]
    frozen_offset = targets - vocab_index * rows_here
    fresh_offset = targets - rows_here * n_vocab - vocab_index * new_here
    frozen_hit = (
        lax.broadcasted_iota(jnp.int32, frozen.shape, 1) == frozen_offset[:, None]
    ).astype(f32)
    fresh_hit = (
        lax.broadcasted_iota(jnp.int32, fresh_logits.shape, 1) == fresh_offset[:, None]
    ).astype(f32)
    weight_row = loss_scale * loss_mask.astype(f32)[:, None]
    frozen_grad = (weight_row * (frozen_prob - frozen_hit)).astype(bf16)
    fresh_grad = (weight_row * (fresh_prob - fresh_hit)).astype(bf16)
    mix_term = jnp.dot(fresh_grad, factor_rows, preferred_element_type=f32)
    mix_total = lax.psum(mix_term, "vocab").astype(bf16)
    grad_part = lax.psum_scatter(
        lax.dot_general(
            head_full, frozen_grad, (((0,), (1,)), ((), ())), preferred_element_type=f32
        ),
        "vocab",
        scatter_dimension=0,
        tiled=True,
    )
    basis_cols = lax.dynamic_slice_in_dim(factor_basis, vocab_index * width_here, width_here, 1)
    hidden_grad = (
        grad_part.T + jnp.dot(mix_total, basis_cols, preferred_element_type=f32)
    ).astype(bf16)
    rows_term = dot_first(fresh_grad, hidden_basis)
    basis_term = dot_first(mix_total, hidden)
    rows_grad, basis_grad = (
        lax.psum(rows_term.astype(bf16), "tok").astype(f32),
        lax.psum(basis_term.astype(bf16), "tok").astype(f32),
    )
    return hidden_grad, rows_grad, basis_grad


def solution(mesh):
    in_specs = (
        P("tok", "vocab"),
        P(("vocab", "tok"), None),
        P("vocab", None),
        P(),
        P("tok"),
        P("tok"),
    )
    out_specs = (P("tok", "vocab"), P("vocab", None), P(None, "vocab"))

    def on_device(hidden, head, factor_rows, *rest):
        even = [n & (n - 1) == 0 for n in (mesh.shape["vocab"], head.shape[0], factor_rows.shape[0])]
        few = 2 <= mesh.shape["vocab"] <= 16 and mesh.shape["tok"] == 4 and all(even)
        few = few and hidden.shape[0] == 2 * factor_rows.shape[1]
        return (on_few if few else on_many)(hidden, head, factor_rows, *rest)

    return jax.shard_map(
        on_device, mesh=mesh, in_specs=in_specs, out_specs=out_specs, check_vma=False
    )
```

```python
import jax
import jax.numpy as jnp
from jax import lax
from jax.experimental import pallas as pl
from jax.experimental.pallas import tpu as pltpu
from jax.sharding import PartitionSpec as P

loss_scale = 64.0
f32 = jnp.float32
bf16 = jnp.bfloat16
contract_last = (((1,), (1,)), ((), ()))
contract_first = (((0,), (0,)), ((), ()))


def dot_last(a, b):
    return lax.dot_general(a, b, contract_last, preferred_element_type=f32)


def dot_first(a, b):
    return lax.dot_general(a, b, contract_first, preferred_element_type=f32)


def swap(value, axis, bit):
    size = lax.axis_size(axis)
    return lax.ppermute(value, axis, [(i, i ^ bit) for i in range(size)])


def swap_core(value):
    return swap(value, "tok", 1)


def swap_x(value):
    return swap(value, "tok", 2)


def swap_y(value):
    return swap(value, "vocab", 1)


def swap_z(value, step):
    return swap(value, "vocab", 2 * step)


in_vmem = pl.BlockSpec(memory_space=pltpu.VMEM)


def copy_blocks(shapes, moves, *arrays, source=pltpu.HBM):
    def kernel(*refs):
        ins, outs, sems = refs[: len(arrays)], refs[len(arrays) : -1], refs[-1]
        copies = []
        for n, (origin, columns, target, row, column) in enumerate(moves()):
            src, dst = ins[origin], outs[target]
            if columns is not None:
                src = src.at[:, pl.ds(pl.multiple_of(columns[0], 128), columns[1])]
            dst = dst.at[pl.ds(row, src.shape[0]), pl.ds(column, src.shape[1])]
            copies.append(pltpu.make_async_copy(src, dst, sems.at[n]))
        for copy in copies:
            copy.start()
        for copy in copies:
            copy.wait()

    size = sum(2 * shape[0] * shape[1] for shape in shapes)
    return pl.pallas_call(
        kernel,
        out_shape=[jax.ShapeDtypeStruct(shape, bf16) for shape in shapes],
        in_specs=[pl.BlockSpec(memory_space=source)] * len(arrays),
        out_specs=[in_vmem] * len(shapes),
        scratch_shapes=[pltpu.SemaphoreType.DMA((32,))],
        compiler_params=pltpu.CompilerParams(vmem_limit_bytes=12 << 20),
        cost_estimate=pl.CostEstimate(flops=0, bytes_accessed=2 * size, transcendentals=0),
    )(*arrays)


def logits_of(groups, tokens, rider=None):
    toks, width = tokens[0].shape
    heights = [group[0].shape[0] for group in groups]
    total, depth = sum(heights), width * len(tokens)
    flat = [a for group in groups for a in group]
    riders = [] if rider is None else [rider]
    extra = 0 if rider is None else rider.shape[0] // 2
    n_flat, n_all = len(flat), len(flat) + len(tokens) + len(riders)

    def kernel(*refs):
        out = refs[n_all]
        at, row = 0, 0
        for group, height in zip(groups, heights):
            result, column = None, 0
            for part in group:
                for c in range(0, part.shape[1], width):
                    token = refs[n_flat + (column + c) // width]
                    term = dot_last(refs[at][:, c : c + width], token[...])
                    result = term if result is None else result + term
                at, column = at + 1, column + part.shape[1]
            out[row : row + height, :] = result
            row += height
        if extra:
            wide = refs[n_all - 1][...].astype(f32)
            out[row:, :] = jnp.concatenate([wide[:extra], wide[extra:]], axis=1)

    return pl.pallas_call(
        kernel,
        out_shape=jax.ShapeDtypeStruct((total + extra, toks), f32),
        in_specs=[in_vmem] * n_all,
        out_specs=in_vmem,
        compiler_params=pltpu.CompilerParams(vmem_limit_bytes=12 << 20),
        cost_estimate=pl.CostEstimate(
            flops=2 * total * depth * toks,
            bytes_accessed=2 * (total + toks) * depth + 4 * total * toks,
            transcendentals=0,
        ),
    )(*flat, *tokens, *riders)


def on_few(hidden, head, factor_rows, factor_basis, targets, loss_mask):
    n_vocab, n_tok = lax.axis_size("vocab"), lax.axis_size("tok")
    n_z = n_vocab // 2
    bits = [1 << b for b in range(n_z.bit_length() - 1)]
    v = lax.axis_index("vocab")
    t = lax.axis_index("tok")
    toks, width = hidden.shape
    rows = head.shape[0]
    new_here = factor_rows.shape[0]
    rank = factor_basis.shape[0]
    depth = n_z * width

    near_first = v * (n_tok * rows) + (t >> 1) * (2 * rows)
    far_first = (v ^ 1) * (n_tok * rows) + (t >> 1) * (2 * rows)
    turn = (t & 1) * rows
    new_first = v * new_here
    hidden, head, near_first, far_first, turn, new_first = lax.optimization_barrier(
        (hidden, head, near_first, far_first, turn, new_first)
    )

    def start_of(j, other):
        return (lax.axis_index("vocab") ^ (2 * j + other)) * width

    cuts = [0, n_z]
    chunks = [range(a, b) for a, b in zip(cuts, cuts[1:]) if a < b]
    sends = copy_blocks(
        [(rows, len(chunk) * width) for chunk in chunks],
        lambda: [
            (0, (start_of(j, 1), width), n, 0, (j - chunk[0]) * width)
            for n, chunk in enumerate(chunks)
            for j in chunk
        ],
        head,
    )
    beside = [swap_y(send) for send in sends]

    def half(array, after):
        array, _ = lax.optimization_barrier((array, after))
        moves = lambda: [(0, (start_of(j, 0), width), 0, 0, j * width) for j in range(n_z)]
        return copy_blocks([(array.shape[0], depth)], moves, array)[0]

    after, _ = lax.optimization_barrier((hidden, sends[0]))
    shards, cross = {0: hidden}, {0: swap_x(hidden)}
    for bit in reversed(bits):
        near = swap_z(hidden if bit == 1 else hidden, bit)
        for j in [j for j in shards if j]:
            shards[j], *_ = lax.optimization_barrier((shards[j], near))
            shards[j ^ bit] = swap_z(shards[j], bit)
        shards[bit] = near
    for j in range(1, n_z):
        sent = shards[j]
        waits = [] if j == 1 else [cross[j - 2]] if j < n_z - 1 else [cross[j - 2], beside[0]]
        if waits:
            sent, *_ = lax.optimization_barrier((sent, *waits))
        cross[j] = swap_x(sent)
    kept = half(head, cross[1])
    kept_core = swap_core(kept)
    basis_half = half(factor_basis, cross[0])

    beside_core = []
    for n, came in enumerate(beside):
        came, *_ = lax.optimization_barrier((came, cross[n_z - 2], shards[n_z - 1]))
        beside_core.append(swap_core(came))

    in_order = lambda parts: [parts[j] for j in range(n_z)]
    basis_ready, *_ = lax.optimization_barrier((basis_half, cross[1]))
    upper = [[kept], [kept_core], [basis_ready]]
    upper_own = logits_of(upper, in_order(shards))
    beside_core[-1], *_ = lax.optimization_barrier((beside_core[-1], upper_own))
    lower_own = logits_of([beside, beside_core], in_order(shards))
    cross[0], _ = lax.optimization_barrier((cross[0], lower_own))
    both_cross = logits_of(upper + [beside, beside_core], in_order(cross), factor_rows)
    n_up = 2 * rows + rank

    def add_over_y(up, low, up_came, low_came):
        near = up[: 2 * rows] + low_came
        far = low + up_came[: 2 * rows]
        return near, far, (up[2 * rows :] + up_came[2 * rows :]).astype(bf16)

    upper_came, lower_came = swap_y(upper_own), swap_y(lower_own)
    cross_came = swap_y(both_cross)
    upper_came, _ = lax.optimization_barrier((upper_came, both_cross))
    near_own, far_own, basis_own = add_over_y(upper_own, lower_own, upper_came, lower_came)
    near_cross, far_cross, basis_cross = add_over_y(
        both_cross[:n_up], both_cross[n_up : n_up + 2 * rows], cross_came[:n_up], cross_came[n_up : n_up + 2 * rows]
    )
    hidden_basis = jnp.concatenate([basis_own, basis_cross], axis=1)

    n_rows = n_up + 2 * rows
    rows_came = cross_came[n_rows:].astype(bf16)
    rows_pair = jnp.concatenate([factor_rows, rows_came[:, :rank], rows_came[:, rank:]], axis=0)

    def merge(a, b):
        top = jnp.maximum(a[0], b[0])
        return jnp.stack([top, a[1] * jnp.exp(a[0] - top) + b[1] * jnp.exp(b[0] - top)])

    def local(*logits):
        top = jnp.max(logits[0], axis=0)
        for l in logits[1:]:
            top = jnp.maximum(top, jnp.max(l, axis=0))
        total = jnp.sum(jnp.exp(logits[0] - top[None, :]), axis=0)
        for l in logits[1:]:
            total = total + jnp.sum(jnp.exp(l - top[None, :]), axis=0)
        return jnp.stack([top, total])

    info = jnp.stack([targets.astype(f32), loss_mask.astype(f32)])
    stats = jnp.concatenate([local(near_own, far_own), local(near_cross, far_cross)], axis=1)
    sent = jnp.concatenate([stats, jnp.concatenate([info, info], axis=1)], axis=0)
    came = swap_x(sent)
    stats = merge(stats, jnp.concatenate([came[:2, toks:], came[:2, :toks]], axis=1))
    info = jnp.concatenate([info, came[2:, :toks]], axis=1)
    target_row = info[0].astype(jnp.int32)
    weight_row = loss_scale * info[1]
    fresh = lax.dot_general(
        rows_pair, hidden_basis, (((1,), (0,)), ((), ())), preferred_element_type=f32
    )
    stats = merge(stats, local(fresh))
    for bit in bits:
        stats = merge(stats, swap_z(stats, bit))
    row_top, sum_exp = stats[0], stats[1]
    scale_row = weight_row / sum_exp

    def grad_of(frozen, first, cols):
        row_ids = (lax.broadcasted_iota(jnp.int32, frozen.shape, 0) ^ turn) + first
        hit = jnp.where(row_ids == target_row[None, cols], weight_row[None, cols], 0.0)
        return (jnp.exp(frozen - row_top[None, cols]) * scale_row[None, cols] - hit).astype(bf16)

    at_own, at_cross = slice(0, toks), slice(toks, 2 * toks)
    grad_cross = (grad_of(near_cross, near_first, at_cross), grad_of(far_cross, far_first, at_cross))
    grad_own = (grad_of(near_own, near_first, at_own), grad_of(far_own, far_first, at_own))

    laid = [kept, kept_core] + beside + beside_core
    laid[0], _ = lax.optimization_barrier((kept, both_cross))
    places, row = [], 0
    for group in ([kept], [kept_core], beside, beside_core):
        column = 0
        for array in group:
            places.append((len(places), None, 0, row, column))
            column += array.shape[1]
        row += rows
    (weights,) = copy_blocks([(4 * rows, depth)], lambda: places, *laid, source=pltpu.VMEM)

    def part(grads, j):
        return dot_first(grads, weights[:, j * width : (j + 1) * width])

    grad_cross = jnp.concatenate(grad_cross, axis=0)
    grad_own = jnp.concatenate(grad_own, axis=0)
    sums, from_x, first_z = {}, {}, None
    for j in reversed(range(n_z)):
        send = part(grad_cross, j).astype(bf16)
        if j + 2 in from_x:
            send, _, _ = lax.optimization_barrier((send, from_x[j + 2], first_z))
        first_send = send if j == n_z - 1 else first_send
        from_x[j] = swap_x(send)
        sums[j] = part(grad_own, j) + from_x[j].astype(f32)
        if first_z is None:
            first_z = sums[j].astype(bf16)
    fresh, _ = lax.optimization_barrier((fresh, first_send))
    fresh_ids = lax.broadcasted_iota(jnp.int32, (2 * new_here, toks), 0) ^ new_first
    fresh_ids = fresh_ids + rows * n_tok * n_vocab
    fresh_hit = jnp.where(fresh_ids == targets[None, :], weight_row[None, :toks], 0.0)
    fresh_grad = (
        jnp.exp(fresh[:, :toks] - row_top[None, :toks]) * scale_row[None, :toks] - fresh_hit
    ).astype(bf16)
    mix_total = dot_first(rows_pair, fresh_grad)
    for bit in bits:
        mix_total = mix_total + swap_z(mix_total, bit)
    mix_total = mix_total.astype(bf16)
    rows_part = dot_last(fresh_grad[:new_here], hidden_basis[:, :toks])
    basis_part = jnp.dot(mix_total, hidden, preferred_element_type=f32)

    came_z = None
    for bit in bits:
        for j in [j for j in sorted(sums, reverse=True) if j & bit]:
            total = sums.pop(j)
            send = first_z if j == n_z - 1 else total.astype(bf16)
            if bit == bits[0] and came_z is not None:
                send, _ = lax.optimization_barrier((send, came_z))
            came = swap_z(send, bit)
            came_z = came if came_z is None else came_z
            sums[j ^ bit] = sums[j ^ bit] + came.astype(f32)
    hidden_grad = (sums[0] + dot_first(mix_total, basis_half[:, :width])).astype(bf16)

    factor_part = jnp.concatenate([basis_part, rows_part], axis=1)
    factor_two = lax.reduce_precision(factor_part + swap_core(factor_part), 8, 7)
    factor_two, _ = lax.optimization_barrier((factor_two, from_x[min(1, n_z - 1)]))
    factor_grad = factor_two + swap_x(factor_two.astype(bf16)).astype(f32)
    basis_grad, rows_grad = factor_grad[:, :width], factor_grad[:, width:]
    return hidden_grad, rows_grad, basis_grad


def on_many(hidden, head, factor_rows, factor_basis, targets, loss_mask):
    n_vocab = lax.axis_size("vocab")
    n_tok = lax.axis_size("tok")
    vocab_index = lax.axis_index("vocab")
    rows_here = head.shape[0] * n_tok
    new_here = factor_rows.shape[0]
    width_here = hidden.shape[1]
    gathered = lax.all_gather(hidden, "vocab", axis=1, tiled=True)
    head_full = lax.all_gather(head, "tok", axis=0, tiled=True)
    frozen = dot_last(gathered, head_full)
    hidden_basis = dot_last(gathered, factor_basis).astype(bf16)
    fresh_logits = dot_last(hidden_basis, factor_rows)
    local_max = jnp.maximum(jnp.max(frozen, axis=1), jnp.max(fresh_logits, axis=1))
    row_top = lax.pmax(local_max, "vocab")
    local_sum = jnp.sum(jnp.exp(frozen - row_top[:, None]), axis=1) + jnp.sum(
        jnp.exp(fresh_logits - row_top[:, None]), axis=1
    )
    sum_exp = lax.psum(local_sum, "vocab")
    frozen_prob = jnp.exp(frozen - row_top[:, None]) / sum_exp[:, None]
    fresh_prob = jnp.exp(fresh_logits - row_top[:, None]) / sum_exp[:, None]
    frozen_offset = targets - vocab_index * rows_here
    fresh_offset = targets - rows_here * n_vocab - vocab_index * new_here
    frozen_hit = (
        lax.broadcasted_iota(jnp.int32, frozen.shape, 1) == frozen_offset[:, None]
    ).astype(f32)
    fresh_hit = (
        lax.broadcasted_iota(jnp.int32, fresh_logits.shape, 1) == fresh_offset[:, None]
    ).astype(f32)
    weight_row = loss_scale * loss_mask.astype(f32)[:, None]
    frozen_grad = (weight_row * (frozen_prob - frozen_hit)).astype(bf16)
    fresh_grad = (weight_row * (fresh_prob - fresh_hit)).astype(bf16)
    mix_term = jnp.dot(fresh_grad, factor_rows, preferred_element_type=f32)
    mix_total = lax.psum(mix_term, "vocab").astype(bf16)
    grad_part = lax.psum_scatter(
        lax.dot_general(
            head_full, frozen_grad, (((0,), (1,)), ((), ())), preferred_element_type=f32
        ),
        "vocab",
        scatter_dimension=0,
        tiled=True,
    )
    basis_cols = lax.dynamic_slice_in_dim(factor_basis, vocab_index * width_here, width_here, 1)
    hidden_grad = (
        grad_part.T + jnp.dot(mix_total, basis_cols, preferred_element_type=f32)
    ).astype(bf16)
    rows_term = dot_first(fresh_grad, hidden_basis)
    basis_term = dot_first(mix_total, hidden)
    rows_grad, basis_grad = (
        lax.psum(rows_term.astype(bf16), "tok").astype(f32),
        lax.psum(basis_term.astype(bf16), "tok").astype(f32),
    )
    return hidden_grad, rows_grad, basis_grad


def solution(mesh):
    in_specs = (
        P("tok", "vocab"),
        P(("vocab", "tok"), None),
        P("vocab", None),
        P(),
        P("tok"),
        P("tok"),
    )
    out_specs = (P("tok", "vocab"), P("vocab", None), P(None, "vocab"))

    def on_device(hidden, head, factor_rows, *rest):
        even = [n & (n - 1) == 0 for n in (mesh.shape["vocab"], head.shape[0], factor_rows.shape[0])]
        few = 2 <= mesh.shape["vocab"] <= 16 and mesh.shape["tok"] == 4 and all(even)
        few = few and hidden.shape[0] == 2 * factor_rows.shape[1]
        return (on_few if few else on_many)(hidden, head, factor_rows, *rest)

    return jax.shard_map(
        on_device, mesh=mesh, in_specs=in_specs, out_specs=out_specs, check_vma=False
    )
```

```python
import jax
import jax.numpy as jnp
from jax import lax
from jax.experimental import pallas as pl
from jax.experimental.pallas import tpu as pltpu
from jax.sharding import PartitionSpec as P

loss_scale = 64.0
f32 = jnp.float32
bf16 = jnp.bfloat16
contract_last = (((1,), (1,)), ((), ()))
contract_first = (((0,), (0,)), ((), ()))


def dot_last(a, b):
    return lax.dot_general(a, b, contract_last, preferred_element_type=f32)


def dot_first(a, b):
    return lax.dot_general(a, b, contract_first, preferred_element_type=f32)


def swap(value, axis, bit):
    size = lax.axis_size(axis)
    return lax.ppermute(value, axis, [(i, i ^ bit) for i in range(size)])


def swap_core(value):
    return swap(value, "tok", 1)


def swap_x(value):
    return swap(value, "tok", 2)


def swap_y(value):
    return swap(value, "vocab", 1)


def swap_z(value, step):
    return swap(value, "vocab", 2 * step)


in_vmem = pl.BlockSpec(memory_space=pltpu.VMEM)


def copy_blocks(shapes, moves, *arrays, source=pltpu.HBM):
    def kernel(*refs):
        ins, outs, sems = refs[: len(arrays)], refs[len(arrays) : -1], refs[-1]
        copies = []
        for n, (origin, columns, target, row, column) in enumerate(moves()):
            src, dst = ins[origin], outs[target]
            if columns is not None:
                src = src.at[:, pl.ds(pl.multiple_of(columns[0], 128), columns[1])]
            dst = dst.at[pl.ds(row, src.shape[0]), pl.ds(column, src.shape[1])]
            copies.append(pltpu.make_async_copy(src, dst, sems.at[n]))
        for copy in copies:
            copy.start()
        for copy in copies:
            copy.wait()

    size = sum(2 * shape[0] * shape[1] for shape in shapes)
    return pl.pallas_call(
        kernel,
        out_shape=[jax.ShapeDtypeStruct(shape, bf16) for shape in shapes],
        in_specs=[pl.BlockSpec(memory_space=source)] * len(arrays),
        out_specs=[in_vmem] * len(shapes),
        scratch_shapes=[pltpu.SemaphoreType.DMA((32,))],
        compiler_params=pltpu.CompilerParams(vmem_limit_bytes=12 << 20),
        cost_estimate=pl.CostEstimate(flops=0, bytes_accessed=2 * size, transcendentals=0),
    )(*arrays)


def logits_of(groups, tokens, rider=None):
    toks, width = tokens[0].shape
    heights = [group[0].shape[0] for group in groups]
    total, depth = sum(heights), width * len(tokens)
    flat = [a for group in groups for a in group]
    riders = [] if rider is None else [rider]
    extra = 0 if rider is None else rider.shape[0] // 2
    n_flat, n_all = len(flat), len(flat) + len(tokens) + len(riders)

    def kernel(*refs):
        out = refs[n_all]
        at, row = 0, 0
        for group, height in zip(groups, heights):
            result, column = None, 0
            for part in group:
                for c in range(0, part.shape[1], width):
                    token = refs[n_flat + (column + c) // width]
                    term = dot_last(refs[at][:, c : c + width], token[...])
                    result = term if result is None else result + term
                at, column = at + 1, column + part.shape[1]
            out[row : row + height, :] = result
            row += height
        if extra:
            wide = refs[n_all - 1][...].astype(f32)
            out[row:, :] = jnp.concatenate([wide[:extra], wide[extra:]], axis=1)

    return pl.pallas_call(
        kernel,
        out_shape=jax.ShapeDtypeStruct((total + extra, toks), f32),
        in_specs=[in_vmem] * n_all,
        out_specs=in_vmem,
        compiler_params=pltpu.CompilerParams(vmem_limit_bytes=12 << 20),
        cost_estimate=pl.CostEstimate(
            flops=2 * total * depth * toks,
            bytes_accessed=2 * (total + toks) * depth + 4 * total * toks,
            transcendentals=0,
        ),
    )(*flat, *tokens, *riders)


def finish(total, came):
    def kernel(total_ref, came_ref, out):
        out[...] = (total_ref[...] + came_ref[...].astype(f32)).astype(bf16)

    return pl.pallas_call(
        kernel,
        out_shape=jax.ShapeDtypeStruct(total.shape, bf16),
        in_specs=[in_vmem] * 2,
        out_specs=in_vmem,
        compiler_params=pltpu.CompilerParams(vmem_limit_bytes=4 << 20),
        cost_estimate=pl.CostEstimate(
            flops=8 * total.size, bytes_accessed=8 * total.size, transcendentals=0
        ),
    )(total, came)


def on_few(hidden, head, factor_rows, factor_basis, targets, loss_mask):
    n_vocab, n_tok = lax.axis_size("vocab"), lax.axis_size("tok")
    n_z = n_vocab // 2
    bits = [1 << b for b in range(n_z.bit_length() - 1)]
    v = lax.axis_index("vocab")
    t = lax.axis_index("tok")
    toks, width = hidden.shape
    rows = head.shape[0]
    new_here = factor_rows.shape[0]
    rank = factor_basis.shape[0]
    depth = n_z * width

    near_first = v * (n_tok * rows) + (t >> 1) * (2 * rows)
    far_first = (v ^ 1) * (n_tok * rows) + (t >> 1) * (2 * rows)
    turn = (t & 1) * rows
    new_first = v * new_here
    hidden, head, near_first, far_first, turn, new_first = lax.optimization_barrier(
        (hidden, head, near_first, far_first, turn, new_first)
    )

    def start_of(j, other):
        return (lax.axis_index("vocab") ^ (2 * j + other)) * width

    cuts = [0, n_z]
    chunks = [range(a, b) for a, b in zip(cuts, cuts[1:]) if a < b]
    sends = copy_blocks(
        [(rows, len(chunk) * width) for chunk in chunks],
        lambda: [
            (0, (start_of(j, 1), width), n, 0, (j - chunk[0]) * width)
            for n, chunk in enumerate(chunks)
            for j in chunk
        ],
        head,
    )
    beside = [swap_y(send) for send in sends]

    def half(array, after):
        array, _ = lax.optimization_barrier((array, after))
        moves = lambda: [(0, (start_of(j, 0), width), 0, 0, j * width) for j in range(n_z)]
        return copy_blocks([(array.shape[0], depth)], moves, array)[0]

    after, _ = lax.optimization_barrier((hidden, sends[0]))
    shards, cross = {0: hidden}, {0: swap_x(hidden)}
    for bit in reversed(bits):
        near = swap_z(hidden if bit == 1 else hidden, bit)
        for j in [j for j in shards if j]:
            shards[j], *_ = lax.optimization_barrier((shards[j], near))
            shards[j ^ bit] = swap_z(shards[j], bit)
        shards[bit] = near
    for j in range(1, n_z):
        sent = shards[j]
        waits = [] if j == 1 else [cross[j - 2]] if j < n_z - 1 else [cross[j - 2], beside[0]]
        if waits:
            sent, *_ = lax.optimization_barrier((sent, *waits))
        cross[j] = swap_x(sent)
    kept = half(head, cross[1])
    kept_core = swap_core(kept)
    basis_half = half(factor_basis, cross[0])

    beside_core = []
    for n, came in enumerate(beside):
        came, *_ = lax.optimization_barrier((came, cross[n_z - 2], shards[n_z - 1]))
        beside_core.append(swap_core(came))

    in_order = lambda parts: [parts[j] for j in range(n_z)]
    basis_ready, *_ = lax.optimization_barrier((basis_half, cross[1]))
    upper = [[kept], [kept_core], [basis_ready]]
    upper_own = logits_of(upper, in_order(shards))
    beside_core[-1], *_ = lax.optimization_barrier((beside_core[-1], upper_own))
    lower_own = logits_of([beside, beside_core], in_order(shards))
    cross[0], _ = lax.optimization_barrier((cross[0], lower_own))
    both_cross = logits_of(upper + [beside, beside_core], in_order(cross), factor_rows)
    n_up = 2 * rows + rank

    def add_over_y(up, low, up_came, low_came):
        near = up[: 2 * rows] + low_came
        far = low + up_came[: 2 * rows]
        return near, far, (up[2 * rows :] + up_came[2 * rows :]).astype(bf16)

    upper_came, lower_came = swap_y(upper_own), swap_y(lower_own)
    cross_came = swap_y(both_cross)
    upper_came, _ = lax.optimization_barrier((upper_came, both_cross))
    near_own, far_own, basis_own = add_over_y(upper_own, lower_own, upper_came, lower_came)
    near_cross, far_cross, basis_cross = add_over_y(
        both_cross[:n_up], both_cross[n_up : n_up + 2 * rows], cross_came[:n_up], cross_came[n_up : n_up + 2 * rows]
    )
    hidden_basis = jnp.concatenate([basis_own, basis_cross], axis=1)

    n_rows = n_up + 2 * rows
    rows_came = cross_came[n_rows:].astype(bf16)
    rows_pair = jnp.concatenate([factor_rows, rows_came[:, :rank], rows_came[:, rank:]], axis=0)

    def merge(a, b):
        top = jnp.maximum(a[0], b[0])
        return jnp.stack([top, a[1] * jnp.exp(a[0] - top) + b[1] * jnp.exp(b[0] - top)])

    def local(*logits):
        top = jnp.max(logits[0], axis=0)
        for l in logits[1:]:
            top = jnp.maximum(top, jnp.max(l, axis=0))
        total = jnp.sum(jnp.exp(logits[0] - top[None, :]), axis=0)
        for l in logits[1:]:
            total = total + jnp.sum(jnp.exp(l - top[None, :]), axis=0)
        return jnp.stack([top, total])

    info = jnp.stack([targets.astype(f32), loss_mask.astype(f32)])
    stats = jnp.concatenate([local(near_own, far_own), local(near_cross, far_cross)], axis=1)
    sent = jnp.concatenate([stats, jnp.concatenate([info, info], axis=1)], axis=0)
    came = swap_x(sent)
    stats = merge(stats, jnp.concatenate([came[:2, toks:], came[:2, :toks]], axis=1))
    info = jnp.concatenate([info, came[2:, :toks]], axis=1)
    target_row = info[0].astype(jnp.int32)
    weight_row = loss_scale * info[1]
    fresh = lax.dot_general(
        rows_pair, hidden_basis, (((1,), (0,)), ((), ())), preferred_element_type=f32
    )
    stats = merge(stats, local(fresh))
    for bit in bits:
        stats = merge(stats, swap_z(stats, bit))
    row_top, sum_exp = stats[0], stats[1]
    scale_row = weight_row / sum_exp

    def grad_of(frozen, first, cols):
        row_ids = (lax.broadcasted_iota(jnp.int32, frozen.shape, 0) ^ turn) + first
        hit = jnp.where(row_ids == target_row[None, cols], weight_row[None, cols], 0.0)
        return (jnp.exp(frozen - row_top[None, cols]) * scale_row[None, cols] - hit).astype(bf16)

    at_own, at_cross = slice(0, toks), slice(toks, 2 * toks)
    grad_cross = (grad_of(near_cross, near_first, at_cross), grad_of(far_cross, far_first, at_cross))
    grad_own = (grad_of(near_own, near_first, at_own), grad_of(far_own, far_first, at_own))

    laid = [kept, kept_core] + beside + beside_core
    laid[0], _ = lax.optimization_barrier((kept, both_cross))
    places, row = [], 0
    for group in ([kept], [kept_core], beside, beside_core):
        column = 0
        for array in group:
            places.append((len(places), None, 0, row, column))
            column += array.shape[1]
        row += rows
    (weights,) = copy_blocks([(4 * rows, depth)], lambda: places, *laid, source=pltpu.VMEM)

    def part(grads, j):
        return dot_first(grads, weights[:, j * width : (j + 1) * width])

    grad_cross = jnp.concatenate(grad_cross, axis=0)
    grad_own = jnp.concatenate(grad_own, axis=0)
    sums, from_x, first_z = {}, {}, None
    for j in reversed(range(n_z)):
        send = part(grad_cross, j).astype(bf16)
        if j + 2 in from_x:
            waits = (from_x[j + 2], first_came) if j == 0 else (first_z, first_z)
            send, *_ = lax.optimization_barrier((send, *waits))
        if j == n_z - 2:
            send, _ = lax.optimization_barrier((send, first_send))
        first_send = send if j == n_z - 1 else first_send
        from_x[j] = swap_x(send)
        sums[j] = part(grad_own, j) + from_x[j].astype(f32)
        if first_z is None:
            first_z = sums[j].astype(bf16)
            first_came = swap_z(first_z, bits[0]) if bits else first_z
    fresh, _ = lax.optimization_barrier((fresh, first_z))
    fresh_ids = lax.broadcasted_iota(jnp.int32, (2 * new_here, toks), 0) ^ new_first
    fresh_ids = fresh_ids + rows * n_tok * n_vocab
    fresh_hit = jnp.where(fresh_ids == targets[None, :], weight_row[None, :toks], 0.0)
    fresh_grad = (
        jnp.exp(fresh[:, :toks] - row_top[None, :toks]) * scale_row[None, :toks] - fresh_hit
    ).astype(bf16)
    mix_total = dot_first(rows_pair, fresh_grad)
    for bit in bits:
        if bit > 1:
            mix_total, *_ = lax.optimization_barrier((mix_total, first_came))
        mix_total = mix_total + swap_z(mix_total, bit)
    mix_total = mix_total.astype(bf16)
    rows_part = dot_last(fresh_grad[:new_here], hidden_basis[:, :toks])
    basis_part = jnp.dot(mix_total, hidden, preferred_element_type=f32)

    came_z = None
    for bit in bits:
        for j in [j for j in sorted(sums, reverse=True) if j & bit]:
            total = sums.pop(j)
            send = first_z if j == n_z - 1 else total.astype(bf16)
            if bit == bits[0] and came_z is not None:
                send, _ = lax.optimization_barrier((send, came_z))
            came = first_came if j == n_z - 1 else swap_z(send, bit)
            came_z = came if came_z is None else came_z
            total = sums[j ^ bit]
            sums[j ^ bit] = total + came.astype(f32)
    hidden_grad = finish(total + dot_first(mix_total, basis_half[:, :width]), came)

    factor_part = jnp.concatenate([basis_part, rows_part], axis=1)
    factor_two = lax.reduce_precision(factor_part + swap_core(factor_part), 8, 7)
    factor_two, _ = lax.optimization_barrier((factor_two, from_x[min(1, n_z - 1)]))
    factor_grad = factor_two + swap_x(factor_two.astype(bf16)).astype(f32)
    basis_grad, rows_grad = factor_grad[:, :width], factor_grad[:, width:]
    return hidden_grad, rows_grad, basis_grad


def on_many(hidden, head, factor_rows, factor_basis, targets, loss_mask):
    n_vocab = lax.axis_size("vocab")
    n_tok = lax.axis_size("tok")
    vocab_index = lax.axis_index("vocab")
    rows_here = head.shape[0] * n_tok
    new_here = factor_rows.shape[0]
    width_here = hidden.shape[1]
    gathered = lax.all_gather(hidden, "vocab", axis=1, tiled=True)
    head_full = lax.all_gather(head, "tok", axis=0, tiled=True)
    frozen = dot_last(gathered, head_full)
    hidden_basis = dot_last(gathered, factor_basis).astype(bf16)
    fresh_logits = dot_last(hidden_basis, factor_rows)
    local_max = jnp.maximum(jnp.max(frozen, axis=1), jnp.max(fresh_logits, axis=1))
    row_top = lax.pmax(local_max, "vocab")
    local_sum = jnp.sum(jnp.exp(frozen - row_top[:, None]), axis=1) + jnp.sum(
        jnp.exp(fresh_logits - row_top[:, None]), axis=1
    )
    sum_exp = lax.psum(local_sum, "vocab")
    frozen_prob = jnp.exp(frozen - row_top[:, None]) / sum_exp[:, None]
    fresh_prob = jnp.exp(fresh_logits - row_top[:, None]) / sum_exp[:, None]
    frozen_offset = targets - vocab_index * rows_here
    fresh_offset = targets - rows_here * n_vocab - vocab_index * new_here
    frozen_hit = (
        lax.broadcasted_iota(jnp.int32, frozen.shape, 1) == frozen_offset[:, None]
    ).astype(f32)
    fresh_hit = (
        lax.broadcasted_iota(jnp.int32, fresh_logits.shape, 1) == fresh_offset[:, None]
    ).astype(f32)
    weight_row = loss_scale * loss_mask.astype(f32)[:, None]
    frozen_grad = (weight_row * (frozen_prob - frozen_hit)).astype(bf16)
    fresh_grad = (weight_row * (fresh_prob - fresh_hit)).astype(bf16)
    mix_term = jnp.dot(fresh_grad, factor_rows, preferred_element_type=f32)
    mix_total = lax.psum(mix_term, "vocab").astype(bf16)
    grad_part = lax.psum_scatter(
        lax.dot_general(
            head_full, frozen_grad, (((0,), (1,)), ((), ())), preferred_element_type=f32
        ),
        "vocab",
        scatter_dimension=0,
        tiled=True,
    )
    basis_cols = lax.dynamic_slice_in_dim(factor_basis, vocab_index * width_here, width_here, 1)
    hidden_grad = (
        grad_part.T + jnp.dot(mix_total, basis_cols, preferred_element_type=f32)
    ).astype(bf16)
    rows_term = dot_first(fresh_grad, hidden_basis)
    basis_term = dot_first(mix_total, hidden)
    rows_grad, basis_grad = (
        lax.psum(rows_term.astype(bf16), "tok").astype(f32),
        lax.psum(basis_term.astype(bf16), "tok").astype(f32),
    )
    return hidden_grad, rows_grad, basis_grad


def solution(mesh):
    in_specs = (
        P("tok", "vocab"),
        P(("vocab", "tok"), None),
        P("vocab", None),
        P(),
        P("tok"),
        P("tok"),
    )
    out_specs = (P("tok", "vocab"), P("vocab", None), P(None, "vocab"))

    def on_device(hidden, head, factor_rows, *rest):
        even = [n & (n - 1) == 0 for n in (mesh.shape["vocab"], head.shape[0], factor_rows.shape[0])]
        few = 2 <= mesh.shape["vocab"] <= 16 and mesh.shape["tok"] == 4 and all(even)
        few = few and hidden.shape[0] == 2 * factor_rows.shape[1]
        return (on_few if few else on_many)(hidden, head, factor_rows, *rest)

    return jax.shard_map(
        on_device, mesh=mesh, in_specs=in_specs, out_specs=out_specs, check_vma=False
    )
```

```python
import jax
import jax.numpy as jnp
from jax import lax
from jax.experimental import pallas as pl
from jax.experimental.pallas import tpu as pltpu
from jax.sharding import PartitionSpec as P

loss_scale = 64.0
f32 = jnp.float32
bf16 = jnp.bfloat16
contract_last = (((1,), (1,)), ((), ()))
contract_first = (((0,), (0,)), ((), ()))


def dot_last(a, b):
    return lax.dot_general(a, b, contract_last, preferred_element_type=f32)


def dot_first(a, b):
    return lax.dot_general(a, b, contract_first, preferred_element_type=f32)


def swap(value, axis, bit):
    size = lax.axis_size(axis)
    return lax.ppermute(value, axis, [(i, i ^ bit) for i in range(size)])


def swap_core(value):
    return swap(value, "tok", 1)


def swap_x(value):
    return swap(value, "tok", 2)


def swap_y(value):
    return swap(value, "vocab", 1)


def swap_z(value, step):
    return swap(value, "vocab", 2 * step)


in_vmem = pl.BlockSpec(memory_space=pltpu.VMEM)


def copy_blocks(shapes, moves, *arrays, source=pltpu.HBM):
    def kernel(*refs):
        ins, outs, sems = refs[: len(arrays)], refs[len(arrays) : -1], refs[-1]
        copies = []
        for n, (origin, columns, target, row, column) in enumerate(moves()):
            src, dst = ins[origin], outs[target]
            if columns is not None:
                src = src.at[:, pl.ds(pl.multiple_of(columns[0], 128), columns[1])]
            dst = dst.at[pl.ds(row, src.shape[0]), pl.ds(column, src.shape[1])]
            copies.append(pltpu.make_async_copy(src, dst, sems.at[n]))
        for copy in copies:
            copy.start()
        for copy in copies:
            copy.wait()

    size = sum(2 * shape[0] * shape[1] for shape in shapes)
    return pl.pallas_call(
        kernel,
        out_shape=[jax.ShapeDtypeStruct(shape, bf16) for shape in shapes],
        in_specs=[pl.BlockSpec(memory_space=source)] * len(arrays),
        out_specs=[in_vmem] * len(shapes),
        scratch_shapes=[pltpu.SemaphoreType.DMA((32,))],
        compiler_params=pltpu.CompilerParams(vmem_limit_bytes=12 << 20),
        cost_estimate=pl.CostEstimate(flops=0, bytes_accessed=2 * size, transcendentals=0),
    )(*arrays)


def logits_of(groups, tokens, rider=None):
    toks, width = tokens[0].shape
    heights = [group[0].shape[0] for group in groups]
    total, depth = sum(heights), width * len(tokens)
    flat = [a for group in groups for a in group]
    riders = [] if rider is None else [rider]
    extra = 0 if rider is None else rider.shape[0] // 2
    n_flat, n_all = len(flat), len(flat) + len(tokens) + len(riders)

    def kernel(*refs):
        out = refs[n_all]
        at, row = 0, 0
        for group, height in zip(groups, heights):
            result, column = None, 0
            for part in group:
                for c in range(0, part.shape[1], width):
                    token = refs[n_flat + (column + c) // width]
                    term = dot_last(refs[at][:, c : c + width], token[...])
                    result = term if result is None else result + term
                at, column = at + 1, column + part.shape[1]
            out[row : row + height, :] = result
            row += height
        if extra:
            wide = refs[n_all - 1][...].astype(f32)
            out[row:, :] = jnp.concatenate([wide[:extra], wide[extra:]], axis=1)

    return pl.pallas_call(
        kernel,
        out_shape=jax.ShapeDtypeStruct((total + extra, toks), f32),
        in_specs=[in_vmem] * n_all,
        out_specs=in_vmem,
        compiler_params=pltpu.CompilerParams(vmem_limit_bytes=12 << 20),
        cost_estimate=pl.CostEstimate(
            flops=2 * total * depth * toks,
            bytes_accessed=2 * (total + toks) * depth + 4 * total * toks,
            transcendentals=0,
        ),
    )(*flat, *tokens, *riders)


def finish(total, came):
    def kernel(total_ref, came_ref, out):
        out[...] = (total_ref[...] + came_ref[...].astype(f32)).astype(bf16)

    return pl.pallas_call(
        kernel,
        out_shape=jax.ShapeDtypeStruct(total.shape, bf16),
        in_specs=[in_vmem] * 2,
        out_specs=in_vmem,
        compiler_params=pltpu.CompilerParams(vmem_limit_bytes=4 << 20),
        cost_estimate=pl.CostEstimate(
            flops=8 * total.size, bytes_accessed=8 * total.size, transcendentals=0
        ),
    )(total, came)


def on_few(hidden, head, factor_rows, factor_basis, targets, loss_mask):
    n_vocab, n_tok = lax.axis_size("vocab"), lax.axis_size("tok")
    n_z = n_vocab // 2
    bits = [1 << b for b in range(n_z.bit_length() - 1)]
    v = lax.axis_index("vocab")
    t = lax.axis_index("tok")
    toks, width = hidden.shape
    rows = head.shape[0]
    new_here = factor_rows.shape[0]
    rank = factor_basis.shape[0]
    depth = n_z * width

    near_first = v * (n_tok * rows) + (t >> 1) * (2 * rows)
    far_first = (v ^ 1) * (n_tok * rows) + (t >> 1) * (2 * rows)
    turn = (t & 1) * rows
    new_first = v * new_here
    hidden, head, near_first, far_first, turn, new_first = lax.optimization_barrier(
        (hidden, head, near_first, far_first, turn, new_first)
    )

    def start_of(j, other):
        return (lax.axis_index("vocab") ^ (2 * j + other)) * width

    cuts = [0, n_z]
    chunks = [range(a, b) for a, b in zip(cuts, cuts[1:]) if a < b]
    sends = copy_blocks(
        [(rows, len(chunk) * width) for chunk in chunks],
        lambda: [
            (0, (start_of(j, 1), width), n, 0, (j - chunk[0]) * width)
            for n, chunk in enumerate(chunks)
            for j in chunk
        ],
        head,
    )
    beside = [swap_y(send) for send in sends]

    def half(array, after):
        array, _ = lax.optimization_barrier((array, after))
        moves = lambda: [(0, (start_of(j, 0), width), 0, 0, j * width) for j in range(n_z)]
        return copy_blocks([(array.shape[0], depth)], moves, array)[0]

    after, _ = lax.optimization_barrier((hidden, sends[0]))
    shards, cross = {0: hidden}, {0: swap_x(hidden)}
    for bit in reversed(bits):
        near = swap_z(hidden if bit == 1 else hidden, bit)
        for j in [j for j in shards if j]:
            shards[j], *_ = lax.optimization_barrier((shards[j], near))
            shards[j ^ bit] = swap_z(shards[j], bit)
        shards[bit] = near
    for j in range(1, n_z):
        sent = shards[j]
        waits = [] if j == 1 else [cross[j - 2]] if j < n_z - 1 else [cross[j - 2], beside[0]]
        if waits:
            sent, *_ = lax.optimization_barrier((sent, *waits))
        cross[j] = swap_x(sent)
    kept = half(head, cross[1])
    kept_core = swap_core(kept)
    basis_half = half(factor_basis, cross[0])

    beside_core = []
    for n, came in enumerate(beside):
        came, *_ = lax.optimization_barrier((came, cross[n_z - 2], shards[n_z - 1]))
        beside_core.append(swap_core(came))

    in_order = lambda parts: [parts[j] for j in range(n_z)]
    basis_ready, *_ = lax.optimization_barrier((basis_half, cross[1]))
    upper = [[kept], [kept_core], [basis_ready]]
    upper_own = logits_of(upper, in_order(shards))
    beside_core[-1], *_ = lax.optimization_barrier((beside_core[-1], upper_own))
    lower_own = logits_of([beside, beside_core], in_order(shards))
    cross[0], _ = lax.optimization_barrier((cross[0], lower_own))
    both_cross = logits_of(upper + [beside, beside_core], in_order(cross), factor_rows)
    n_up = 2 * rows + rank

    def add_over_y(up, low, up_came, low_came):
        near = up[: 2 * rows] + low_came
        far = low + up_came[: 2 * rows]
        return near, far, (up[2 * rows :] + up_came[2 * rows :]).astype(bf16)

    upper_came, lower_came = swap_y(upper_own), swap_y(lower_own)
    cross_came = swap_y(both_cross)
    upper_came, _ = lax.optimization_barrier((upper_came, both_cross))
    near_own, far_own, basis_own = add_over_y(upper_own, lower_own, upper_came, lower_came)
    near_cross, far_cross, basis_cross = add_over_y(
        both_cross[:n_up], both_cross[n_up : n_up + 2 * rows], cross_came[:n_up], cross_came[n_up : n_up + 2 * rows]
    )
    hidden_basis = jnp.concatenate([basis_own, basis_cross], axis=1)

    n_rows = n_up + 2 * rows
    rows_came = cross_came[n_rows:].astype(bf16)
    rows_pair = jnp.concatenate([factor_rows, rows_came[:, :rank], rows_came[:, rank:]], axis=0)

    def merge(a, b):
        top = jnp.maximum(a[0], b[0])
        return jnp.stack([top, a[1] * jnp.exp(a[0] - top) + b[1] * jnp.exp(b[0] - top)])

    def local(*logits):
        top = jnp.max(logits[0], axis=0)
        for l in logits[1:]:
            top = jnp.maximum(top, jnp.max(l, axis=0))
        total = jnp.sum(jnp.exp(logits[0] - top[None, :]), axis=0)
        for l in logits[1:]:
            total = total + jnp.sum(jnp.exp(l - top[None, :]), axis=0)
        return jnp.stack([top, total])

    info = jnp.stack([targets.astype(f32), loss_mask.astype(f32)])
    stats = jnp.concatenate([local(near_own, far_own), local(near_cross, far_cross)], axis=1)
    sent = jnp.concatenate([stats, jnp.concatenate([info, info], axis=1)], axis=0)
    came = swap_x(sent)
    stats = merge(stats, jnp.concatenate([came[:2, toks:], came[:2, :toks]], axis=1))
    info = jnp.concatenate([info, came[2:, :toks]], axis=1)
    target_row = info[0].astype(jnp.int32)
    weight_row = loss_scale * info[1]
    fresh = lax.dot_general(
        rows_pair, hidden_basis, (((1,), (0,)), ((), ())), preferred_element_type=f32
    )
    stats = merge(stats, local(fresh))
    for bit in bits:
        stats = merge(stats, swap_z(stats, bit))
    row_top, sum_exp = stats[0], stats[1]
    scale_row = weight_row / sum_exp

    def grad_of(frozen, first, cols):
        row_ids = (lax.broadcasted_iota(jnp.int32, frozen.shape, 0) ^ turn) + first
        hit = jnp.where(row_ids == target_row[None, cols], weight_row[None, cols], 0.0)
        return (jnp.exp(frozen - row_top[None, cols]) * scale_row[None, cols] - hit).astype(bf16)

    at_own, at_cross = slice(0, toks), slice(toks, 2 * toks)
    grad_cross = (grad_of(near_cross, near_first, at_cross), grad_of(far_cross, far_first, at_cross))
    grad_own = (grad_of(near_own, near_first, at_own), grad_of(far_own, far_first, at_own))

    laid = [kept, kept_core] + beside + beside_core
    laid[0], _ = lax.optimization_barrier((kept, both_cross))
    places, row = [], 0
    for group in ([kept], [kept_core], beside, beside_core):
        column = 0
        for array in group:
            places.append((len(places), None, 0, row, column))
            column += array.shape[1]
        row += rows
    (weights,) = copy_blocks([(4 * rows, depth)], lambda: places, *laid, source=pltpu.VMEM)

    def part(grads, j):
        return dot_first(grads, weights[:, j * width : (j + 1) * width])

    grad_cross = jnp.concatenate(grad_cross, axis=0)
    grad_own = jnp.concatenate(grad_own, axis=0)
    sums, from_x, first_z = {}, {}, None
    for j in reversed(range(n_z)):
        send = part(grad_cross, j).astype(bf16)
        if j + 2 in from_x:
            waits = (from_x[j + 2], first_came) if j == 0 else (first_z, first_z)
            send, *_ = lax.optimization_barrier((send, *waits))
        if j == n_z - 2:
            send, _ = lax.optimization_barrier((send, first_send))
        first_send = send if j == n_z - 1 else first_send
        from_x[j] = swap_x(send)
        sums[j] = part(grad_own, j) + from_x[j].astype(f32)
        if first_z is None:
            first_z = sums[j].astype(bf16)
            first_came = swap_z(first_z, bits[0]) if bits else first_z
    fresh, _ = lax.optimization_barrier((fresh, first_z))
    fresh_ids = lax.broadcasted_iota(jnp.int32, (2 * new_here, toks), 0) ^ new_first
    fresh_ids = fresh_ids + rows * n_tok * n_vocab
    fresh_hit = jnp.where(fresh_ids == targets[None, :], weight_row[None, :toks], 0.0)
    fresh_grad = (
        jnp.exp(fresh[:, :toks] - row_top[None, :toks]) * scale_row[None, :toks] - fresh_hit
    ).astype(bf16)
    mix_total = dot_first(rows_pair, fresh_grad)
    for bit in reversed(bits):
        if bit == 1:
            mix_total, *_ = lax.optimization_barrier((mix_total, first_came))
        mix_total = mix_total + swap_z(mix_total, bit)
    mix_total = mix_total.astype(bf16)
    rows_part = dot_last(fresh_grad[:new_here], hidden_basis[:, :toks])
    basis_part = jnp.dot(mix_total, hidden, preferred_element_type=f32)

    came_z = None
    for bit in bits:
        for j in [j for j in sorted(sums, reverse=True) if j & bit]:
            total = sums.pop(j)
            send = first_z if j == n_z - 1 else total.astype(bf16)
            if bit == bits[0] and came_z is not None:
                send, _ = lax.optimization_barrier((send, came_z))
            came = first_came if j == n_z - 1 else swap_z(send, bit)
            came_z = came if came_z is None else came_z
            total = sums[j ^ bit]
            sums[j ^ bit] = total + came.astype(f32)
    factor_part = jnp.concatenate([basis_part, rows_part], axis=1)
    factor_two = lax.reduce_precision(factor_part + swap_core(factor_part), 8, 7)
    factor_two, _ = lax.optimization_barrier((factor_two, from_x[min(1, n_z - 1)]))
    factor_grad = factor_two + swap_x(factor_two.astype(bf16)).astype(f32)
    basis_grad, rows_grad = factor_grad[:, :width], factor_grad[:, width:]
    came, basis_grad, rows_grad = lax.optimization_barrier((came, basis_grad, rows_grad))
    hidden_grad = finish(total + dot_first(mix_total, basis_half[:, :width]), came)

    return hidden_grad, rows_grad, basis_grad


def on_many(hidden, head, factor_rows, factor_basis, targets, loss_mask):
    n_vocab = lax.axis_size("vocab")
    n_tok = lax.axis_size("tok")
    vocab_index = lax.axis_index("vocab")
    rows_here = head.shape[0] * n_tok
    new_here = factor_rows.shape[0]
    width_here = hidden.shape[1]
    gathered = lax.all_gather(hidden, "vocab", axis=1, tiled=True)
    head_full = lax.all_gather(head, "tok", axis=0, tiled=True)
    frozen = dot_last(gathered, head_full)
    hidden_basis = dot_last(gathered, factor_basis).astype(bf16)
    fresh_logits = dot_last(hidden_basis, factor_rows)
    local_max = jnp.maximum(jnp.max(frozen, axis=1), jnp.max(fresh_logits, axis=1))
    row_top = lax.pmax(local_max, "vocab")
    local_sum = jnp.sum(jnp.exp(frozen - row_top[:, None]), axis=1) + jnp.sum(
        jnp.exp(fresh_logits - row_top[:, None]), axis=1
    )
    sum_exp = lax.psum(local_sum, "vocab")
    frozen_prob = jnp.exp(frozen - row_top[:, None]) / sum_exp[:, None]
    fresh_prob = jnp.exp(fresh_logits - row_top[:, None]) / sum_exp[:, None]
    frozen_offset = targets - vocab_index * rows_here
    fresh_offset = targets - rows_here * n_vocab - vocab_index * new_here
    frozen_hit = (
        lax.broadcasted_iota(jnp.int32, frozen.shape, 1) == frozen_offset[:, None]
    ).astype(f32)
    fresh_hit = (
        lax.broadcasted_iota(jnp.int32, fresh_logits.shape, 1) == fresh_offset[:, None]
    ).astype(f32)
    weight_row = loss_scale * loss_mask.astype(f32)[:, None]
    frozen_grad = (weight_row * (frozen_prob - frozen_hit)).astype(bf16)
    fresh_grad = (weight_row * (fresh_prob - fresh_hit)).astype(bf16)
    mix_term = jnp.dot(fresh_grad, factor_rows, preferred_element_type=f32)
    mix_total = lax.psum(mix_term, "vocab").astype(bf16)
    grad_part = lax.psum_scatter(
        lax.dot_general(
            head_full, frozen_grad, (((0,), (1,)), ((), ())), preferred_element_type=f32
        ),
        "vocab",
        scatter_dimension=0,
        tiled=True,
    )
    basis_cols = lax.dynamic_slice_in_dim(factor_basis, vocab_index * width_here, width_here, 1)
    hidden_grad = (
        grad_part.T + jnp.dot(mix_total, basis_cols, preferred_element_type=f32)
    ).astype(bf16)
    rows_term = dot_first(fresh_grad, hidden_basis)
    basis_term = dot_first(mix_total, hidden)
    rows_grad, basis_grad = (
        lax.psum(rows_term.astype(bf16), "tok").astype(f32),
        lax.psum(basis_term.astype(bf16), "tok").astype(f32),
    )
    return hidden_grad, rows_grad, basis_grad


def solution(mesh):
    in_specs = (
        P("tok", "vocab"),
        P(("vocab", "tok"), None),
        P("vocab", None),
        P(),
        P("tok"),
        P("tok"),
    )
    out_specs = (P("tok", "vocab"), P("vocab", None), P(None, "vocab"))

    def on_device(hidden, head, factor_rows, *rest):
        even = [n & (n - 1) == 0 for n in (mesh.shape["vocab"], head.shape[0], factor_rows.shape[0])]
        few = 2 <= mesh.shape["vocab"] <= 16 and mesh.shape["tok"] == 4 and all(even)
        few = few and hidden.shape[0] == 2 * factor_rows.shape[1]
        return (on_few if few else on_many)(hidden, head, factor_rows, *rest)

    return jax.shard_map(
        on_device, mesh=mesh, in_specs=in_specs, out_specs=out_specs, check_vma=False
    )
```

```python
import jax
import jax.numpy as jnp
from jax import lax
from jax.experimental import pallas as pl
from jax.experimental.pallas import tpu as pltpu
from jax.sharding import PartitionSpec as P

loss_scale = 64.0
f32 = jnp.float32
bf16 = jnp.bfloat16
contract_last = (((1,), (1,)), ((), ()))
contract_first = (((0,), (0,)), ((), ()))


def dot_last(a, b):
    return lax.dot_general(a, b, contract_last, preferred_element_type=f32)


def dot_first(a, b):
    return lax.dot_general(a, b, contract_first, preferred_element_type=f32)


def swap(value, axis, bit):
    size = lax.axis_size(axis)
    return lax.ppermute(value, axis, [(i, i ^ bit) for i in range(size)])


def swap_core(value):
    return swap(value, "tok", 1)


def swap_x(value):
    return swap(value, "tok", 2)


def swap_y(value):
    return swap(value, "vocab", 1)


def swap_z(value, step):
    return swap(value, "vocab", 2 * step)


in_vmem = pl.BlockSpec(memory_space=pltpu.VMEM)


def copy_blocks(shapes, moves, *arrays, source=pltpu.HBM):
    def kernel(*refs):
        ins, outs, sems = refs[: len(arrays)], refs[len(arrays) : -1], refs[-1]
        copies = []
        for n, (origin, columns, target, row, column) in enumerate(moves()):
            src, dst = ins[origin], outs[target]
            if columns is not None:
                src = src.at[:, pl.ds(pl.multiple_of(columns[0], 128), columns[1])]
            dst = dst.at[pl.ds(row, src.shape[0]), pl.ds(column, src.shape[1])]
            copies.append(pltpu.make_async_copy(src, dst, sems.at[n]))
        for copy in copies:
            copy.start()
        for copy in copies:
            copy.wait()

    size = sum(2 * shape[0] * shape[1] for shape in shapes)
    return pl.pallas_call(
        kernel,
        out_shape=[jax.ShapeDtypeStruct(shape, bf16) for shape in shapes],
        in_specs=[pl.BlockSpec(memory_space=source)] * len(arrays),
        out_specs=[in_vmem] * len(shapes),
        scratch_shapes=[pltpu.SemaphoreType.DMA((32,))],
        compiler_params=pltpu.CompilerParams(vmem_limit_bytes=12 << 20),
        cost_estimate=pl.CostEstimate(flops=0, bytes_accessed=2 * size, transcendentals=0),
    )(*arrays)


def logits_of(groups, tokens, rider=None, first=0, before=None):
    toks, width = tokens[0].shape
    heights = [group[0].shape[0] for group in groups]
    total, depth = sum(heights), width * len(tokens)
    blocks = range(first, first + len(tokens))
    flat = [a for group in groups for a in group]
    riders = [a for a in (before, rider) if a is not None]
    extra = 0 if rider is None else rider.shape[0] // 2
    n_flat, n_all = len(flat), len(flat) + len(tokens) + len(riders)

    def kernel(*refs):
        out = refs[n_all]
        at, row = 0, 0
        for group, height in zip(groups, heights):
            result, column = None, 0
            if before is not None:
                result = refs[n_flat + len(tokens)][row : row + height, :]
            for part in group:
                for c in range(0, part.shape[1], width):
                    block = (column + c) // width
                    if block not in blocks:
                        continue
                    token = refs[n_flat + block - first]
                    term = dot_last(refs[at][:, c : c + width], token[...])
                    result = term if result is None else result + term
                at, column = at + 1, column + part.shape[1]
            out[row : row + height, :] = result
            row += height
        if extra:
            wide = refs[n_all - 1][...].astype(f32)
            out[row:, :] = jnp.concatenate([wide[:extra], wide[extra:]], axis=1)

    return pl.pallas_call(
        kernel,
        out_shape=jax.ShapeDtypeStruct((total + extra, toks), f32),
        in_specs=[in_vmem] * n_all,
        out_specs=in_vmem,
        compiler_params=pltpu.CompilerParams(vmem_limit_bytes=12 << 20),
        cost_estimate=pl.CostEstimate(
            flops=2 * total * depth * toks,
            bytes_accessed=2 * (total + toks) * depth + 4 * total * toks,
            transcendentals=0,
        ),
    )(*flat, *tokens, *riders)


def finish(total, pieces, factor, factor_came):
    width = total.shape[1]

    def kernel(total_ref, *refs):
        result = total_ref[...]
        for piece in refs[: len(pieces)]:
            result = result + piece[...].astype(f32)
        factor_ref, came_ref, hidden_out, basis_out, rows_out = refs[len(pieces) :]
        hidden_out[...] = result.astype(bf16)
        both = factor_ref[...] + came_ref[...].astype(f32)
        basis_out[...] = both[:, :width]
        rows_out[...] = both[:, width:]

    rank, wide = factor.shape
    return pl.pallas_call(
        kernel,
        out_shape=[
            jax.ShapeDtypeStruct(total.shape, bf16),
            jax.ShapeDtypeStruct((rank, width), f32),
            jax.ShapeDtypeStruct((rank, wide - width), f32),
        ],
        in_specs=[in_vmem] * (3 + len(pieces)),
        out_specs=[in_vmem] * 3,
        compiler_params=pltpu.CompilerParams(vmem_limit_bytes=4 << 20),
        cost_estimate=pl.CostEstimate(
            flops=3 * total.size, bytes_accessed=12 * total.size, transcendentals=0
        ),
    )(total, *pieces, factor, factor_came)


def on_few(hidden, head, factor_rows, factor_basis, targets, loss_mask):
    n_vocab, n_tok = lax.axis_size("vocab"), lax.axis_size("tok")
    n_z = n_vocab // 2
    bits = [1 << b for b in range(n_z.bit_length() - 1)]
    v = lax.axis_index("vocab")
    t = lax.axis_index("tok")
    toks, width = hidden.shape
    rows = head.shape[0]
    new_here = factor_rows.shape[0]
    rank = factor_basis.shape[0]
    depth = n_z * width

    near_first = v * (n_tok * rows) + (t >> 1) * (2 * rows)
    far_first = (v ^ 1) * (n_tok * rows) + (t >> 1) * (2 * rows)
    turn = (t & 1) * rows
    new_first = v * new_here
    hidden, head, near_first, far_first, turn, new_first = lax.optimization_barrier(
        (hidden, head, near_first, far_first, turn, new_first)
    )

    def start_of(j, other):
        return (lax.axis_index("vocab") ^ (2 * j + other)) * width

    cuts = [0, n_z]
    chunks = [range(a, b) for a, b in zip(cuts, cuts[1:]) if a < b]
    sends = copy_blocks(
        [(rows, len(chunk) * width) for chunk in chunks],
        lambda: [
            (0, (start_of(j, 1), width), n, 0, (j - chunk[0]) * width)
            for n, chunk in enumerate(chunks)
            for j in chunk
        ],
        head,
    )
    beside = [swap_y(send) for send in sends]

    def half(array, after):
        array, _ = lax.optimization_barrier((array, after))
        moves = lambda: [(0, (start_of(j, 0), width), 0, 0, j * width) for j in range(n_z)]
        return copy_blocks([(array.shape[0], depth)], moves, array)[0]

    after, _ = lax.optimization_barrier((hidden, sends[0]))
    shards, cross = {0: hidden}, {0: swap_x(hidden)}
    for bit in reversed(bits):
        near = swap_z(hidden if bit == 1 else hidden, bit)
        for j in [j for j in shards if j]:
            shards[j], *_ = lax.optimization_barrier((shards[j], near))
            shards[j ^ bit] = swap_z(shards[j], bit)
        shards[bit] = near
    for j in range(1, n_z):
        sent = shards[j]
        waits = [] if j == 1 else [cross[j - 2]] if j < n_z - 1 else [cross[j - 2], beside[0]]
        if waits:
            sent, *_ = lax.optimization_barrier((sent, *waits))
        cross[j] = swap_x(sent)
    kept = half(head, cross[1])
    kept_core = swap_core(kept)
    basis_half = half(factor_basis, cross[0])

    beside_core = []
    for n, came in enumerate(beside):
        came, *_ = lax.optimization_barrier((came, cross[n_z - 2], shards[n_z - 1]))
        beside_core.append(swap_core(came))

    in_order = lambda parts: [parts[j] for j in range(n_z)]
    basis_ready, *_ = lax.optimization_barrier((basis_half, cross[1]))
    upper = [[kept], [kept_core], [basis_ready]]
    upper_own = logits_of(upper, in_order(shards))
    beside_core[-1], *_ = lax.optimization_barrier((beside_core[-1], upper_own))
    lower_own = logits_of([beside, beside_core], in_order(shards))
    cross[0], _ = lax.optimization_barrier((cross[0], lower_own))
    every = upper + [beside, beside_core]
    early_cross = logits_of(every, in_order(cross)[:-1]) if n_z > 1 else None
    both_cross = logits_of(every, in_order(cross)[-1:], factor_rows, n_z - 1, early_cross)
    n_up = 2 * rows + rank

    def add_over_y(up, low, up_came, low_came):
        near = up[: 2 * rows] + low_came
        far = low + up_came[: 2 * rows]
        return near, far, (up[2 * rows :] + up_came[2 * rows :]).astype(bf16)

    upper_came, lower_came = swap_y(upper_own), swap_y(lower_own)
    cross_came = swap_y(both_cross)
    upper_came, _ = lax.optimization_barrier((upper_came, both_cross))
    near_own, far_own, basis_own = add_over_y(upper_own, lower_own, upper_came, lower_came)
    near_cross, far_cross, basis_cross = add_over_y(
        both_cross[:n_up], both_cross[n_up : n_up + 2 * rows], cross_came[:n_up], cross_came[n_up : n_up + 2 * rows]
    )
    hidden_basis = jnp.concatenate([basis_own, basis_cross], axis=1)

    n_rows = n_up + 2 * rows
    rows_came = cross_came[n_rows:].astype(bf16)
    rows_pair = jnp.concatenate([factor_rows, rows_came[:, :rank], rows_came[:, rank:]], axis=0)

    def merge(a, b):
        top = jnp.maximum(a[0], b[0])
        return jnp.stack([top, a[1] * jnp.exp(a[0] - top) + b[1] * jnp.exp(b[0] - top)])

    def local(*logits):
        top = jnp.max(logits[0], axis=0)
        for l in logits[1:]:
            top = jnp.maximum(top, jnp.max(l, axis=0))
        total = jnp.sum(jnp.exp(logits[0] - top[None, :]), axis=0)
        for l in logits[1:]:
            total = total + jnp.sum(jnp.exp(l - top[None, :]), axis=0)
        return jnp.stack([top, total])

    info = jnp.stack([targets.astype(f32), loss_mask.astype(f32)])
    stats = jnp.concatenate([local(near_own, far_own), local(near_cross, far_cross)], axis=1)
    sent = jnp.concatenate([stats, jnp.concatenate([info, info], axis=1)], axis=0)
    came = swap_x(sent)
    stats = merge(stats, jnp.concatenate([came[:2, toks:], came[:2, :toks]], axis=1))
    info = jnp.concatenate([info, came[2:, :toks]], axis=1)
    target_row = info[0].astype(jnp.int32)
    weight_row = loss_scale * info[1]
    fresh = lax.dot_general(
        rows_pair, hidden_basis, (((1,), (0,)), ((), ())), preferred_element_type=f32
    )
    stats = merge(stats, local(fresh))
    for bit in bits:
        stats = merge(stats, swap_z(stats, bit))
    row_top, sum_exp = stats[0], stats[1]
    scale_row = weight_row / sum_exp

    def grad_of(frozen, first, cols):
        row_ids = (lax.broadcasted_iota(jnp.int32, frozen.shape, 0) ^ turn) + first
        hit = jnp.where(row_ids == target_row[None, cols], weight_row[None, cols], 0.0)
        return (jnp.exp(frozen - row_top[None, cols]) * scale_row[None, cols] - hit).astype(bf16)

    at_own, at_cross = slice(0, toks), slice(toks, 2 * toks)
    grad_cross = (grad_of(near_cross, near_first, at_cross), grad_of(far_cross, far_first, at_cross))
    grad_own = (grad_of(near_own, near_first, at_own), grad_of(far_own, far_first, at_own))

    laid = [kept, kept_core] + beside + beside_core
    laid[0], _ = lax.optimization_barrier((kept, both_cross))
    places, row = [], 0
    for group in ([kept], [kept_core], beside, beside_core):
        column = 0
        for array in group:
            places.append((len(places), None, 0, row, column))
            column += array.shape[1]
        row += rows
    (weights,) = copy_blocks([(4 * rows, depth)], lambda: places, *laid, source=pltpu.VMEM)

    def part(grads, j):
        return dot_first(grads, weights[:, j * width : (j + 1) * width])

    grad_cross = jnp.concatenate(grad_cross, axis=0)
    grad_own = jnp.concatenate(grad_own, axis=0)
    sums, from_x, first_z = {}, {}, None
    for j in reversed(range(n_z)):
        send = part(grad_cross, j).astype(bf16)
        if j + 2 in from_x:
            waits = (from_x[j + 2], first_came) if j == 0 else (first_z, first_z)
            send, *_ = lax.optimization_barrier((send, *waits))
        if j == n_z - 2:
            send, _ = lax.optimization_barrier((send, first_send))
        first_send = send if j == n_z - 1 else first_send
        from_x[j] = swap_x(send)
        sums[j] = part(grad_own, j) + from_x[j].astype(f32)
        if first_z is None:
            first_z = sums[j].astype(bf16)
            first_came = swap_z(first_z, bits[0]) if bits else first_z
    fresh, _ = lax.optimization_barrier((fresh, first_z))
    fresh_ids = lax.broadcasted_iota(jnp.int32, (2 * new_here, toks), 0) ^ new_first
    fresh_ids = fresh_ids + rows * n_tok * n_vocab
    fresh_hit = jnp.where(fresh_ids == targets[None, :], weight_row[None, :toks], 0.0)
    fresh_grad = (
        jnp.exp(fresh[:, :toks] - row_top[None, :toks]) * scale_row[None, :toks] - fresh_hit
    ).astype(bf16)
    mix_total = dot_first(rows_pair, fresh_grad)
    for bit in bits:
        if bit > 1:
            mix_total, *_ = lax.optimization_barrier((mix_total, first_came))
        mix_total = mix_total + swap_z(mix_total, bit)
    mix_total = mix_total.astype(bf16)
    rows_part = dot_last(fresh_grad[:new_here], hidden_basis[:, :toks])
    basis_part = jnp.dot(mix_total, hidden, preferred_element_type=f32)

    came_z, pieces = None, []
    for bit in bits:
        for j in [j for j in sorted(sums, reverse=True) if j & bit]:
            total = sums.pop(j)
            send = first_z if j == n_z - 1 else total.astype(bf16)
            if bit == bits[0] and came_z is not None:
                send, _ = lax.optimization_barrier((send, came_z))
            came = first_came if j == n_z - 1 else swap_z(send, bit)
            came_z = came if came_z is None else came_z
            if j ^ bit:
                sums[j ^ bit] = sums[j ^ bit] + came.astype(f32)
            else:
                pieces.append(came)
    total = sums[0] + dot_first(mix_total, basis_half[:, :width])

    factor_part = jnp.concatenate([basis_part, rows_part], axis=1)
    factor_two = lax.reduce_precision(factor_part + swap_core(factor_part), 8, 7)
    factor_two, _ = lax.optimization_barrier((factor_two, from_x[min(1, n_z - 1)]))
    factor_came = swap_x(factor_two.astype(bf16))
    hidden_grad, basis_grad, rows_grad = finish(total, pieces, factor_two, factor_came)
    return hidden_grad, rows_grad, basis_grad


def on_many(hidden, head, factor_rows, factor_basis, targets, loss_mask):
    n_vocab = lax.axis_size("vocab")
    n_tok = lax.axis_size("tok")
    vocab_index = lax.axis_index("vocab")
    rows_here = head.shape[0] * n_tok
    new_here = factor_rows.shape[0]
    width_here = hidden.shape[1]
    gathered = lax.all_gather(hidden, "vocab", axis=1, tiled=True)
    head_full = lax.all_gather(head, "tok", axis=0, tiled=True)
    frozen = dot_last(gathered, head_full)
    hidden_basis = dot_last(gathered, factor_basis).astype(bf16)
    fresh_logits = dot_last(hidden_basis, factor_rows)
    local_max = jnp.maximum(jnp.max(frozen, axis=1), jnp.max(fresh_logits, axis=1))
    row_top = lax.pmax(local_max, "vocab")
    local_sum = jnp.sum(jnp.exp(frozen - row_top[:, None]), axis=1) + jnp.sum(
        jnp.exp(fresh_logits - row_top[:, None]), axis=1
    )
    sum_exp = lax.psum(local_sum, "vocab")
    frozen_prob = jnp.exp(frozen - row_top[:, None]) / sum_exp[:, None]
    fresh_prob = jnp.exp(fresh_logits - row_top[:, None]) / sum_exp[:, None]
    frozen_offset = targets - vocab_index * rows_here
    fresh_offset = targets - rows_here * n_vocab - vocab_index * new_here
    frozen_hit = (
        lax.broadcasted_iota(jnp.int32, frozen.shape, 1) == frozen_offset[:, None]
    ).astype(f32)
    fresh_hit = (
        lax.broadcasted_iota(jnp.int32, fresh_logits.shape, 1) == fresh_offset[:, None]
    ).astype(f32)
    weight_row = loss_scale * loss_mask.astype(f32)[:, None]
    frozen_grad = (weight_row * (frozen_prob - frozen_hit)).astype(bf16)
    fresh_grad = (weight_row * (fresh_prob - fresh_hit)).astype(bf16)
    mix_term = jnp.dot(fresh_grad, factor_rows, preferred_element_type=f32)
    mix_total = lax.psum(mix_term, "vocab").astype(bf16)
    grad_part = lax.psum_scatter(
        lax.dot_general(
            head_full, frozen_grad, (((0,), (1,)), ((), ())), preferred_element_type=f32
        ),
        "vocab",
        scatter_dimension=0,
        tiled=True,
    )
    basis_cols = lax.dynamic_slice_in_dim(factor_basis, vocab_index * width_here, width_here, 1)
    hidden_grad = (
        grad_part.T + jnp.dot(mix_total, basis_cols, preferred_element_type=f32)
    ).astype(bf16)
    rows_term = dot_first(fresh_grad, hidden_basis)
    basis_term = dot_first(mix_total, hidden)
    rows_grad, basis_grad = (
        lax.psum(rows_term.astype(bf16), "tok").astype(f32),
        lax.psum(basis_term.astype(bf16), "tok").astype(f32),
    )
    return hidden_grad, rows_grad, basis_grad


def solution(mesh):
    in_specs = (
        P("tok", "vocab"),
        P(("vocab", "tok"), None),
        P("vocab", None),
        P(),
        P("tok"),
        P("tok"),
    )
    out_specs = (P("tok", "vocab"), P("vocab", None), P(None, "vocab"))

    def on_device(hidden, head, factor_rows, *rest):
        even = [n & (n - 1) == 0 for n in (mesh.shape["vocab"], head.shape[0], factor_rows.shape[0])]
        few = 2 <= mesh.shape["vocab"] <= 16 and mesh.shape["tok"] == 4 and all(even)
        few = few and hidden.shape[0] == 2 * factor_rows.shape[1]
        return (on_few if few else on_many)(hidden, head, factor_rows, *rest)

    return jax.shard_map(
        on_device, mesh=mesh, in_specs=in_specs, out_specs=out_specs, check_vma=False
    )
```

```python
import jax
import jax.numpy as jnp
from jax import lax
from jax.experimental import pallas as pl
from jax.experimental.pallas import tpu as pltpu
from jax.sharding import PartitionSpec as P

loss_scale = 64.0
f32 = jnp.float32
bf16 = jnp.bfloat16
contract_last = (((1,), (1,)), ((), ()))
contract_first = (((0,), (0,)), ((), ()))


def dot_last(a, b):
    return lax.dot_general(a, b, contract_last, preferred_element_type=f32)


def dot_first(a, b):
    return lax.dot_general(a, b, contract_first, preferred_element_type=f32)


def swap(value, axis, bit):
    size = lax.axis_size(axis)
    return lax.ppermute(value, axis, [(i, i ^ bit) for i in range(size)])


def swap_core(value):
    return swap(value, "tok", 1)


def swap_x(value):
    return swap(value, "tok", 2)


def swap_y(value):
    return swap(value, "vocab", 1)


def swap_z(value, step):
    return swap(value, "vocab", 2 * step)


in_vmem = pl.BlockSpec(memory_space=pltpu.VMEM)


def copy_blocks(shapes, moves, *arrays, source=pltpu.HBM):
    def kernel(*refs):
        ins, outs, sems = refs[: len(arrays)], refs[len(arrays) : -1], refs[-1]
        copies = []
        for n, (origin, columns, target, row, column) in enumerate(moves()):
            src, dst = ins[origin], outs[target]
            if columns is not None:
                src = src.at[:, pl.ds(pl.multiple_of(columns[0], 128), columns[1])]
            dst = dst.at[pl.ds(row, src.shape[0]), pl.ds(column, src.shape[1])]
            copies.append(pltpu.make_async_copy(src, dst, sems.at[n]))
        for copy in copies:
            copy.start()
        for copy in copies:
            copy.wait()

    size = sum(2 * shape[0] * shape[1] for shape in shapes)
    return pl.pallas_call(
        kernel,
        out_shape=[jax.ShapeDtypeStruct(shape, bf16) for shape in shapes],
        in_specs=[pl.BlockSpec(memory_space=source)] * len(arrays),
        out_specs=[in_vmem] * len(shapes),
        scratch_shapes=[pltpu.SemaphoreType.DMA((32,))],
        compiler_params=pltpu.CompilerParams(vmem_limit_bytes=12 << 20),
        cost_estimate=pl.CostEstimate(flops=0, bytes_accessed=2 * size, transcendentals=0),
    )(*arrays)


def logits_of(groups, tokens, rider=None, first=0, before=None):
    toks, width = tokens[0].shape
    heights = [group[0].shape[0] for group in groups]
    total, depth = sum(heights), width * len(tokens)
    blocks = range(first, first + len(tokens))
    flat = [a for group in groups for a in group]
    riders = [a for a in (before, rider) if a is not None]
    extra = 0 if rider is None else rider.shape[0] // 2
    n_flat, n_all = len(flat), len(flat) + len(tokens) + len(riders)

    def kernel(*refs):
        out = refs[n_all]
        at, row = 0, 0
        for group, height in zip(groups, heights):
            result, column = None, 0
            if before is not None:
                result = refs[n_flat + len(tokens)][row : row + height, :]
            for part in group:
                for c in range(0, part.shape[1], width):
                    block = (column + c) // width
                    if block not in blocks:
                        continue
                    token = refs[n_flat + block - first]
                    term = dot_last(refs[at][:, c : c + width], token[...])
                    result = term if result is None else result + term
                at, column = at + 1, column + part.shape[1]
            out[row : row + height, :] = result
            row += height
        if extra:
            wide = refs[n_all - 1][...].astype(f32)
            out[row:, :] = jnp.concatenate([wide[:extra], wide[extra:]], axis=1)

    return pl.pallas_call(
        kernel,
        out_shape=jax.ShapeDtypeStruct((total + extra, toks), f32),
        in_specs=[in_vmem] * n_all,
        out_specs=in_vmem,
        compiler_params=pltpu.CompilerParams(vmem_limit_bytes=12 << 20),
        cost_estimate=pl.CostEstimate(
            flops=2 * total * depth * toks,
            bytes_accessed=2 * (total + toks) * depth + 4 * total * toks,
            transcendentals=0,
        ),
    )(*flat, *tokens, *riders)


def finish(total, pieces, factor, factor_came):
    width = total.shape[1]

    def kernel(total_ref, *refs):
        result = total_ref[...]
        for piece in refs[: len(pieces)]:
            result = result + piece[...].astype(f32)
        factor_ref, came_ref, hidden_out, basis_out, rows_out = refs[len(pieces) :]
        hidden_out[...] = result.astype(bf16)
        both = factor_ref[...] + came_ref[...].astype(f32)
        basis_out[...] = both[:, :width]
        rows_out[...] = both[:, width:]

    rank, wide = factor.shape
    return pl.pallas_call(
        kernel,
        out_shape=[
            jax.ShapeDtypeStruct(total.shape, bf16),
            jax.ShapeDtypeStruct((rank, width), f32),
            jax.ShapeDtypeStruct((rank, wide - width), f32),
        ],
        in_specs=[in_vmem] * (3 + len(pieces)),
        out_specs=[in_vmem] * 3,
        compiler_params=pltpu.CompilerParams(vmem_limit_bytes=4 << 20),
        cost_estimate=pl.CostEstimate(
            flops=3 * total.size, bytes_accessed=12 * total.size, transcendentals=0
        ),
    )(total, *pieces, factor, factor_came)


def on_few(hidden, head, factor_rows, factor_basis, targets, loss_mask):
    n_vocab, n_tok = lax.axis_size("vocab"), lax.axis_size("tok")
    n_z = n_vocab // 2
    bits = [1 << b for b in range(n_z.bit_length() - 1)]
    v = lax.axis_index("vocab")
    t = lax.axis_index("tok")
    toks, width = hidden.shape
    rows = head.shape[0]
    new_here = factor_rows.shape[0]
    rank = factor_basis.shape[0]
    depth = n_z * width

    near_first = v * (n_tok * rows) + (t >> 1) * (2 * rows)
    far_first = (v ^ 1) * (n_tok * rows) + (t >> 1) * (2 * rows)
    turn = (t & 1) * rows
    new_first = v * new_here
    hidden, head, near_first, far_first, turn, new_first = lax.optimization_barrier(
        (hidden, head, near_first, far_first, turn, new_first)
    )

    def start_of(j, other):
        return (lax.axis_index("vocab") ^ (2 * j + other)) * width

    cuts = [0, n_z]
    chunks = [range(a, b) for a, b in zip(cuts, cuts[1:]) if a < b]
    sends = copy_blocks(
        [(rows, len(chunk) * width) for chunk in chunks],
        lambda: [
            (0, (start_of(j, 1), width), n, 0, (j - chunk[0]) * width)
            for n, chunk in enumerate(chunks)
            for j in chunk
        ],
        head,
    )
    beside = [swap_y(send) for send in sends]

    def half(array, after):
        array, _ = lax.optimization_barrier((array, after))
        moves = lambda: [(0, (start_of(j, 0), width), 0, 0, j * width) for j in range(n_z)]
        return copy_blocks([(array.shape[0], depth)], moves, array)[0]

    after, _ = lax.optimization_barrier((hidden, sends[0]))
    shards, cross = {0: hidden}, {0: swap_x(hidden)}
    for bit in reversed(bits):
        near = swap_z(hidden if bit == 1 else hidden, bit)
        for j in [j for j in shards if j]:
            shards[j], *_ = lax.optimization_barrier((shards[j], near))
            shards[j ^ bit] = swap_z(shards[j], bit)
        shards[bit] = near
    for j in range(1, n_z):
        sent = shards[j]
        waits = [] if j == 1 else [cross[j - 2]] if j < n_z - 1 else [cross[j - 2], beside[0]]
        if waits:
            sent, *_ = lax.optimization_barrier((sent, *waits))
        cross[j] = swap_x(sent)
    kept = half(head, cross[1])
    kept_core = swap_core(kept)
    basis_half = half(factor_basis, cross[0])

    beside_core = []
    for n, came in enumerate(beside):
        came, *_ = lax.optimization_barrier((came, cross[n_z - 2], shards[n_z - 1]))
        beside_core.append(swap_core(came))

    in_order = lambda parts: [parts[j] for j in range(n_z)]
    basis_ready, *_ = lax.optimization_barrier((basis_half, cross[1]))
    upper = [[kept], [kept_core], [basis_ready]]
    upper_own = logits_of(upper, in_order(shards))
    beside_core[-1], *_ = lax.optimization_barrier((beside_core[-1], upper_own))
    lower_own = logits_of([beside, beside_core], in_order(shards))
    cross[0], _ = lax.optimization_barrier((cross[0], lower_own))
    every = upper + [beside, beside_core]
    early_cross = logits_of(every, in_order(cross)[:-1]) if n_z > 1 else None
    both_cross = logits_of(every, in_order(cross)[-1:], factor_rows, n_z - 1, early_cross)
    n_up = 2 * rows + rank

    def add_over_y(up, low, up_came, low_came):
        near = up[: 2 * rows] + low_came
        far = low + up_came[: 2 * rows]
        return near, far, (up[2 * rows :] + up_came[2 * rows :]).astype(bf16)

    upper_came, lower_came = swap_y(upper_own), swap_y(lower_own)
    cross_came = swap_y(both_cross)
    upper_came, _ = lax.optimization_barrier((upper_came, both_cross))
    near_own, far_own, basis_own = add_over_y(upper_own, lower_own, upper_came, lower_came)
    near_cross, far_cross, basis_cross = add_over_y(
        both_cross[:n_up], both_cross[n_up : n_up + 2 * rows], cross_came[:n_up], cross_came[n_up : n_up + 2 * rows]
    )
    hidden_basis = jnp.concatenate([basis_own, basis_cross], axis=1)

    n_rows = n_up + 2 * rows
    rows_came = cross_came[n_rows:].astype(bf16)
    rows_pair = jnp.concatenate([factor_rows, rows_came[:, :rank], rows_came[:, rank:]], axis=0)

    def merge(a, b):
        top = jnp.maximum(a[0], b[0])
        return jnp.stack([top, a[1] * jnp.exp(a[0] - top) + b[1] * jnp.exp(b[0] - top)])

    def local(*logits):
        top = jnp.max(logits[0], axis=0)
        for l in logits[1:]:
            top = jnp.maximum(top, jnp.max(l, axis=0))
        total = jnp.sum(jnp.exp(logits[0] - top[None, :]), axis=0)
        for l in logits[1:]:
            total = total + jnp.sum(jnp.exp(l - top[None, :]), axis=0)
        return jnp.stack([top, total])

    info = jnp.stack([targets.astype(f32), loss_mask.astype(f32)])
    stats = jnp.concatenate([local(near_own, far_own), local(near_cross, far_cross)], axis=1)
    sent = jnp.concatenate([stats, jnp.concatenate([info, info], axis=1)], axis=0)
    came = swap_x(sent)
    stats = merge(stats, jnp.concatenate([came[:2, toks:], came[:2, :toks]], axis=1))
    info = jnp.concatenate([info, came[2:, :toks]], axis=1)
    target_row = info[0].astype(jnp.int32)
    weight_row = loss_scale * info[1]
    fresh = lax.dot_general(
        rows_pair, hidden_basis, (((1,), (0,)), ((), ())), preferred_element_type=f32
    )
    stats = merge(stats, local(fresh))
    for bit in bits:
        stats = merge(stats, swap_z(stats, bit))
    row_top, sum_exp = stats[0], stats[1]
    scale_row = weight_row / sum_exp

    def grad_of(frozen, first, cols):
        row_ids = (lax.broadcasted_iota(jnp.int32, frozen.shape, 0) ^ turn) + first
        hit = jnp.where(row_ids == target_row[None, cols], weight_row[None, cols], 0.0)
        return (jnp.exp(frozen - row_top[None, cols]) * scale_row[None, cols] - hit).astype(bf16)

    at_own, at_cross = slice(0, toks), slice(toks, 2 * toks)
    grad_cross = (grad_of(near_cross, near_first, at_cross), grad_of(far_cross, far_first, at_cross))
    grad_own = (grad_of(near_own, near_first, at_own), grad_of(far_own, far_first, at_own))

    laid = [kept, kept_core] + beside + beside_core
    laid[0], _ = lax.optimization_barrier((kept, both_cross))
    places, row = [], 0
    for group in ([kept], [kept_core], beside, beside_core):
        column = 0
        for array in group:
            places.append((len(places), None, 0, row, column))
            column += array.shape[1]
        row += rows
    (weights,) = copy_blocks([(4 * rows, depth)], lambda: places, *laid, source=pltpu.VMEM)

    def part(grads, j):
        return dot_first(grads, weights[:, j * width : (j + 1) * width])

    grad_cross = jnp.concatenate(grad_cross, axis=0)
    grad_own = jnp.concatenate(grad_own, axis=0)
    sums, from_x, first_z = {}, {}, None
    for j in reversed(range(n_z)):
        send = part(grad_cross, j).astype(bf16)
        if j + 2 in from_x:
            waits = (from_x[j + 2], first_came) if j == 0 else (first_z, first_z)
            send, *_ = lax.optimization_barrier((send, *waits))
        if j == n_z - 2:
            send, _ = lax.optimization_barrier((send, first_send))
        first_send = send if j == n_z - 1 else first_send
        from_x[j] = swap_x(send)
        sums[j] = part(grad_own, j) + from_x[j].astype(f32)
        if first_z is None:
            first_z = sums[j].astype(bf16)
            first_came = swap_z(first_z, bits[0]) if bits else first_z
    fresh, _ = lax.optimization_barrier((fresh, first_z))
    fresh_ids = lax.broadcasted_iota(jnp.int32, (2 * new_here, toks), 0) ^ new_first
    fresh_ids = fresh_ids + rows * n_tok * n_vocab
    fresh_hit = jnp.where(fresh_ids == targets[None, :], weight_row[None, :toks], 0.0)
    fresh_grad = (
        jnp.exp(fresh[:, :toks] - row_top[None, :toks]) * scale_row[None, :toks] - fresh_hit
    ).astype(bf16)
    mix_total = dot_first(rows_pair, fresh_grad)
    for bit in bits:
        if bit > 1:
            mix_total, *_ = lax.optimization_barrier((mix_total, first_came))
        mix_total = mix_total + swap_z(mix_total, bit)
    mix_total = mix_total.astype(bf16)
    rows_part = dot_last(fresh_grad[:new_here], hidden_basis[:, :toks])
    basis_part = jnp.dot(mix_total, hidden, preferred_element_type=f32)

    came_z, pieces = None, []
    for bit in bits:
        for j in [j for j in sorted(sums, reverse=True) if j & bit]:
            total = sums.pop(j)
            send = first_z if j == n_z - 1 else total.astype(bf16)
            if bit == bits[0] and came_z is not None:
                send, _ = lax.optimization_barrier((send, came_z))
            came = first_came if j == n_z - 1 else swap_z(send, bit)
            came_z = came if came_z is None else came_z
            if j ^ bit or bit != bits[-1]:
                sums[j ^ bit] = sums[j ^ bit] + came.astype(f32)
            else:
                pieces.append(came)
    total = sums[0] + dot_first(mix_total, basis_half[:, :width])

    factor_part = jnp.concatenate([basis_part, rows_part], axis=1)
    factor_two = lax.reduce_precision(factor_part + swap_core(factor_part), 8, 7)
    factor_two, _ = lax.optimization_barrier((factor_two, from_x[min(1, n_z - 1)]))
    factor_came = swap_x(factor_two.astype(bf16))
    hidden_grad, basis_grad, rows_grad = finish(total, pieces, factor_two, factor_came)
    return hidden_grad, rows_grad, basis_grad


def on_many(hidden, head, factor_rows, factor_basis, targets, loss_mask):
    n_vocab = lax.axis_size("vocab")
    n_tok = lax.axis_size("tok")
    vocab_index = lax.axis_index("vocab")
    rows_here = head.shape[0] * n_tok
    new_here = factor_rows.shape[0]
    width_here = hidden.shape[1]
    gathered = lax.all_gather(hidden, "vocab", axis=1, tiled=True)
    head_full = lax.all_gather(head, "tok", axis=0, tiled=True)
    frozen = dot_last(gathered, head_full)
    hidden_basis = dot_last(gathered, factor_basis).astype(bf16)
    fresh_logits = dot_last(hidden_basis, factor_rows)
    local_max = jnp.maximum(jnp.max(frozen, axis=1), jnp.max(fresh_logits, axis=1))
    row_top = lax.pmax(local_max, "vocab")
    local_sum = jnp.sum(jnp.exp(frozen - row_top[:, None]), axis=1) + jnp.sum(
        jnp.exp(fresh_logits - row_top[:, None]), axis=1
    )
    sum_exp = lax.psum(local_sum, "vocab")
    frozen_prob = jnp.exp(frozen - row_top[:, None]) / sum_exp[:, None]
    fresh_prob = jnp.exp(fresh_logits - row_top[:, None]) / sum_exp[:, None]
    frozen_offset = targets - vocab_index * rows_here
    fresh_offset = targets - rows_here * n_vocab - vocab_index * new_here
    frozen_hit = (
        lax.broadcasted_iota(jnp.int32, frozen.shape, 1) == frozen_offset[:, None]
    ).astype(f32)
    fresh_hit = (
        lax.broadcasted_iota(jnp.int32, fresh_logits.shape, 1) == fresh_offset[:, None]
    ).astype(f32)
    weight_row = loss_scale * loss_mask.astype(f32)[:, None]
    frozen_grad = (weight_row * (frozen_prob - frozen_hit)).astype(bf16)
    fresh_grad = (weight_row * (fresh_prob - fresh_hit)).astype(bf16)
    mix_term = jnp.dot(fresh_grad, factor_rows, preferred_element_type=f32)
    mix_total = lax.psum(mix_term, "vocab").astype(bf16)
    grad_part = lax.psum_scatter(
        lax.dot_general(
            head_full, frozen_grad, (((0,), (1,)), ((), ())), preferred_element_type=f32
        ),
        "vocab",
        scatter_dimension=0,
        tiled=True,
    )
    basis_cols = lax.dynamic_slice_in_dim(factor_basis, vocab_index * width_here, width_here, 1)
    hidden_grad = (
        grad_part.T + jnp.dot(mix_total, basis_cols, preferred_element_type=f32)
    ).astype(bf16)
    rows_term = dot_first(fresh_grad, hidden_basis)
    basis_term = dot_first(mix_total, hidden)
    rows_grad, basis_grad = (
        lax.psum(rows_term.astype(bf16), "tok").astype(f32),
        lax.psum(basis_term.astype(bf16), "tok").astype(f32),
    )
    return hidden_grad, rows_grad, basis_grad


def solution(mesh):
    in_specs = (
        P("tok", "vocab"),
        P(("vocab", "tok"), None),
        P("vocab", None),
        P(),
        P("tok"),
        P("tok"),
    )
    out_specs = (P("tok", "vocab"), P("vocab", None), P(None, "vocab"))

    def on_device(hidden, head, factor_rows, *rest):
        even = [n & (n - 1) == 0 for n in (mesh.shape["vocab"], head.shape[0], factor_rows.shape[0])]
        few = 2 <= mesh.shape["vocab"] <= 16 and mesh.shape["tok"] == 4 and all(even)
        few = few and hidden.shape[0] == 2 * factor_rows.shape[1]
        return (on_few if few else on_many)(hidden, head, factor_rows, *rest)

    return jax.shard_map(
        on_device, mesh=mesh, in_specs=in_specs, out_specs=out_specs, check_vma=False
    )
```

```python
import jax
import jax.numpy as jnp
from jax import lax
from jax.experimental import pallas as pl
from jax.experimental.pallas import tpu as pltpu
from jax.sharding import PartitionSpec as P

loss_scale = 64.0
f32 = jnp.float32
bf16 = jnp.bfloat16
contract_last = (((1,), (1,)), ((), ()))
contract_first = (((0,), (0,)), ((), ()))


def dot_last(a, b):
    return lax.dot_general(a, b, contract_last, preferred_element_type=f32)


def dot_first(a, b):
    return lax.dot_general(a, b, contract_first, preferred_element_type=f32)


def swap(value, axis, bit):
    size = lax.axis_size(axis)
    return lax.ppermute(value, axis, [(i, i ^ bit) for i in range(size)])


def swap_core(value):
    return swap(value, "tok", 1)


def swap_x(value):
    return swap(value, "tok", 2)


def swap_y(value):
    return swap(value, "vocab", 1)


def swap_z(value, step):
    return swap(value, "vocab", 2 * step)


in_vmem = pl.BlockSpec(memory_space=pltpu.VMEM)


def copy_blocks(shapes, moves, *arrays, source=pltpu.HBM):
    def kernel(*refs):
        ins, outs, sems = refs[: len(arrays)], refs[len(arrays) : -1], refs[-1]
        copies = []
        for n, (origin, columns, target, row, column) in enumerate(moves()):
            src, dst = ins[origin], outs[target]
            if columns is not None:
                src = src.at[:, pl.ds(pl.multiple_of(columns[0], 128), columns[1])]
            dst = dst.at[pl.ds(row, src.shape[0]), pl.ds(column, src.shape[1])]
            copies.append(pltpu.make_async_copy(src, dst, sems.at[n]))
        for copy in copies:
            copy.start()
        for copy in copies:
            copy.wait()

    size = sum(2 * shape[0] * shape[1] for shape in shapes)
    return pl.pallas_call(
        kernel,
        out_shape=[jax.ShapeDtypeStruct(shape, bf16) for shape in shapes],
        in_specs=[pl.BlockSpec(memory_space=source)] * len(arrays),
        out_specs=[in_vmem] * len(shapes),
        scratch_shapes=[pltpu.SemaphoreType.DMA((32,))],
        compiler_params=pltpu.CompilerParams(vmem_limit_bytes=12 << 20),
        cost_estimate=pl.CostEstimate(flops=0, bytes_accessed=2 * size, transcendentals=0),
    )(*arrays)


def logits_of(groups, tokens, rider=None, first=0, before=None):
    toks, width = tokens[0].shape
    heights = [group[0].shape[0] for group in groups]
    total, depth = sum(heights), width * len(tokens)
    blocks = range(first, first + len(tokens))
    flat = [a for group in groups for a in group]
    riders = [a for a in (before, rider) if a is not None]
    extra = 0 if rider is None else rider.shape[0] // 2
    n_flat, n_all = len(flat), len(flat) + len(tokens) + len(riders)

    def kernel(*refs):
        out = refs[n_all]
        at, row = 0, 0
        for group, height in zip(groups, heights):
            result, column = None, 0
            if before is not None:
                result = refs[n_flat + len(tokens)][row : row + height, :]
            for part in group:
                for c in range(0, part.shape[1], width):
                    block = (column + c) // width
                    if block not in blocks:
                        continue
                    token = refs[n_flat + block - first]
                    term = dot_last(refs[at][:, c : c + width], token[...])
                    result = term if result is None else result + term
                at, column = at + 1, column + part.shape[1]
            out[row : row + height, :] = result
            row += height
        if extra:
            wide = refs[n_all - 1][...].astype(f32)
            out[row:, :] = jnp.concatenate([wide[:extra], wide[extra:]], axis=1)

    return pl.pallas_call(
        kernel,
        out_shape=jax.ShapeDtypeStruct((total + extra, toks), f32),
        in_specs=[in_vmem] * n_all,
        out_specs=in_vmem,
        compiler_params=pltpu.CompilerParams(vmem_limit_bytes=12 << 20),
        cost_estimate=pl.CostEstimate(
            flops=2 * total * depth * toks,
            bytes_accessed=2 * (total + toks) * depth + 4 * total * toks,
            transcendentals=0,
        ),
    )(*flat, *tokens, *riders)


def finish(total, pieces, factor, factor_came):
    width = total.shape[1]

    def kernel(total_ref, *refs):
        result = total_ref[...]
        for piece in refs[: len(pieces)]:
            result = result + piece[...].astype(f32)
        factor_ref, came_ref, hidden_out, basis_out, rows_out = refs[len(pieces) :]
        hidden_out[...] = result.astype(bf16)
        both = factor_ref[...] + came_ref[...].astype(f32)
        basis_out[...] = both[:, :width]
        rows_out[...] = both[:, width:]

    rank, wide = factor.shape
    return pl.pallas_call(
        kernel,
        out_shape=[
            jax.ShapeDtypeStruct(total.shape, bf16),
            jax.ShapeDtypeStruct((rank, width), f32),
            jax.ShapeDtypeStruct((rank, wide - width), f32),
        ],
        in_specs=[in_vmem] * (3 + len(pieces)),
        out_specs=[in_vmem] * 3,
        compiler_params=pltpu.CompilerParams(vmem_limit_bytes=4 << 20),
        cost_estimate=pl.CostEstimate(
            flops=3 * total.size, bytes_accessed=12 * total.size, transcendentals=0
        ),
    )(total, *pieces, factor, factor_came)


def on_few(hidden, head, factor_rows, factor_basis, targets, loss_mask):
    n_vocab, n_tok = lax.axis_size("vocab"), lax.axis_size("tok")
    n_z = n_vocab // 2
    bits = [1 << b for b in range(n_z.bit_length() - 1)]
    v = lax.axis_index("vocab")
    t = lax.axis_index("tok")
    toks, width = hidden.shape
    rows = head.shape[0]
    new_here = factor_rows.shape[0]
    rank = factor_basis.shape[0]
    depth = n_z * width

    near_first = v * (n_tok * rows) + (t >> 1) * (2 * rows)
    far_first = (v ^ 1) * (n_tok * rows) + (t >> 1) * (2 * rows)
    turn = (t & 1) * rows
    new_first = v * new_here
    hidden, head, near_first, far_first, turn, new_first = lax.optimization_barrier(
        (hidden, head, near_first, far_first, turn, new_first)
    )

    def start_of(j, other):
        return (lax.axis_index("vocab") ^ (2 * j + other)) * width

    cuts = [0, n_z]
    chunks = [range(a, b) for a, b in zip(cuts, cuts[1:]) if a < b]
    sends = copy_blocks(
        [(rows, len(chunk) * width) for chunk in chunks],
        lambda: [
            (0, (start_of(j, 1), width), n, 0, (j - chunk[0]) * width)
            for n, chunk in enumerate(chunks)
            for j in chunk
        ],
        head,
    )
    beside = [swap_y(send) for send in sends]

    def half(array, after):
        array, _ = lax.optimization_barrier((array, after))
        moves = lambda: [(0, (start_of(j, 0), width), 0, 0, j * width) for j in range(n_z)]
        return copy_blocks([(array.shape[0], depth)], moves, array)[0]

    after, _ = lax.optimization_barrier((hidden, sends[0]))
    shards, cross = {0: hidden}, {0: swap_x(after)}
    for bit in reversed(bits):
        near = swap_z(hidden if bit == 1 else hidden, bit)
        for j in [j for j in shards if j]:
            shards[j], *_ = lax.optimization_barrier((shards[j], near))
            shards[j ^ bit] = swap_z(shards[j], bit)
        shards[bit] = near
    for j in range(1, n_z):
        sent = shards[j]
        waits = [] if j == 1 else [cross[j - 2]] if j < n_z - 1 else [cross[j - 2]]
        if waits:
            sent, *_ = lax.optimization_barrier((sent, *waits))
        cross[j] = swap_x(sent)
    kept = half(head, cross[1])
    kept_core = swap_core(kept)
    basis_half = half(factor_basis, cross[0])

    beside_core = []
    for n, came in enumerate(beside):
        came, *_ = lax.optimization_barrier((came, cross[1], cross[n_z - 2], shards[n_z - 1]))
        beside_core.append(swap_core(came))

    in_order = lambda parts: [parts[j] for j in range(n_z)]
    basis_ready, *_ = lax.optimization_barrier((basis_half, cross[n_z - 2], shards[n_z - 1]))
    upper = [[kept], [kept_core], [basis_ready]]
    upper_own = logits_of(upper, in_order(shards))
    beside_core[-1], *_ = lax.optimization_barrier((beside_core[-1], upper_own))
    lower_own = logits_of([beside, beside_core], in_order(shards))
    cross[0], _ = lax.optimization_barrier((cross[0], lower_own))
    every = upper + [beside, beside_core]
    early_cross = logits_of(every, in_order(cross)[:-1]) if n_z > 1 else None
    both_cross = logits_of(every, in_order(cross)[-1:], factor_rows, n_z - 1, early_cross)
    n_up = 2 * rows + rank

    def add_over_y(up, low, up_came, low_came):
        near = up[: 2 * rows] + low_came
        far = low + up_came[: 2 * rows]
        return near, far, (up[2 * rows :] + up_came[2 * rows :]).astype(bf16)

    upper_came, lower_came = swap_y(upper_own), swap_y(lower_own)
    cross_came = swap_y(both_cross)
    upper_came, _ = lax.optimization_barrier((upper_came, both_cross))
    near_own, far_own, basis_own = add_over_y(upper_own, lower_own, upper_came, lower_came)
    near_cross, far_cross, basis_cross = add_over_y(
        both_cross[:n_up], both_cross[n_up : n_up + 2 * rows], cross_came[:n_up], cross_came[n_up : n_up + 2 * rows]
    )
    hidden_basis = jnp.concatenate([basis_own, basis_cross], axis=1)

    n_rows = n_up + 2 * rows
    rows_came = cross_came[n_rows:].astype(bf16)
    rows_pair = jnp.concatenate([factor_rows, rows_came[:, :rank], rows_came[:, rank:]], axis=0)

    def merge(a, b):
        top = jnp.maximum(a[0], b[0])
        return jnp.stack([top, a[1] * jnp.exp(a[0] - top) + b[1] * jnp.exp(b[0] - top)])

    def local(*logits):
        top = jnp.max(logits[0], axis=0)
        for l in logits[1:]:
            top = jnp.maximum(top, jnp.max(l, axis=0))
        total = jnp.sum(jnp.exp(logits[0] - top[None, :]), axis=0)
        for l in logits[1:]:
            total = total + jnp.sum(jnp.exp(l - top[None, :]), axis=0)
        return jnp.stack([top, total])

    info = jnp.stack([targets.astype(f32), loss_mask.astype(f32)])
    stats = jnp.concatenate([local(near_own, far_own), local(near_cross, far_cross)], axis=1)
    sent = jnp.concatenate([stats, jnp.concatenate([info, info], axis=1)], axis=0)
    came = swap_x(sent)
    stats = merge(stats, jnp.concatenate([came[:2, toks:], came[:2, :toks]], axis=1))
    info = jnp.concatenate([info, came[2:, :toks]], axis=1)
    target_row = info[0].astype(jnp.int32)
    weight_row = loss_scale * info[1]
    fresh = lax.dot_general(
        rows_pair, hidden_basis, (((1,), (0,)), ((), ())), preferred_element_type=f32
    )
    stats = merge(stats, local(fresh))
    for bit in bits:
        stats = merge(stats, swap_z(stats, bit))
    row_top, sum_exp = stats[0], stats[1]
    scale_row = weight_row / sum_exp

    def grad_of(frozen, first, cols):
        row_ids = (lax.broadcasted_iota(jnp.int32, frozen.shape, 0) ^ turn) + first
        hit = jnp.where(row_ids == target_row[None, cols], weight_row[None, cols], 0.0)
        return (jnp.exp(frozen - row_top[None, cols]) * scale_row[None, cols] - hit).astype(bf16)

    at_own, at_cross = slice(0, toks), slice(toks, 2 * toks)
    grad_cross = (grad_of(near_cross, near_first, at_cross), grad_of(far_cross, far_first, at_cross))
    grad_own = (grad_of(near_own, near_first, at_own), grad_of(far_own, far_first, at_own))

    laid = [kept, kept_core] + beside + beside_core
    laid[0], _ = lax.optimization_barrier((kept, both_cross))
    places, row = [], 0
    for group in ([kept], [kept_core], beside, beside_core):
        column = 0
        for array in group:
            places.append((len(places), None, 0, row, column))
            column += array.shape[1]
        row += rows
    (weights,) = copy_blocks([(4 * rows, depth)], lambda: places, *laid, source=pltpu.VMEM)

    def part(grads, j):
        return dot_first(grads, weights[:, j * width : (j + 1) * width])

    grad_cross = jnp.concatenate(grad_cross, axis=0)
    grad_own = jnp.concatenate(grad_own, axis=0)
    sums, from_x, first_z = {}, {}, None
    for j in reversed(range(n_z)):
        send = part(grad_cross, j).astype(bf16)
        if j + 2 in from_x:
            waits = (from_x[j + 2], first_came) if j == 0 else (first_z, first_z)
            send, *_ = lax.optimization_barrier((send, *waits))
        if j == n_z - 2:
            send, _ = lax.optimization_barrier((send, first_send))
        first_send = send if j == n_z - 1 else first_send
        from_x[j] = swap_x(send)
        sums[j] = part(grad_own, j) + from_x[j].astype(f32)
        if first_z is None:
            first_z = sums[j].astype(bf16)
            first_came = swap_z(first_z, bits[0]) if bits else first_z
    fresh, _ = lax.optimization_barrier((fresh, first_z))
    fresh_ids = lax.broadcasted_iota(jnp.int32, (2 * new_here, toks), 0) ^ new_first
    fresh_ids = fresh_ids + rows * n_tok * n_vocab
    fresh_hit = jnp.where(fresh_ids == targets[None, :], weight_row[None, :toks], 0.0)
    fresh_grad = (
        jnp.exp(fresh[:, :toks] - row_top[None, :toks]) * scale_row[None, :toks] - fresh_hit
    ).astype(bf16)
    mix_total = dot_first(rows_pair, fresh_grad)
    for bit in bits:
        if bit > 1:
            mix_total, *_ = lax.optimization_barrier((mix_total, first_came))
        mix_total = mix_total + swap_z(mix_total, bit)
    mix_total = mix_total.astype(bf16)
    rows_part = dot_last(fresh_grad[:new_here], hidden_basis[:, :toks])
    basis_part = jnp.dot(mix_total, hidden, preferred_element_type=f32)

    came_z, pieces = None, []
    for bit in bits:
        for j in [j for j in sorted(sums, reverse=True) if j & bit]:
            total = sums.pop(j)
            send = first_z if j == n_z - 1 else total.astype(bf16)
            if bit == bits[0] and came_z is not None:
                send, _ = lax.optimization_barrier((send, came_z))
            came = first_came if j == n_z - 1 else swap_z(send, bit)
            came_z = came if came_z is None else came_z
            if j ^ bit or bit != bits[-1]:
                sums[j ^ bit] = sums[j ^ bit] + came.astype(f32)
            else:
                pieces.append(came)
    total = sums[0] + dot_first(mix_total, basis_half[:, :width])

    factor_part = jnp.concatenate([basis_part, rows_part], axis=1)
    factor_two = lax.reduce_precision(factor_part + swap_core(factor_part), 8, 7)
    factor_two, _ = lax.optimization_barrier((factor_two, from_x[min(1, n_z - 1)]))
    factor_came = swap_x(factor_two.astype(bf16))
    hidden_grad, basis_grad, rows_grad = finish(total, pieces, factor_two, factor_came)
    return hidden_grad, rows_grad, basis_grad


def on_many(hidden, head, factor_rows, factor_basis, targets, loss_mask):
    n_vocab = lax.axis_size("vocab")
    n_tok = lax.axis_size("tok")
    vocab_index = lax.axis_index("vocab")
    rows_here = head.shape[0] * n_tok
    new_here = factor_rows.shape[0]
    width_here = hidden.shape[1]
    gathered = lax.all_gather(hidden, "vocab", axis=1, tiled=True)
    head_full = lax.all_gather(head, "tok", axis=0, tiled=True)
    frozen = dot_last(gathered, head_full)
    hidden_basis = dot_last(gathered, factor_basis).astype(bf16)
    fresh_logits = dot_last(hidden_basis, factor_rows)
    local_max = jnp.maximum(jnp.max(frozen, axis=1), jnp.max(fresh_logits, axis=1))
    row_top = lax.pmax(local_max, "vocab")
    local_sum = jnp.sum(jnp.exp(frozen - row_top[:, None]), axis=1) + jnp.sum(
        jnp.exp(fresh_logits - row_top[:, None]), axis=1
    )
    sum_exp = lax.psum(local_sum, "vocab")
    frozen_prob = jnp.exp(frozen - row_top[:, None]) / sum_exp[:, None]
    fresh_prob = jnp.exp(fresh_logits - row_top[:, None]) / sum_exp[:, None]
    frozen_offset = targets - vocab_index * rows_here
    fresh_offset = targets - rows_here * n_vocab - vocab_index * new_here
    frozen_hit = (
        lax.broadcasted_iota(jnp.int32, frozen.shape, 1) == frozen_offset[:, None]
    ).astype(f32)
    fresh_hit = (
        lax.broadcasted_iota(jnp.int32, fresh_logits.shape, 1) == fresh_offset[:, None]
    ).astype(f32)
    weight_row = loss_scale * loss_mask.astype(f32)[:, None]
    frozen_grad = (weight_row * (frozen_prob - frozen_hit)).astype(bf16)
    fresh_grad = (weight_row * (fresh_prob - fresh_hit)).astype(bf16)
    mix_term = jnp.dot(fresh_grad, factor_rows, preferred_element_type=f32)
    mix_total = lax.psum(mix_term, "vocab").astype(bf16)
    grad_part = lax.psum_scatter(
        lax.dot_general(
            head_full, frozen_grad, (((0,), (1,)), ((), ())), preferred_element_type=f32
        ),
        "vocab",
        scatter_dimension=0,
        tiled=True,
    )
    basis_cols = lax.dynamic_slice_in_dim(factor_basis, vocab_index * width_here, width_here, 1)
    hidden_grad = (
        grad_part.T + jnp.dot(mix_total, basis_cols, preferred_element_type=f32)
    ).astype(bf16)
    rows_term = dot_first(fresh_grad, hidden_basis)
    basis_term = dot_first(mix_total, hidden)
    rows_grad, basis_grad = (
        lax.psum(rows_term.astype(bf16), "tok").astype(f32),
        lax.psum(basis_term.astype(bf16), "tok").astype(f32),
    )
    return hidden_grad, rows_grad, basis_grad


def solution(mesh):
    in_specs = (
        P("tok", "vocab"),
        P(("vocab", "tok"), None),
        P("vocab", None),
        P(),
        P("tok"),
        P("tok"),
    )
    out_specs = (P("tok", "vocab"), P("vocab", None), P(None, "vocab"))

    def on_device(hidden, head, factor_rows, *rest):
        even = [n & (n - 1) == 0 for n in (mesh.shape["vocab"], head.shape[0], factor_rows.shape[0])]
        few = 2 <= mesh.shape["vocab"] <= 16 and mesh.shape["tok"] == 4 and all(even)
        few = few and hidden.shape[0] == 2 * factor_rows.shape[1]
        return (on_few if few else on_many)(hidden, head, factor_rows, *rest)

    return jax.shard_map(
        on_device, mesh=mesh, in_specs=in_specs, out_specs=out_specs, check_vma=False
    )
```

```python
import jax
import jax.numpy as jnp
from jax import lax
from jax.experimental import pallas as pl
from jax.experimental.pallas import tpu as pltpu
from jax.sharding import PartitionSpec as P

loss_scale = 64.0
f32 = jnp.float32
bf16 = jnp.bfloat16
contract_last = (((1,), (1,)), ((), ()))
contract_first = (((0,), (0,)), ((), ()))


def dot_last(a, b):
    return lax.dot_general(a, b, contract_last, preferred_element_type=f32)


def dot_first(a, b):
    return lax.dot_general(a, b, contract_first, preferred_element_type=f32)


def swap(value, axis, bit):
    size = lax.axis_size(axis)
    return lax.ppermute(value, axis, [(i, i ^ bit) for i in range(size)])


def swap_core(value):
    return swap(value, "tok", 1)


def swap_x(value):
    return swap(value, "tok", 2)


def swap_y(value):
    return swap(value, "vocab", 1)


def swap_z(value, step):
    return swap(value, "vocab", 2 * step)


in_vmem = pl.BlockSpec(memory_space=pltpu.VMEM)


def copy_blocks(shapes, moves, *arrays, source=pltpu.HBM):
    def kernel(*refs):
        ins, outs, sems = refs[: len(arrays)], refs[len(arrays) : -1], refs[-1]
        copies = []
        for n, (origin, columns, target, row, column) in enumerate(moves()):
            src, dst = ins[origin], outs[target]
            if columns is not None:
                src = src.at[:, pl.ds(pl.multiple_of(columns[0], 128), columns[1])]
            dst = dst.at[pl.ds(row, src.shape[0]), pl.ds(column, src.shape[1])]
            copies.append(pltpu.make_async_copy(src, dst, sems.at[n]))
        for copy in copies:
            copy.start()
        for copy in copies:
            copy.wait()

    size = sum(2 * shape[0] * shape[1] for shape in shapes)
    return pl.pallas_call(
        kernel,
        out_shape=[jax.ShapeDtypeStruct(shape, bf16) for shape in shapes],
        in_specs=[pl.BlockSpec(memory_space=source)] * len(arrays),
        out_specs=[in_vmem] * len(shapes),
        scratch_shapes=[pltpu.SemaphoreType.DMA((32,))],
        compiler_params=pltpu.CompilerParams(vmem_limit_bytes=12 << 20),
        cost_estimate=pl.CostEstimate(flops=0, bytes_accessed=2 * size, transcendentals=0),
    )(*arrays)


def logits_of(groups, tokens, rider=None, first=0, before=None):
    toks, width = tokens[0].shape
    heights = [group[0].shape[0] for group in groups]
    total, depth = sum(heights), width * len(tokens)
    blocks = range(first, first + len(tokens))
    flat = [a for group in groups for a in group]
    riders = [a for a in (before, rider) if a is not None]
    extra = 0 if rider is None else rider.shape[0] // 2
    n_flat, n_all = len(flat), len(flat) + len(tokens) + len(riders)

    def kernel(*refs):
        out = refs[n_all]
        at, row = 0, 0
        for group, height in zip(groups, heights):
            result, column = None, 0
            if before is not None:
                result = refs[n_flat + len(tokens)][row : row + height, :]
            for part in group:
                for c in range(0, part.shape[1], width):
                    block = (column + c) // width
                    if block not in blocks:
                        continue
                    token = refs[n_flat + block - first]
                    term = dot_last(refs[at][:, c : c + width], token[...])
                    result = term if result is None else result + term
                at, column = at + 1, column + part.shape[1]
            out[row : row + height, :] = result
            row += height
        if extra:
            wide = refs[n_all - 1][...].astype(f32)
            out[row:, :] = jnp.concatenate([wide[:extra], wide[extra:]], axis=1)

    return pl.pallas_call(
        kernel,
        out_shape=jax.ShapeDtypeStruct((total + extra, toks), f32),
        in_specs=[in_vmem] * n_all,
        out_specs=in_vmem,
        compiler_params=pltpu.CompilerParams(vmem_limit_bytes=12 << 20),
        cost_estimate=pl.CostEstimate(
            flops=2 * total * depth * toks,
            bytes_accessed=2 * (total + toks) * depth + 4 * total * toks,
            transcendentals=0,
        ),
    )(*flat, *tokens, *riders)


def finish(total, pieces, factor, factor_came):
    width = total.shape[1]

    def kernel(total_ref, *refs):
        result = total_ref[...]
        for piece in refs[: len(pieces)]:
            result = result + piece[...].astype(f32)
        factor_ref, came_ref, hidden_out, basis_out, rows_out = refs[len(pieces) :]
        hidden_out[...] = result.astype(bf16)
        both = factor_ref[...] + came_ref[...].astype(f32)
        basis_out[...] = both[:, :width]
        rows_out[...] = both[:, width:]

    rank, wide = factor.shape
    return pl.pallas_call(
        kernel,
        out_shape=[
            jax.ShapeDtypeStruct(total.shape, bf16),
            jax.ShapeDtypeStruct((rank, width), f32),
            jax.ShapeDtypeStruct((rank, wide - width), f32),
        ],
        in_specs=[in_vmem] * (3 + len(pieces)),
        out_specs=[in_vmem] * 3,
        compiler_params=pltpu.CompilerParams(vmem_limit_bytes=4 << 20),
        cost_estimate=pl.CostEstimate(
            flops=3 * total.size, bytes_accessed=12 * total.size, transcendentals=0
        ),
    )(total, *pieces, factor, factor_came)


def on_few(hidden, head, factor_rows, factor_basis, targets, loss_mask):
    n_vocab, n_tok = lax.axis_size("vocab"), lax.axis_size("tok")
    n_z = n_vocab // 2
    bits = [1 << b for b in range(n_z.bit_length() - 1)]
    v = lax.axis_index("vocab")
    t = lax.axis_index("tok")
    toks, width = hidden.shape
    rows = head.shape[0]
    new_here = factor_rows.shape[0]
    rank = factor_basis.shape[0]
    depth = n_z * width

    near_first = v * (n_tok * rows) + (t >> 1) * (2 * rows)
    far_first = (v ^ 1) * (n_tok * rows) + (t >> 1) * (2 * rows)
    turn = (t & 1) * rows
    new_first = v * new_here
    hidden, head, near_first, far_first, turn, new_first = lax.optimization_barrier(
        (hidden, head, near_first, far_first, turn, new_first)
    )

    def start_of(j, other):
        return (lax.axis_index("vocab") ^ (2 * j + other)) * width

    cuts = [0, n_z]
    chunks = [range(a, b) for a, b in zip(cuts, cuts[1:]) if a < b]
    sends = copy_blocks(
        [(rows, len(chunk) * width) for chunk in chunks],
        lambda: [
            (0, (start_of(j, 1), width), n, 0, (j - chunk[0]) * width)
            for n, chunk in enumerate(chunks)
            for j in chunk
        ],
        head,
    )
    beside = [swap_y(send) for send in sends]

    def half(array, after):
        array, _ = lax.optimization_barrier((array, after))
        moves = lambda: [(0, (start_of(j, 0), width), 0, 0, j * width) for j in range(n_z)]
        return copy_blocks([(array.shape[0], depth)], moves, array)[0]

    after, _ = lax.optimization_barrier((hidden, sends[0]))
    shards, cross = {0: hidden}, {0: swap_x(hidden)}
    for bit in reversed(bits):
        near = swap_z(hidden if bit == 1 else hidden, bit)
        for j in [j for j in shards if j]:
            shards[j], *_ = lax.optimization_barrier((shards[j], near))
            shards[j ^ bit] = swap_z(shards[j], bit)
        shards[bit] = near
    for j in range(1, n_z):
        sent = shards[j]
        waits = [] if j == 1 else [cross[j - 2]] if j < n_z - 1 else [cross[j - 2], beside[0]]
        if waits:
            sent, *_ = lax.optimization_barrier((sent, *waits))
        cross[j] = swap_x(sent)
    kept = half(head, cross[1])
    kept_core = swap_core(kept)
    basis_half = half(factor_basis, cross[0])

    beside_core = []
    for n, came in enumerate(beside):
        came, *_ = lax.optimization_barrier((came, cross[n_z - 2], shards[n_z - 1]))
        beside_core.append(swap_core(came))

    in_order = lambda parts: [parts[j] for j in range(n_z)]
    basis_ready, *_ = lax.optimization_barrier((basis_half, cross[1]))
    upper = [[kept], [kept_core], [basis_ready]]
    upper_own = logits_of(upper, in_order(shards))
    beside_core[-1], *_ = lax.optimization_barrier((beside_core[-1], upper_own))
    lower_own = logits_of([beside, beside_core], in_order(shards))
    cross[0], _ = lax.optimization_barrier((cross[0], lower_own))
    every = upper + [beside, beside_core]
    early_cross = logits_of(every, in_order(cross)[:-1]) if n_z > 1 else None
    both_cross = logits_of(every, in_order(cross)[-1:], factor_rows, n_z - 1, early_cross)
    n_up = 2 * rows + rank

    def add_over_y(up, low, up_came, low_came):
        near = up[: 2 * rows] + low_came
        far = low + up_came[: 2 * rows]
        return near, far, (up[2 * rows :] + up_came[2 * rows :]).astype(bf16)

    upper_came, lower_came = swap_y(upper_own), swap_y(lower_own)
    cross_came = swap_y(both_cross)
    upper_came, _ = lax.optimization_barrier((upper_came, both_cross))
    near_own, far_own, basis_own = add_over_y(upper_own, lower_own, upper_came, lower_came)
    near_cross, far_cross, basis_cross = add_over_y(
        both_cross[:n_up], both_cross[n_up : n_up + 2 * rows], cross_came[:n_up], cross_came[n_up : n_up + 2 * rows]
    )
    hidden_basis = jnp.concatenate([basis_own, basis_cross], axis=1)

    n_rows = n_up + 2 * rows
    rows_came = cross_came[n_rows:].astype(bf16)
    rows_pair = jnp.concatenate([factor_rows, rows_came[:, :rank], rows_came[:, rank:]], axis=0)

    def merge(a, b):
        top = jnp.maximum(a[0], b[0])
        return jnp.stack([top, a[1] * jnp.exp(a[0] - top) + b[1] * jnp.exp(b[0] - top)])

    def local(*logits):
        top = jnp.max(logits[0], axis=0)
        for l in logits[1:]:
            top = jnp.maximum(top, jnp.max(l, axis=0))
        total = jnp.sum(jnp.exp(logits[0] - top[None, :]), axis=0)
        for l in logits[1:]:
            total = total + jnp.sum(jnp.exp(l - top[None, :]), axis=0)
        return jnp.stack([top, total])

    info = jnp.stack([targets.astype(f32), loss_mask.astype(f32)])
    stats = jnp.concatenate([local(near_own, far_own), local(near_cross, far_cross)], axis=1)
    sent = jnp.concatenate([stats, jnp.concatenate([info, info], axis=1)], axis=0)
    came = swap_x(sent)
    stats = merge(stats, jnp.concatenate([came[:2, toks:], came[:2, :toks]], axis=1))
    info = jnp.concatenate([info, came[2:, :toks]], axis=1)
    target_row = info[0].astype(jnp.int32)
    weight_row = loss_scale * info[1]
    fresh = lax.dot_general(
        rows_pair, hidden_basis, (((1,), (0,)), ((), ())), preferred_element_type=f32
    )
    stats = merge(stats, local(fresh))
    for bit in bits:
        stats = merge(stats, swap_z(stats, bit))
    row_top, sum_exp = stats[0], stats[1]
    scale_row = weight_row / sum_exp

    def grad_of(frozen, first, cols):
        row_ids = (lax.broadcasted_iota(jnp.int32, frozen.shape, 0) ^ turn) + first
        hit = jnp.where(row_ids == target_row[None, cols], weight_row[None, cols], 0.0)
        return (jnp.exp(frozen - row_top[None, cols]) * scale_row[None, cols] - hit).astype(bf16)

    at_own, at_cross = slice(0, toks), slice(toks, 2 * toks)
    grad_cross = (grad_of(near_cross, near_first, at_cross), grad_of(far_cross, far_first, at_cross))
    grad_own = (grad_of(near_own, near_first, at_own), grad_of(far_own, far_first, at_own))

    laid = [kept, kept_core] + beside + beside_core
    laid[0], _ = lax.optimization_barrier((kept, both_cross))
    places, row = [], 0
    for group in ([kept], [kept_core], beside, beside_core):
        column = 0
        for array in group:
            places.append((len(places), None, 0, row, column))
            column += array.shape[1]
        row += rows
    (weights,) = copy_blocks([(4 * rows, depth)], lambda: places, *laid, source=pltpu.VMEM)

    def part(grads, j):
        return dot_first(grads, weights[:, j * width : (j + 1) * width])

    grad_cross = jnp.concatenate(grad_cross, axis=0)
    grad_own = jnp.concatenate(grad_own, axis=0)
    sums, from_x, first_z = {}, {}, None
    for j in reversed(range(n_z)):
        send = part(grad_cross, j).astype(bf16)
        if j + 2 in from_x:
            waits = (from_x[j + 2], first_came) if j == 0 else (first_z, first_z)
            send, *_ = lax.optimization_barrier((send, *waits))
        first_send = send if j == n_z - 1 else first_send
        from_x[j] = swap_x(send)
        sums[j] = part(grad_own, j) + from_x[j].astype(f32)
        if first_z is None:
            first_z = sums[j].astype(bf16)
            first_came = swap_z(first_z, bits[0]) if bits else first_z
    fresh, _ = lax.optimization_barrier((fresh, first_z))
    fresh_ids = lax.broadcasted_iota(jnp.int32, (2 * new_here, toks), 0) ^ new_first
    fresh_ids = fresh_ids + rows * n_tok * n_vocab
    fresh_hit = jnp.where(fresh_ids == targets[None, :], weight_row[None, :toks], 0.0)
    fresh_grad = (
        jnp.exp(fresh[:, :toks] - row_top[None, :toks]) * scale_row[None, :toks] - fresh_hit
    ).astype(bf16)
    mix_total = dot_first(rows_pair, fresh_grad)
    for bit in bits:
        if bit > 1:
            mix_total, *_ = lax.optimization_barrier((mix_total, first_came))
        mix_total = mix_total + swap_z(mix_total, bit)
    mix_total = mix_total.astype(bf16)
    rows_part = dot_last(fresh_grad[:new_here], hidden_basis[:, :toks])
    basis_part = jnp.dot(mix_total, hidden, preferred_element_type=f32)

    came_z, pieces = None, []
    for bit in bits:
        for j in [j for j in sorted(sums, reverse=True) if j & bit]:
            total = sums.pop(j)
            send = first_z if j == n_z - 1 else total.astype(bf16)
            if bit == bits[0] and came_z is not None:
                send, _ = lax.optimization_barrier((send, came_z))
            came = first_came if j == n_z - 1 else swap_z(send, bit)
            came_z = came if came_z is None else came_z
            if j ^ bit or bit != bits[-1]:
                sums[j ^ bit] = sums[j ^ bit] + came.astype(f32)
            else:
                pieces.append(came)
    total = sums[0] + dot_first(mix_total, basis_half[:, :width])

    factor_part = jnp.concatenate([basis_part, rows_part], axis=1)
    factor_two = lax.reduce_precision(factor_part + swap_core(factor_part), 8, 7)
    factor_two, _ = lax.optimization_barrier((factor_two, from_x[min(1, n_z - 1)]))
    factor_came = swap_x(factor_two.astype(bf16))
    hidden_grad, basis_grad, rows_grad = finish(total, pieces, factor_two, factor_came)
    return hidden_grad, rows_grad, basis_grad


def on_many(hidden, head, factor_rows, factor_basis, targets, loss_mask):
    n_vocab = lax.axis_size("vocab")
    n_tok = lax.axis_size("tok")
    vocab_index = lax.axis_index("vocab")
    rows_here = head.shape[0] * n_tok
    new_here = factor_rows.shape[0]
    width_here = hidden.shape[1]
    gathered = lax.all_gather(hidden, "vocab", axis=1, tiled=True)
    head_full = lax.all_gather(head, "tok", axis=0, tiled=True)
    frozen = dot_last(gathered, head_full)
    hidden_basis = dot_last(gathered, factor_basis).astype(bf16)
    fresh_logits = dot_last(hidden_basis, factor_rows)
    local_max = jnp.maximum(jnp.max(frozen, axis=1), jnp.max(fresh_logits, axis=1))
    row_top = lax.pmax(local_max, "vocab")
    local_sum = jnp.sum(jnp.exp(frozen - row_top[:, None]), axis=1) + jnp.sum(
        jnp.exp(fresh_logits - row_top[:, None]), axis=1
    )
    sum_exp = lax.psum(local_sum, "vocab")
    frozen_prob = jnp.exp(frozen - row_top[:, None]) / sum_exp[:, None]
    fresh_prob = jnp.exp(fresh_logits - row_top[:, None]) / sum_exp[:, None]
    frozen_offset = targets - vocab_index * rows_here
    fresh_offset = targets - rows_here * n_vocab - vocab_index * new_here
    frozen_hit = (
        lax.broadcasted_iota(jnp.int32, frozen.shape, 1) == frozen_offset[:, None]
    ).astype(f32)
    fresh_hit = (
        lax.broadcasted_iota(jnp.int32, fresh_logits.shape, 1) == fresh_offset[:, None]
    ).astype(f32)
    weight_row = loss_scale * loss_mask.astype(f32)[:, None]
    frozen_grad = (weight_row * (frozen_prob - frozen_hit)).astype(bf16)
    fresh_grad = (weight_row * (fresh_prob - fresh_hit)).astype(bf16)
    mix_term = jnp.dot(fresh_grad, factor_rows, preferred_element_type=f32)
    mix_total = lax.psum(mix_term, "vocab").astype(bf16)
    grad_part = lax.psum_scatter(
        lax.dot_general(
            head_full, frozen_grad, (((0,), (1,)), ((), ())), preferred_element_type=f32
        ),
        "vocab",
        scatter_dimension=0,
        tiled=True,
    )
    basis_cols = lax.dynamic_slice_in_dim(factor_basis, vocab_index * width_here, width_here, 1)
    hidden_grad = (
        grad_part.T + jnp.dot(mix_total, basis_cols, preferred_element_type=f32)
    ).astype(bf16)
    rows_term = dot_first(fresh_grad, hidden_basis)
    basis_term = dot_first(mix_total, hidden)
    rows_grad, basis_grad = (
        lax.psum(rows_term.astype(bf16), "tok").astype(f32),
        lax.psum(basis_term.astype(bf16), "tok").astype(f32),
    )
    return hidden_grad, rows_grad, basis_grad


def solution(mesh):
    in_specs = (
        P("tok", "vocab"),
        P(("vocab", "tok"), None),
        P("vocab", None),
        P(),
        P("tok"),
        P("tok"),
    )
    out_specs = (P("tok", "vocab"), P("vocab", None), P(None, "vocab"))

    def on_device(hidden, head, factor_rows, *rest):
        even = [n & (n - 1) == 0 for n in (mesh.shape["vocab"], head.shape[0], factor_rows.shape[0])]
        few = 2 <= mesh.shape["vocab"] <= 16 and mesh.shape["tok"] == 4 and all(even)
        few = few and hidden.shape[0] == 2 * factor_rows.shape[1]
        return (on_few if few else on_many)(hidden, head, factor_rows, *rest)

    return jax.shard_map(
        on_device, mesh=mesh, in_specs=in_specs, out_specs=out_specs, check_vma=False
    )
```
